32 devices in a mesh: dp: 8 (over y, x, core), seq: 4 (over z).
Axes of the slice: x: 2, y: 2, z: 4, core: 2. Of those that a mesh axis runs over, the one named last changes fastest.
Arguments:
- tokens: bfloat16 [32, 1024, 768], P('dp', 'seq'), may hold values from -8 to 8
- doc_lengths: int32 [32, 4], P('dp'), may hold values from 1 to 768, 1024 in all within a row
- query_weight: bfloat16 [768, 768], P(('dp', 'seq')), may hold values from -0.21875 to 0.21875
- key_weight: bfloat16 [768, 768], P(('dp', 'seq')), may hold values from -0.21875 to 0.21875
- value_weight: bfloat16 [768, 768], P(('dp', 'seq')), may hold values from -0.21875 to 0.21875
- out_weight: bfloat16 [768, 768], P(('dp', 'seq')), may hold values from -1.75 to 1.75
- pool_weight: bfloat16 [10, 768], P(None, ('dp', 'seq')), may hold values from -2.5 to 2.5
- first_gain: bfloat16 [768], P(('dp', 'seq')), may hold values from 0.5 to 1.5
- first_shift: bfloat16 [768], P(('dp', 'seq')), may hold values from -1.25 to 1.25
- inner_weight: bfloat16 [768, 3072], P(('dp', 'seq')), may hold values from -0.21875 to 0.21875
- inner_bias: bfloat16 [3072], P(('dp', 'seq')), may hold values from -1.75 to 1.75
- outer_weight: bfloat16 [3072, 768], P(('dp', 'seq')), may hold values from -0.21875 to 0.21875
- outer_bias: bfloat16 [768], P(('dp', 'seq')), may hold values from -1.25 to 1.25
- second_gain: bfloat16 [768], P(('dp', 'seq')), may hold values from 0.5 to 1.5
- second_shift: bfloat16 [768], P(('dp', 'seq')), may hold values from -1.25 to 1.25
- cotangent: bfloat16 [32, 1024, 768], P('dp', 'seq'), may hold values from -6 to 6
Outputs:
- block_output: bfloat16 [32, 1024, 768], P('dp', 'seq')
- input_grad: bfloat16 [32, 1024, 768], P('dp', 'seq')
- query_grad: float32 [768, 768], P(('dp', 'seq'))
- key_grad: float32 [768, 768], P(('dp', 'seq'))
- value_grad: float32 [768, 768], P(('dp', 'seq'))
- out_grad: float32 [768, 768], P(('dp', 'seq'))
- pool_grad: float32 [10, 768], P(None, ('dp', 'seq'))
- first_gain_grad: float32 [768], P(('dp', 'seq'))
- first_shift_grad: float32 [768], P(('dp', 'seq'))
- inner_grad: float32 [768, 3072], P(('dp', 'seq'))
- inner_bias_grad: float32 [3072], P(('dp', 'seq'))
- outer_grad: float32 [3072, 768], P(('dp', 'seq'))
- outer_bias_grad: float32 [768], P(('dp', 'seq'))
- second_gain_grad: float32 [768], P(('dp', 'seq'))
- second_shift_grad: float32 [768], P(('dp', 'seq'))
The draws below stay inside these ranges and needn't reach their ends.
Inputs may be any that keep to these rules, and one draw needn't show every extreme that they name: `doc_lengths`: each row's 4 lengths sum to 1024; the largest of each row is exactly 768.
All inputs are finite; a program needn't handle non-finite values.
Results may differ from the reference program's by a relative error of at most 0.015.
The reference program's roundings to bfloat16 on the way count: a program that leaves them out, or rounds other values in their place, can miss the bound.
Values may be sent and summed in bfloat16 or wider, within the bound.
No kernel may reach another device: no remote copies, remote signals or barrier semaphores. Data moves between devices by JAX's collectives and lax.ppermute only.
A program may use at most 256 MiB of HBM per device.

```python
import math
import jax
import jax.numpy as jnp
import numpy as np
from jax import lax

D = 768
HEADS = 12
HEAD_DIM = 64
FF = 3072
WIN = 128
PWIN = 512
LEN = 1024
MOSTDOC = 768
NDOC = 4
SEQS = 32


def raised(result, stream_key, source, target, parts, factor):
    def block_of(position):
        return (jnp.arange(result.shape[position]) // (result.shape[position] // parts)).reshape((-1,) + (1,) * (result.ndim - 1 - position))

    first = jax.random.permutation(stream_key, parts)[block_of(target)]
    second = (block_of(target) + parts // 2) % parts
    return jnp.where((block_of(source) == first) | (block_of(source) == second), factor * result, result)


def block_scale(own_key, extent, cuts, smallest, high):
    factor_of = 1.0
    for axis_at, blocks in cuts:
        draws = jax.random.uniform(jax.random.fold_in(jax.random.fold_in(own_key, 6), axis_at), (blocks,), jnp.float32, smallest / len(cuts), high / len(cuts))
        factor_of = factor_of * jnp.repeat(jnp.exp(draws), extent[axis_at] // blocks).reshape((-1,) + (1,) * (len(extent) - 1 - axis_at))
    return factor_of


def profile(count, total, bound, lean):
    loads = [(1 << 20) // math.isqrt(rank ** lean) + 1 for rank in range(2, count + 1)]
    surplus, holding = total - bound - (count - 1), [1] * (count - 1)
    while surplus > 0:
        movable = [i for i in range(count - 1) if holding[i] < bound]
        mass, remaining = sum([loads[i] for i in movable]), surplus
        for i in movable:
            extra = min(bound - holding[i], max(1, remaining * loads[i] // mass), surplus)
            holding[i] = holding[i] + extra
            surplus = surplus - extra
    return np.array([bound] + holding)


def uneven(own_key, count, total, bound, slope):
    if count == 2:
        one = jax.random.randint(own_key, (), max(1, total - bound), min(bound, total - 1) + 1)
        return jnp.stack([one, total - one])
    sizes = jnp.asarray(profile(count, total, bound, slope), jnp.int32)
    couples = (count - 1) // 2
    source_of, receiver = sizes[1:1 + 2 * couples:2], sizes[2:2 + 2 * couples:2]
    room = jnp.minimum(source_of - 1, bound - receiver)
    passed = jax.random.randint(jax.random.fold_in(own_key, 1), (couples,), 0, 1 << 20) % (room + 1)
    sizes = sizes.at[1:1 + 2 * couples:2].set(source_of - passed).at[2:2 + 2 * couples:2].set(receiver + passed)
    return sizes[jax.random.permutation(jax.random.fold_in(own_key, 2), count)]


def scatter_about(rng, shape, width, most, cuts=(), kind=jnp.bfloat16):
    factor_of = block_scale(rng, shape, cuts, -0.22, 0.18) if cuts else 1.0
    drawn = jax.random.normal(rng, shape, jnp.float32) * width * factor_of
    return jnp.minimum(jnp.maximum(drawn, -most), most).astype(kind)


def heavy_noise(rng, dims, spread, most, split, heavy, held_as=jnp.bfloat16):
    entries = spread * jax.random.normal(rng, dims, jnp.float32)
    if split:
        entries = entries * block_scale(rng, dims, split, -0.22, 0.18)
    return jnp.clip(raised(entries, jax.random.fold_in(rng, 3), *heavy), -most, most).astype(held_as)


def setup_inputs(seed: int = 0) -> dict:
    key_list = jax.random.split(jax.random.key(seed), 17)
    tokens = heavy_noise(key_list[0], (SEQS, LEN, D), 1.0, 8.0, ((0, 8), (1, 4)), (0, 2, 8, 2.0))
    doc_lengths = jax.vmap(lambda own: uneven(own, NDOC, LEN, MOSTDOC, 2))(jax.random.split(key_list[1], SEQS)).reshape((SEQS, NDOC)).astype(jnp.int32)
    query_weight = scatter_about(key_list[2], (D, D), D ** -0.5, 0.21875, ((0, 32),))
    key_weight = scatter_about(key_list[3], (D, D), D ** -0.5, 0.21875, ((0, 32),))
    value_weight = scatter_about(key_list[4], (D, D), D ** -0.5, 0.21875, ((0, 32),))
    out_weight = scatter_about(key_list[5], (D, D), (D // 64) ** -0.5, 1.75, ((0, 32),))
    pool_weight = scatter_about(key_list[6], (10, D), 0.45, 2.5, ((1, 32),))
    first_gain = jnp.clip(1.0 + 0.1 * jax.random.normal(key_list[7], (D,), jnp.float32), 0.5, 1.5).astype(jnp.bfloat16)
    first_shift = scatter_about(key_list[8], (D,), 0.2, 1.25, ((0, 32),))
    inner_weight = scatter_about(key_list[9], (D, FF), D ** -0.5, 0.21875, ((0, 32),))
    inner_bias = scatter_about(key_list[10], (FF,), 0.3, 1.75, ((0, 32),))
    outer_weight = scatter_about(key_list[11], (FF, D), (FF // 4) ** -0.5, 0.21875, ((0, 32),))
    outer_bias = scatter_about(key_list[12], (D,), 0.2, 1.25, ((0, 32),))
    second_gain = jnp.clip(1.0 + 0.1 * jax.random.normal(key_list[13], (D,), jnp.float32), 0.5, 1.5).astype(jnp.bfloat16)
    second_shift = scatter_about(key_list[14], (D,), 0.2, 1.25, ((0, 32),))
    cotangent = scatter_about(key_list[15], (SEQS, LEN, D), 1.0, 6.0, ((0, 8), (1, 4)))
    return {"tokens": tokens, "doc_lengths": doc_lengths, "query_weight": query_weight, "key_weight": key_weight, "value_weight": value_weight, "out_weight": out_weight, "pool_weight": pool_weight, "first_gain": first_gain, "first_shift": first_shift, "inner_weight": inner_weight, "inner_bias": inner_bias, "outer_weight": outer_weight, "outer_bias": outer_bias, "second_gain": second_gain, "second_shift": second_shift, "cotangent": cotangent}


@jax.custom_vjp
def low(v):
    return lax.optimization_barrier(v.astype(jnp.bfloat16)).astype(jnp.float32)

@jax.custom_vjp
def low_back(v):
    return v

def low_keep(v):
    return (low(v), None)

def low_pass(kept, grad):
    return (grad,)

def back_keep(v):
    return (v, None)

def back_low(kept, grad):
    return (low(grad),)
low.defvjp(low_keep, low_pass)
low_back.defvjp(back_keep, back_low)
EPS = 1e-05

def matmul(left, right):
    return jnp.dot(left, right, precision=lax.Precision.HIGHEST, preferred_element_type=jnp.float32)

def layer_norm(value, gain, shift):
    row_mean = lax.optimization_barrier(jnp.mean(value, axis=-1, keepdims=True))
    centered = value - row_mean
    scaled = centered * lax.rsqrt(lax.optimization_barrier(jnp.mean(centered * centered, axis=-1, keepdims=True)) + EPS)
    return scaled * gain + shift

def gelu_exact(value):
    return jax.nn.gelu(value, approximate=False)

def document_ids(lengths):
    ends = jnp.cumsum(lengths)
    positions = jnp.arange(LEN, dtype=jnp.int32)
    return lax.optimization_barrier(jnp.sum((positions[:, None] >= ends[None, :]).astype(jnp.int32), axis=1))

def attend_block(start, queries, key_rows, value_rows, pool_key, pool_value, doc, slot_doc):
    block_rows = min(512, LEN)
    scale = HEAD_DIM ** (-0.5)
    query_block = lax.dynamic_slice_in_dim(queries, start, block_rows, 0).reshape(block_rows, HEADS, HEAD_DIM)
    doc_block = lax.dynamic_slice_in_dim(doc, start, block_rows, 0)
    query_pos = start + jnp.arange(block_rows, dtype=jnp.int32)
    key_pos = jnp.arange(LEN, dtype=jnp.int32)
    centers = 4 * jnp.arange(LEN // 4, dtype=jnp.int32) + 2
    near = jnp.einsum('qhe,khe->hqk', query_block, key_rows.reshape(LEN, HEADS, HEAD_DIM), precision=lax.Precision.HIGHEST) * scale
    far = jnp.einsum('qhe,khe->hqk', query_block, pool_key.reshape(LEN // 4, HEADS, HEAD_DIM), precision=lax.Precision.HIGHEST) * scale
    scores = low_back(jnp.concatenate((near, far), axis=2))
    near_ok = (jnp.abs(key_pos[None, :] - query_pos[:, None]) <= WIN // 2) & (doc[None, :] == doc_block[:, None])
    far_ok = (jnp.abs(centers[None, :] - query_pos[:, None]) <= PWIN // 2) & (slot_doc[None, :] == doc_block[:, None])
    allowed = jnp.concatenate((near_ok, far_ok), axis=1)
    scores = jnp.where(allowed[None], scores, -1e+30)
    top = lax.optimization_barrier(jnp.max(scores, axis=2, keepdims=True))
    weights = jnp.exp(scores - top)
    probs = low(weights / lax.optimization_barrier(jnp.sum(weights, axis=2, keepdims=True)))
    mixed = jnp.einsum('hqk,khe->qhe', probs[:, :, :LEN], value_rows.reshape(LEN, HEADS, HEAD_DIM), precision=lax.Precision.HIGHEST)
    mixed = mixed + jnp.einsum('hqk,khe->qhe', probs[:, :, LEN:], pool_value.reshape(LEN // 4, HEADS, HEAD_DIM), precision=lax.Precision.HIGHEST)
    return mixed.reshape(block_rows, HEADS * HEAD_DIM)

def layer(params, inputs, doc):
    w_query, w_key, w_value, w_out, w_pool, gain_one, shift_one, w_inner, bias_inner, w_outer, bias_outer, gain_two, shift_two = params
    queries = low(low_back(matmul(inputs, w_query)))
    key_rows = low(low_back(matmul(inputs, w_key)))
    value_rows = low(low_back(matmul(inputs, w_value)))
    pad_doc = jnp.concatenate((doc, jnp.full((4,), -1, jnp.int32)))
    tap_doc = jnp.stack([pad_doc[tap_index:tap_index + LEN].reshape(LEN // 4, 4)[:, 0] for tap_index in range(5)], axis=1)
    same_doc = (tap_doc == tap_doc[:, 2:3]).astype(jnp.float32)

    def pool_rows(rows_in, kernel):
        padded = jnp.concatenate((rows_in, jnp.zeros((4, D), jnp.float32)), axis=0)
        stacked = jnp.stack([padded[tap_index:tap_index + LEN].reshape(LEN // 4, 4, D)[:, 0] for tap_index in range(5)], axis=1)
        return low(lax.optimization_barrier(jnp.sum(stacked * same_doc[:, :, None] * kernel[None], axis=1)))
    pool_key = pool_rows(key_rows, w_pool[:5])
    pool_value = pool_rows(value_rows, w_pool[5:])
    slot_doc = tap_doc[:, 2]
    block_rows = min(512, LEN)
    starts = jnp.arange(0, LEN, block_rows, dtype=jnp.int32)
    checked = jax.checkpoint(attend_block)
    mixed = lax.map(lambda start: checked(start, queries, key_rows, value_rows, pool_key, pool_value, doc, slot_doc), starts)
    mixed = low(low_back(mixed.reshape(LEN, D)))
    attended = low_back(matmul(mixed, w_out))
    normed_one = layer_norm(inputs + attended, gain_one, shift_one)
    inner = low_back(matmul(low(normed_one), w_inner) + bias_inner)
    hidden = low(gelu_exact(inner))
    outer = low_back(matmul(hidden, w_outer) + bias_outer)
    return layer_norm(normed_one + outer, gain_two, shift_two)

def reference(tokens, doc_lengths, query_weight, key_weight, value_weight, out_weight, pool_weight, first_gain, first_shift, inner_weight, inner_bias, outer_weight, outer_bias, second_gain, second_shift, cotangent):
    params = tuple((item.astype(jnp.float32) for item in (query_weight, key_weight, value_weight, out_weight, pool_weight, first_gain, first_shift, inner_weight, inner_bias, outer_weight, outer_bias, second_gain, second_shift)))

    def one_sequence(carry, packed):
        seq_tokens, seq_lengths, seq_cot = packed
        doc = document_ids(seq_lengths)

        def forward(weights, inputs):
            return layer(weights, inputs, doc)
        output, pull = jax.vjp(forward, params, seq_tokens.astype(jnp.float32))
        d_params, d_inputs = pull(seq_cot.astype(jnp.float32))
        carry = jax.tree.map(lambda first, second: first + second, carry, d_params)
        return (carry, (output.astype(jnp.bfloat16), d_inputs.astype(jnp.bfloat16)))
    start_grads = jax.tree.map(jnp.zeros_like, params)
    grad_sums, (outputs, d_inputs) = lax.scan(one_sequence, start_grads, (tokens, doc_lengths, cotangent))
    return (outputs, d_inputs, grad_sums[0], grad_sums[1], grad_sums[2], grad_sums[3], grad_sums[4], grad_sums[5], grad_sums[6], grad_sums[7], grad_sums[8], grad_sums[9], grad_sums[10], grad_sums[11], grad_sums[12])
```

```python
import functools

import jax
import jax.numpy as jnp
from jax import lax
from jax.experimental import pallas as pl
from jax.experimental.pallas import tpu as pltpu
from jax.sharding import PartitionSpec as P

HEADS = 12
HEAD_DIM = 64
WIN = 128
PWIN = 512
EPS = 1e-05

LANES = 128
QB = 128
HALO = PWIN // 2
PAD = 16
NEAR = QB + WIN
FAR = (QB + PWIN) // 4
KEYS = NEAR + FAR
MASKED = -1e30

F32 = jnp.float32
BF16 = jnp.bfloat16


def nt(left, right):
    return lax.dot_general(left, right, (((1,), (1,)), ((), ())), preferred_element_type=F32)


def tn(left, right):
    return lax.dot_general(left, right, (((0,), (0,)), ((), ())), preferred_element_type=F32)


def nn(left, right):
    return lax.dot_general(left, right, (((1,), (0,)), ((), ())), preferred_element_type=F32)


def slot_taps(wide, slots):
    return [wide[pl.ds(tap, slots, stride=4), :] for tap in range(5)]


def pool(taps, same_ref, w_ref, first):
    total = None
    for tap in range(5):
        term = taps[tap] * same_ref[0, tap] * w_ref[first + tap : first + tap + 1, :]
        total = term if total is None else total + term
    return total.astype(BF16)


def pair_stack(rows):
    lane = lax.broadcasted_iota(jnp.int32, rows.shape, 1)
    zero = jnp.zeros_like(rows)
    return jnp.concatenate(
        (jnp.where(lane < HEAD_DIM, rows, zero), jnp.where(lane < HEAD_DIM, zero, rows)), axis=0
    )


def pair_join(both):
    joined = jnp.concatenate((both[:HEAD_DIM, :QB], both[HEAD_DIM:, QB:]), axis=0)
    return joined.T


def keys_of(ref, pooled, block):
    near = HALO - WIN // 2 + block * QB
    far = block * QB // 4
    return jnp.concatenate((ref[0, near : near + NEAR, :], pooled[far : far + FAR, :]), axis=0)


def scores_of(keys, stacked, bias):
    return nt(keys, stacked) + jnp.concatenate((bias, bias), axis=1)


def attn_fwd_kernel(
    q_ref, k_ref, v_ref, w_ref, same_ref, bias_ref, out_ref, lse_ref, k_wide, v_wide, pk_ref, pv_ref
):
    slots = pk_ref.shape[0]
    k_wide[...] = k_ref[0].astype(F32)
    v_wide[...] = v_ref[0].astype(F32)
    pk_ref[...] = pool(slot_taps(k_wide, slots), same_ref, w_ref, 0)
    pv_ref[...] = pool(slot_taps(v_wide, slots), same_ref, w_ref, 5)
    scale = jnp.asarray(HEAD_DIM**-0.5, BF16)
    for block in range(q_ref.shape[1] // QB):
        rows = slice(block * QB, (block + 1) * QB)
        keys = keys_of(k_ref, pk_ref, block)
        values = keys_of(v_ref, pv_ref, block)
        stacked = pair_stack(q_ref[0, rows, :] * scale)
        scores = scores_of(keys, stacked, bias_ref[0, block])
        top = jnp.max(scores, axis=0, keepdims=True)
        weights = jnp.exp(scores - top)
        denom = jnp.sum(weights, axis=0, keepdims=True)
        probs = (weights * (1.0 / denom)).astype(BF16)
        out_ref[0, rows, :] = pair_join(tn(values, probs)).astype(BF16)
        lse_ref[0, 0, block : block + 1, :] = top + jnp.log(denom)


def attn_bwd_kernel(
    q_ref,
    k_ref,
    v_ref,
    w_ref,
    same_ref,
    bias_ref,
    lse_ref,
    do_ref,
    dq_ref,
    dk_ref,
    dv_ref,
    dw_ref,
    k_wide,
    v_wide,
    pk_ref,
    pv_ref,
    dpk_ref,
    dpv_ref,
):
    slots = pk_ref.shape[0]
    k_wide[...] = k_ref[0].astype(F32)
    v_wide[...] = v_ref[0].astype(F32)
    pk_ref[...] = pool(slot_taps(k_wide, slots), same_ref, w_ref, 0)
    pv_ref[...] = pool(slot_taps(v_wide, slots), same_ref, w_ref, 5)
    dpk_ref[...] = jnp.zeros_like(dpk_ref)
    dpv_ref[...] = jnp.zeros_like(dpv_ref)
    scale = jnp.asarray(HEAD_DIM**-0.5, BF16)
    near_parts = []
    for block in range(q_ref.shape[1] // QB):
        rows = slice(block * QB, (block + 1) * QB)
        keys = keys_of(k_ref, pk_ref, block)
        values = keys_of(v_ref, pv_ref, block)
        stacked = pair_stack(q_ref[0, rows, :] * scale)
        do_stacked = pair_stack(do_ref[0, rows, :])
        probs = jnp.exp(
            scores_of(keys, stacked, bias_ref[0, block]) - lse_ref[0, 0, block : block + 1, :]
        )
        d_probs = nt(values, do_stacked)
        row_dot = jnp.sum(probs * d_probs, axis=0, keepdims=True)
        d_scores = (probs * (d_probs - row_dot)).astype(BF16)
        d_values = nn(probs.astype(BF16), do_stacked)
        d_keys = nn(d_scores, stacked)
        dq_ref[0, rows, :] = (pair_join(tn(keys, d_scores)) * HEAD_DIM**-0.5).astype(BF16)
        far = slice(block * QB // 4, block * QB // 4 + FAR)
        dpk_ref[far, :] += d_keys[NEAR:]
        dpv_ref[far, :] += d_values[NEAR:]
        near_parts.append((d_keys[:NEAR], d_values[:NEAR]))
    sides = ((k_wide, dpk_ref, dk_ref, 0), (v_wide, dpv_ref, dv_ref, 1))
    for wide, d_pool_ref, out_ref, side in sides:
        d_pool = d_pool_ref[...]
        taps = slot_taps(wide, slots)
        masked = [d_pool * same_ref[0, tap] for tap in range(5)]
        for tap in range(5):
            row = 5 * side + tap
            dw_ref[0, row : row + 1, :] = jnp.sum(masked[tap] * taps[tap], axis=0, keepdims=True)
        spread = [masked[tap] * w_ref[5 * side + tap : 5 * side + tap + 1, :] for tap in range(5)]
        wide[4 * slots :, :] = jnp.zeros((wide.shape[0] - 4 * slots, LANES), F32)
        for tap in range(4):
            wide[pl.ds(tap, slots, stride=4), :] = spread[tap]
        wide[pl.ds(4, slots, stride=4), :] += spread[4]
        for block, parts in enumerate(near_parts):
            near = HALO - WIN // 2 + block * QB
            wide[near : near + NEAR, :] += parts[side]
        out_ref[0] = wide[...].astype(BF16)
    dw_ref[0, 10:, :] = jnp.zeros((dw_ref.shape[1] - 10, LANES), F32)


def attention_specs(ext, group, slots):
    return [
        pl.BlockSpec((1, group, LANES), lambda s, p: (s, 0, p)),
        pl.BlockSpec((1, ext, LANES), lambda s, p: (s, 0, p)),
        pl.BlockSpec((1, ext, LANES), lambda s, p: (s, 0, p)),
        pl.BlockSpec((16, LANES), lambda s, p: (0, p)),
        pl.BlockSpec((1, 5, slots, LANES), lambda s, p: (s, 0, 0, 0)),
        pl.BlockSpec((1, group // QB, KEYS, LANES), lambda s, p: (s, 0, 0, 0)),
    ]


def attention_forward(queries, keys, values, taps, same, bias):
    seqs, group, width = queries.shape
    ext = keys.shape[1]
    slots = same.shape[2]
    pairs = width // LANES
    blocks = group // QB
    wide = pltpu.VMEM((ext, LANES), F32)
    pooled = pltpu.VMEM((slots, LANES), BF16)
    return pl.pallas_call(
        attn_fwd_kernel,
        grid=(seqs, pairs),
        in_specs=attention_specs(ext, group, slots),
        out_specs=[
            pl.BlockSpec((1, group, LANES), lambda s, p: (s, 0, p)),
            pl.BlockSpec((1, 1, blocks, 2 * QB), lambda s, p: (s, p, 0, 0)),
        ],
        out_shape=[
            jax.ShapeDtypeStruct((seqs, group, width), BF16),
            jax.ShapeDtypeStruct((seqs, pairs, blocks, 2 * QB), F32),
        ],
        scratch_shapes=[wide, wide, pooled, pooled],
        compiler_params=pltpu.CompilerParams(vmem_limit_bytes=32 << 20),
        cost_estimate=pl.CostEstimate(
            flops=seqs * HEADS * blocks * QB * KEYS * LANES * 8,
            bytes_accessed=seqs * width * (ext * 4 + group * 4),
            transcendentals=seqs * HEADS * group * KEYS,
        ),
        name="attn_fwd",
    )(queries, keys, values, taps, same, bias)


def attention_backward(queries, keys, values, taps, same, bias, lse, d_mixed):
    seqs, group, width = queries.shape
    ext = keys.shape[1]
    slots = same.shape[2]
    pairs = width // LANES
    blocks = group // QB
    wide = pltpu.VMEM((ext, LANES), F32)
    pooled = pltpu.VMEM((slots, LANES), BF16)
    d_pooled = pltpu.VMEM((slots, LANES), F32)
    own = pl.BlockSpec((1, group, LANES), lambda s, p: (s, 0, p))
    extended = pl.BlockSpec((1, ext, LANES), lambda s, p: (s, 0, p))
    return pl.pallas_call(
        attn_bwd_kernel,
        grid=(seqs, pairs),
        in_specs=attention_specs(ext, group, slots)
        + [pl.BlockSpec((1, 1, blocks, 2 * QB), lambda s, p: (s, p, 0, 0)), own],
        out_specs=[
            own,
            extended,
            extended,
            pl.BlockSpec((1, 16, LANES), lambda s, p: (s, 0, p)),
        ],
        out_shape=[
            jax.ShapeDtypeStruct((seqs, group, width), BF16),
            jax.ShapeDtypeStruct((seqs, ext, width), BF16),
            jax.ShapeDtypeStruct((seqs, ext, width), BF16),
            jax.ShapeDtypeStruct((seqs, 16, width), F32),
        ],
        scratch_shapes=[wide, wide, pooled, pooled, d_pooled, d_pooled],
        compiler_params=pltpu.CompilerParams(vmem_limit_bytes=32 << 20),
        cost_estimate=pl.CostEstimate(
            flops=seqs * HEADS * blocks * QB * KEYS * LANES * 20,
            bytes_accessed=seqs * width * (ext * 8 + group * 6),
            transcendentals=seqs * HEADS * group * KEYS,
        ),
        name="attn_bwd",
    )(queries, keys, values, taps, same, bias, lse, d_mixed)


ROWS = 256
HALF_PI = 0.3989422804014327


def row_sum(value):
    return jnp.sum(value, axis=0, keepdims=True)


def row_mean(value):
    return jnp.mean(value, axis=1, keepdims=True)


def normalize(value):
    centered = value - row_mean(value)
    inv = lax.rsqrt(row_mean(centered * centered) + EPS)
    return centered * inv, inv


def normalize_back(grad, normed, inv):
    return inv * (grad - row_mean(grad) - normed * row_mean(grad * normed))


def ffn_kernel(
    panels,
    x_ref,
    mixed_ref,
    cot_ref,
    wo_ref,
    small_ref,
    bias_ref,
    w_in_ref,
    w_out_ref,
    y_ref,
    d_first_ref,
    d_mixed_ref,
    d_wo_ref,
    d_small_ref,
    d_bias_ref,
    d_in_ref,
    d_out_ref,
    n_one,
    inv_one,
    low,
    hidden,
    slope,
    acc,
    d_outer,
    d_inner,
):
    step = pl.program_id(0)
    tokens, width = x_ref.shape
    chunks = tokens // ROWS
    gain_one, shift_one, outer_bias, gain_two, shift_two = (
        small_ref[i : i + 1, :] for i in range(5)
    )

    @pl.when(step == 0)
    def _():
        def body(i, carry):
            rows = pl.ds(pl.multiple_of(i * ROWS, ROWS), ROWS)
            first = x_ref[rows, :].astype(F32) + nn(mixed_ref[rows, :], wo_ref[...])
            normed, inv = normalize(first)
            n_one[rows, :] = normed
            inv_one[rows, :] = jnp.broadcast_to(inv, (ROWS, LANES))
            out = normed * gain_one + shift_one
            low[rows, :] = out.astype(BF16)
            acc[rows, :] = out + outer_bias
            return carry

        lax.fori_loop(0, chunks, body, 0)

    @pl.when(step < panels)
    def _():
        def body(i, carry):
            rows = pl.ds(pl.multiple_of(i * ROWS, ROWS), ROWS)
            inner = nn(low[rows, :], w_in_ref[0]) + bias_ref[0]
            cdf = 0.5 * (1.0 + lax.erf(inner * 0.7071067811865476))
            pdf = HALF_PI * jnp.exp(-0.5 * inner * inner)
            out = (inner * cdf).astype(BF16)
            hidden[step, rows, :] = out
            slope[step, rows, :] = cdf + inner * pdf
            acc[rows, :] += nn(out, w_out_ref[0])
            return carry

        lax.fori_loop(0, chunks, body, 0)

    @pl.when(step == panels)
    def _():
        def body(i, carry):
            d_gain, d_shift, d_bias = carry
            rows = pl.ds(pl.multiple_of(i * ROWS, ROWS), ROWS)
            normed, inv = normalize(acc[rows, :])
            y_ref[rows, :] = (normed * gain_two + shift_two).astype(BF16)
            grad = cot_ref[rows, :].astype(F32)
            d_second = normalize_back(grad * gain_two, normed, inv)
            low_grad = d_second.astype(BF16)
            acc[rows, :] = d_second
            d_outer[rows, :] = low_grad
            return (
                d_gain + row_sum(grad * normed),
                d_shift + row_sum(grad),
                d_bias + row_sum(low_grad.astype(F32)),
            )

        zero = jnp.zeros((1, width), F32)
        d_gain, d_shift, d_bias = lax.fori_loop(0, chunks, body, (zero, zero, zero))
        d_small_ref[2:3, :] = d_bias
        d_small_ref[3:4, :] = d_gain
        d_small_ref[4:5, :] = d_shift
        d_small_ref[5:, :] = jnp.zeros((3, width), F32)

    @pl.when(step >= panels)
    def _():
        panel = step - panels

        def body(i, d_bias):
            rows = pl.ds(pl.multiple_of(i * ROWS, ROWS), ROWS)
            d_hidden = nt(d_outer[rows, :], w_out_ref[0])
            grad = (d_hidden * slope[panel, rows, :]).astype(BF16)
            d_inner[rows, :] = grad
            acc[rows, :] += nt(grad, w_in_ref[0])
            return d_bias + row_sum(grad.astype(F32))

        d_bias_ref[0] = lax.fori_loop(0, chunks, body, jnp.zeros(d_bias_ref.shape[1:], F32))
        d_out_ref[0] = tn(hidden[panel], d_outer[...]).astype(BF16)
        d_in_ref[0] = tn(low[...], d_inner[...]).astype(BF16)

    @pl.when(step == 2 * panels - 1)
    def _():
        def body(i, carry):
            d_gain, d_shift = carry
            rows = pl.ds(pl.multiple_of(i * ROWS, ROWS), ROWS)
            grad = acc[rows, :]
            normed = n_one[rows, :]
            d_first = normalize_back(grad * gain_one, normed, inv_one[rows, 0:1])
            d_first_ref[rows, :] = d_first
            low_grad = d_first.astype(BF16)
            d_outer[rows, :] = low_grad
            d_mixed_ref[rows, :] = nt(low_grad, wo_ref[...]).astype(BF16)
            return d_gain + row_sum(grad * normed), d_shift + row_sum(grad)

        zero = jnp.zeros((1, width), F32)
        d_gain, d_shift = lax.fori_loop(0, chunks, body, (zero, zero))
        d_small_ref[0:1, :] = d_gain
        d_small_ref[1:2, :] = d_shift
        d_wo_ref[...] = tn(mixed_ref[...], d_outer[...]).astype(BF16)


def feed_forward(x, mixed, cot, wo, small, bias, w_in, w_out):
    tokens, width = x.shape
    panels, _, panel = w_in.shape

    def whole(*shape):
        return pl.BlockSpec(
            shape, lambda j: (0,) * len(shape), pipeline_mode=pl.Buffered(buffer_count=1)
        )

    def now(j):
        return (lax.rem(j, panels), 0, 0)

    def later(j):
        return (jnp.maximum(j - panels, 0), 0, 0)

    weight = pl.BlockSpec((1, width, panel), now)
    weight_out = pl.BlockSpec((1, panel, width), now)
    return pl.pallas_call(
        functools.partial(ffn_kernel, panels),
        grid=(2 * panels,),
        in_specs=[
            whole(tokens, width),
            whole(tokens, width),
            whole(tokens, width),
            whole(width, width),
            whole(8, width),
            pl.BlockSpec((1, 1, panel), now),
            weight,
            weight_out,
        ],
        out_specs=[
            whole(tokens, width),
            whole(tokens, width),
            whole(tokens, width),
            whole(width, width),
            whole(8, width),
            pl.BlockSpec((1, 1, panel), later),
            pl.BlockSpec((1, width, panel), later),
            pl.BlockSpec((1, panel, width), later),
        ],
        out_shape=[
            jax.ShapeDtypeStruct((tokens, width), BF16),
            jax.ShapeDtypeStruct((tokens, width), F32),
            jax.ShapeDtypeStruct((tokens, width), BF16),
            jax.ShapeDtypeStruct((width, width), BF16),
            jax.ShapeDtypeStruct((8, width), F32),
            jax.ShapeDtypeStruct((panels, 1, panel), F32),
            jax.ShapeDtypeStruct((panels, width, panel), BF16),
            jax.ShapeDtypeStruct((panels, panel, width), BF16),
        ],
        scratch_shapes=[
            pltpu.VMEM((tokens, width), F32),
            pltpu.VMEM((tokens, LANES), F32),
            pltpu.VMEM((tokens, width), BF16),
            pltpu.VMEM((panels, tokens, panel), BF16),
            pltpu.VMEM((panels, tokens, panel), F32),
            pltpu.VMEM((tokens, width), F32),
            pltpu.VMEM((tokens, width), BF16),
            pltpu.VMEM((tokens, panel), BF16),
        ],
        compiler_params=pltpu.CompilerParams(vmem_limit_bytes=60 << 20),
        cost_estimate=pl.CostEstimate(
            flops=2 * tokens * width * (6 * panels * panel + 3 * width),
            bytes_accessed=8 * panels * panel * width + 16 * tokens * width,
            transcendentals=2 * tokens * panels * panel,
        ),
        name="ffn",
    )(x, mixed, cot, wo, small, bias, w_in, w_out)


def document_of(positions, lengths, seq_len):
    count = lengths.shape[1]
    order = jnp.arange(count)
    ends = jnp.sum(jnp.where(order[None, :] <= order[:, None], lengths[:, None, :], 0), axis=2)
    counted = jnp.sum((positions[None, :, None] >= ends[:, None, :]).astype(jnp.int32), axis=2)
    inside = (positions >= 0) & (positions < seq_len)
    return jnp.where(inside[None, :], counted, -1)


def masks(lengths, offset, group, seq_len):
    ext = group + 2 * HALO
    slots = ext // 4
    positions = offset - HALO + jnp.arange(ext + PAD, dtype=jnp.int32)
    doc = document_of(positions, lengths, seq_len)
    slot_doc = doc[:, 2:ext:4]
    biases = []
    for block in range(group // QB):
        near = HALO - WIN // 2 + block * QB
        far = block * QB // 4
        key_place = jnp.concatenate((jnp.arange(near, near + NEAR), 4 * jnp.arange(far, far + FAR) + 2))
        reach = jnp.concatenate((jnp.full((NEAR,), WIN // 2), jnp.full((FAR,), PWIN // 2)))
        key_doc = jnp.concatenate((doc[:, near : near + NEAR], slot_doc[:, far : far + FAR]), axis=1)
        query_place = HALO + block * QB + jnp.arange(QB)
        query_doc = doc[:, HALO + block * QB : HALO + (block + 1) * QB]
        allowed = (jnp.abs(key_place[:, None] - query_place[None, :]) <= reach[:, None])[None] & (
            key_doc[:, :, None] == query_doc[:, None, :]
        )
        biases.append(jnp.where(allowed, 0.0, MASKED).astype(F32))
    same = jnp.stack(
        [(doc[:, tap : tap + ext : 4] == slot_doc).astype(F32) for tap in range(5)], axis=1
    )
    same = jnp.broadcast_to(same[..., None], same.shape + (LANES,))
    return jnp.stack(biases, axis=1), same, slots


def local(
    tokens,
    doc_lengths,
    query_weight,
    key_weight,
    value_weight,
    out_weight,
    pool_weight,
    first_gain,
    first_shift,
    inner_weight,
    inner_bias,
    outer_weight,
    outer_bias,
    second_gain,
    second_shift,
    cotangent,
):
    axes = ("dp", "seq")
    seq_count = lax.axis_size("seq")
    parts = lax.axis_size("dp") * seq_count
    seq_place = lax.axis_index("seq")
    seqs, group, width = tokens.shape
    ff = inner_weight.shape[1]
    panels = ff // width
    share = query_weight.shape[0]
    count = seqs * group
    ext = group + 2 * HALO + PAD

    def shift(value, by):
        pairs = [(i, i + by) for i in range(seq_count) if 0 <= i + by < seq_count]
        return lax.ppermute(value, "seq", pairs)

    vectors = jnp.concatenate(
        (
            pool_weight.reshape(-1),
            first_gain,
            first_shift,
            inner_bias,
            outer_bias,
            second_gain,
            second_shift,
        )
    )
    small_rows = -(-vectors.shape[0] // width)
    small_rows += -(3 * share + small_rows) % 8
    vectors_row = jnp.pad(vectors, (0, small_rows * width - vectors.shape[0])).reshape(small_rows, width)
    early = jnp.concatenate((query_weight, key_weight, value_weight, vectors_row), axis=0)
    late = jnp.concatenate(
        (
            out_weight,
            inner_weight.reshape(share, panels, width).transpose(1, 0, 2).reshape(-1, width),
            outer_weight,
        ),
        axis=0,
    )
    early = lax.all_gather(early, axes, axis=0)
    late = lax.all_gather(late, axes, axis=0)
    w_query, w_key, w_value = (
        early[:, i * share : (i + 1) * share].reshape(width, width) for i in range(3)
    )
    small = early[:, 3 * share :].reshape(parts, -1)
    w_out = late[:, :share].reshape(width, width)
    w_inner = (
        late[:, share : (1 + panels) * share]
        .reshape(parts, panels, share, width)
        .transpose(1, 0, 2, 3)
        .reshape(panels, width, width)
    )
    w_outer = late[:, (1 + panels) * share :].reshape(panels, width, width)
    taps = small[:, : 10 * share].reshape(parts, 10, share).transpose(1, 0, 2).reshape(10, width)
    taps = jnp.pad(taps.astype(F32), ((0, 6), (0, 0)))
    at = 10 * share
    vector_list = []
    for size in (share, share, ff // parts, share, share, share):
        vector_list.append(small[:, at : at + size].reshape(1, -1).astype(F32))
        at += size
    gain_one, shift_one, bias_inner, bias_outer, gain_two, shift_two = vector_list
    small_rows_f32 = jnp.concatenate(
        (gain_one, shift_one, bias_outer, gain_two, shift_two, jnp.zeros((3, width), F32)), axis=0
    )
    bias_inner = bias_inner.reshape(panels, 1, width)

    from_left = shift(tokens[:, group - HALO :], 1)
    from_right = shift(tokens[:, :HALO], -1)
    beyond = shift(tokens[:, :1], -2)
    x_ext = jnp.concatenate(
        (from_left, tokens, from_right, jnp.pad(beyond, ((0, 0), (0, PAD - 1), (0, 0)))), axis=1
    )
    flat = tokens.reshape(count, width)
    flat_ext = x_ext.reshape(seqs * ext, width)
    bias, same, slots = masks(doc_lengths, seq_place * group, group, group * seq_count)

    queries = nn(flat, w_query).astype(BF16).reshape(seqs, group, width)
    keys = nn(flat_ext, w_key).astype(BF16).reshape(seqs, ext, width)
    values = nn(flat_ext, w_value).astype(BF16).reshape(seqs, ext, width)
    mixed, lse = attention_forward(queries, keys, values, taps, same, bias)
    y, d_first, d_mixed, d_wo, d_small, d_bias, d_in, d_out = feed_forward(
        flat,
        mixed.reshape(count, width),
        cotangent.reshape(count, width),
        w_out,
        small_rows_f32,
        bias_inner,
        w_inner,
        w_outer,
    )
    late_grads = jnp.concatenate(
        (
            d_wo.reshape(parts, share, width),
            d_in.reshape(panels, parts, share, width)
            .transpose(1, 0, 2, 3)
            .reshape(parts, panels * share, width),
            d_out.reshape(parts, panels * share, width),
        ),
        axis=1,
    )
    late_sum = lax.psum_scatter(
        late_grads.reshape(-1, width), axes, scatter_dimension=0, tiled=True
    ).astype(F32)

    d_queries, d_keys, d_values, d_taps = attention_backward(
        queries, keys, values, taps, same, bias, lse, d_mixed.reshape(seqs, group, width)
    )
    d_queries = d_queries.reshape(count, width)
    d_keys = d_keys.reshape(seqs * ext, width)
    d_values = d_values.reshape(seqs * ext, width)
    d_ext = (nt(d_keys, w_key) + nt(d_values, w_value)).reshape(seqs, ext, width)
    right = HALO + group
    to_left = shift(d_ext[:, :HALO].astype(BF16), -1).astype(F32)
    to_right = shift(d_ext[:, right : right + HALO].astype(BF16), 1).astype(F32)
    to_beyond = shift(d_ext[:, right + HALO : right + HALO + 1].astype(BF16), 2).astype(F32)
    d_query_weight = tn(flat, d_queries).astype(BF16)
    d_key_weight = tn(flat_ext, d_keys).astype(BF16)
    d_value_weight = tn(flat_ext, d_values).astype(BF16)
    d_own = nt(d_queries, w_query) + d_first
    d_input = d_own.reshape(seqs, group, width) + d_ext[:, HALO:right]
    d_input = d_input + jnp.pad(to_left, ((0, 0), (group - HALO, 0), (0, 0)))
    d_input = d_input + jnp.pad(to_right, ((0, 0), (0, group - HALO), (0, 0)))
    d_input = d_input + jnp.pad(to_beyond, ((0, 0), (0, group - 1), (0, 0)))

    d_taps = jnp.sum(d_taps, axis=0)[:10]
    d_vectors = jnp.concatenate(
        [d_taps.reshape(10, parts, share).transpose(1, 0, 2).reshape(parts, 10 * share)]
        + [
            piece.reshape(parts, -1)
            for piece in (d_small[0], d_small[1], d_bias, d_small[2], d_small[3], d_small[4])
        ],
        axis=1,
    )
    d_vectors = jnp.pad(d_vectors, ((0, 0), (0, small_rows * width - d_vectors.shape[1])))
    early_grads = jnp.concatenate(
        [g.reshape(parts, share, width) for g in (d_query_weight, d_key_weight, d_value_weight)]
        + [d_vectors.astype(BF16).reshape(parts, small_rows, width)],
        axis=1,
    )
    early_sum = lax.psum_scatter(
        early_grads.reshape(-1, width), axes, scatter_dimension=0, tiled=True
    ).astype(F32)

    vector_sum = early_sum[3 * share :].reshape(-1)
    pieces = []
    at = 10 * share
    for size in (share, share, ff // parts, share, share, share):
        pieces.append(vector_sum[at : at + size])
        at += size
    return (
        y.reshape(seqs, group, width),
        d_input.astype(BF16),
        early_sum[:share],
        early_sum[share : 2 * share],
        early_sum[2 * share : 3 * share],
        late_sum[:share],
        vector_sum[: 10 * share].reshape(10, share),
        pieces[0],
        pieces[1],
        late_sum[share : (1 + panels) * share]
        .reshape(panels, share, width)
        .transpose(1, 0, 2)
        .reshape(share, ff),
        pieces[2],
        late_sum[(1 + panels) * share :],
        pieces[3],
        pieces[4],
        pieces[5],
    )


def solution(mesh):
    rows = P(("dp", "seq"), None)
    vector = P(("dp", "seq"))
    whole = P("dp", "seq", None)
    taps = P(None, ("dp", "seq"))
    weights = (rows, rows, rows, rows, taps, vector, vector, rows, vector, rows, vector, vector, vector)
    return jax.shard_map(
        local,
        mesh=mesh,
        in_specs=(whole, P("dp", None)) + weights + (whole,),
        out_specs=(whole, whole) + weights,
        check_vma=False,
    )
```

```python
import functools

import jax
import jax.numpy as jnp
from jax import lax
from jax.experimental import pallas as pl
from jax.experimental.pallas import tpu as pltpu
from jax.sharding import Mesh
from jax.sharding import PartitionSpec as P

HEADS = 12
HEAD_DIM = 64
WIN = 128
PWIN = 512
EPS = 1e-05

LANES = 128
QB = 128
GROUP = 6
GROUP_BACK = 2
HALO = PWIN // 2
PAD = 16
NEAR = QB + WIN
FAR = (QB + PWIN) // 4
KEYS = NEAR + FAR
MASKED = -1e30
QUICK = pl.CostEstimate(flops=1 << 20, bytes_accessed=1 << 20, transcendentals=0)

F32 = jnp.float32
BF16 = jnp.bfloat16


def nt(left, right):
    return lax.dot_general(left, right, (((1,), (1,)), ((), ())), preferred_element_type=F32)


def tn(left, right):
    return lax.dot_general(left, right, (((0,), (0,)), ((), ())), preferred_element_type=F32)


def nn(left, right):
    return lax.dot_general(left, right, (((1,), (0,)), ((), ())), preferred_element_type=F32)


def slot_taps(wide, slots):
    return [wide[pl.ds(tap, slots, stride=4), :] for tap in range(5)]


def pool(taps, same_ref, w_ref, first, lanes):
    total = None
    for tap in range(5):
        term = taps[tap] * same_ref[0, tap] * w_ref[first + tap : first + tap + 1, lanes]
        total = term if total is None else total + term
    return total.astype(BF16)


def pair_stack(rows):
    lane = lax.broadcasted_iota(jnp.int32, rows.shape, 1)
    zero = jnp.zeros_like(rows)
    return jnp.concatenate(
        (jnp.where(lane < HEAD_DIM, rows, zero), jnp.where(lane < HEAD_DIM, zero, rows)), axis=0
    )


def pair_join(both):
    joined = jnp.concatenate((both[:HEAD_DIM, :QB], both[HEAD_DIM:, QB:]), axis=0)
    return joined.T


def rows_of(block):
    return slice(block * QB, (block + 1) * QB)


def keys_of(ref, pooled, block, lanes):
    near = HALO - WIN // 2 + block * QB
    far = block * QB // 4
    return jnp.concatenate((ref[0, near : near + NEAR, lanes], pooled[far : far + FAR, :]), axis=0)


def scores_of(keys, stacked, bias):
    return nt(keys, stacked) + jnp.concatenate((bias, bias), axis=1)


def attn_fwd_kernel(
    q_ref, k_ref, v_ref, w_ref, same_ref, bias_ref, out_ref, lse_ref, k_wide, v_wide, pk_ref, pv_ref
):
    slots = pk_ref.shape[1]
    scale = jnp.asarray(HEAD_DIM**-0.5, BF16)

    blocks = q_ref.shape[1] // QB

    def body(step, carry):
        jobs = []
        for lane in range(GROUP):
            pair = step * GROUP + lane
            lanes = pl.ds(pl.multiple_of(pair * LANES, LANES), LANES)
            k_wide[lane] = k_ref[0, :, lanes].astype(F32)
            v_wide[lane] = v_ref[0, :, lanes].astype(F32)
            pk_ref[lane] = pool(slot_taps(k_wide.at[lane], slots), same_ref, w_ref, 0, lanes)
            pv_ref[lane] = pool(slot_taps(v_wide.at[lane], slots), same_ref, w_ref, 5, lanes)
            jobs += [(lane, pair, lanes, block) for block in range(blocks)]
        scores = []
        for lane, pair, lanes, block in jobs:
            stacked = pair_stack(q_ref[0, rows_of(block), lanes] * scale)
            keys = keys_of(k_ref, pk_ref.at[lane], block, lanes)
            scores.append(scores_of(keys, stacked, bias_ref[0, block]))
        probs = []
        for (lane, pair, lanes, block), score in zip(jobs, scores):
            top = jnp.max(score, axis=0, keepdims=True)
            weights = jnp.exp(score - top)
            denom = jnp.sum(weights, axis=0, keepdims=True)
            probs.append((weights * (1.0 / denom)).astype(BF16))
            lse_ref[0, pair, block : block + 1, :] = top + jnp.log(denom)
        mixed = []
        for (lane, pair, lanes, block), prob in zip(jobs, probs):
            mixed.append(tn(keys_of(v_ref, pv_ref.at[lane], block, lanes), prob))
        for (lane, pair, lanes, block), value in zip(jobs, mixed):
            out_ref[0, rows_of(block), lanes] = pair_join(value).astype(BF16)
        return carry

    lax.fori_loop(0, q_ref.shape[2] // (LANES * GROUP), body, 0)


def attn_bwd_kernel(
    q_ref,
    k_ref,
    v_ref,
    w_ref,
    same_ref,
    bias_ref,
    lse_ref,
    do_ref,
    dq_ref,
    dk_ref,
    dv_ref,
    dw_ref,
    k_wide,
    v_wide,
    pk_ref,
    pv_ref,
    dpk_ref,
    dpv_ref,
):
    slots = pk_ref.shape[1]
    scale = jnp.asarray(HEAD_DIM**-0.5, BF16)
    blocks = q_ref.shape[1] // QB

    def body(step, carry):
        jobs = []
        for lane in range(GROUP_BACK):
            pair = step * GROUP_BACK + lane
            lanes = pl.ds(pl.multiple_of(pair * LANES, LANES), LANES)
            k_wide[lane] = k_ref[0, :, lanes].astype(F32)
            v_wide[lane] = v_ref[0, :, lanes].astype(F32)
            pk_ref[lane] = pool(slot_taps(k_wide.at[lane], slots), same_ref, w_ref, 0, lanes)
            pv_ref[lane] = pool(slot_taps(v_wide.at[lane], slots), same_ref, w_ref, 5, lanes)
            jobs += [(lane, pair, lanes, block) for block in range(blocks)]
        dpk_ref[...] = jnp.zeros_like(dpk_ref)
        dpv_ref[...] = jnp.zeros_like(dpv_ref)
        scores, d_probs = [], []
        for lane, pair, lanes, block in jobs:
            keys = keys_of(k_ref, pk_ref.at[lane], block, lanes)
            stacked = pair_stack(q_ref[0, rows_of(block), lanes] * scale)
            scores.append(scores_of(keys, stacked, bias_ref[0, block]))
            values = keys_of(v_ref, pv_ref.at[lane], block, lanes)
            d_probs.append(nt(values, pair_stack(do_ref[0, rows_of(block), lanes])))
        probs, d_scores = [], []
        for (lane, pair, lanes, block), score, d_prob in zip(jobs, scores, d_probs):
            prob = jnp.exp(score - lse_ref[0, pair, block : block + 1, :])
            row_dot = jnp.sum(prob * d_prob, axis=0, keepdims=True)
            d_scores.append((prob * (d_prob - row_dot)).astype(BF16))
            probs.append(prob.astype(BF16))
        parts = []
        for (lane, pair, lanes, block), prob, d_score in zip(jobs, probs, d_scores):
            d_values = nn(prob, pair_stack(do_ref[0, rows_of(block), lanes]))
            d_keys = nn(d_score, pair_stack(q_ref[0, rows_of(block), lanes] * scale))
            far = slice(block * QB // 4, block * QB // 4 + FAR)
            dpk_ref[lane, far, :] += d_keys[NEAR:]
            dpv_ref[lane, far, :] += d_values[NEAR:]
            parts.append((d_keys[:NEAR], d_values[:NEAR]))
        d_queries = []
        for (lane, pair, lanes, block), d_score in zip(jobs, d_scores):
            d_queries.append(tn(keys_of(k_ref, pk_ref.at[lane], block, lanes), d_score))
        for (lane, pair, lanes, block), value in zip(jobs, d_queries):
            dq_ref[0, rows_of(block), lanes] = (pair_join(value) * HEAD_DIM**-0.5).astype(BF16)
        for lane in range(GROUP_BACK):
            lanes = jobs[lane * blocks][2]
            for side, (wide_ref, d_pool_ref, out_ref) in enumerate(
                ((k_wide, dpk_ref, dk_ref), (v_wide, dpv_ref, dv_ref))
            ):
                wide = wide_ref.at[lane]
                d_pool = d_pool_ref[lane]
                taps = slot_taps(wide, slots)
                masked = [d_pool * same_ref[0, tap] for tap in range(5)]
                places = [5 * side + tap for tap in range(5)]
                for tap, row in enumerate(places):
                    dw_ref[0, row : row + 1, lanes] = jnp.sum(
                        masked[tap] * taps[tap], axis=0, keepdims=True
                    )
                spread = [
                    masked[tap] * w_ref[row : row + 1, lanes] for tap, row in enumerate(places)
                ]
                wide[4 * slots :, :] = jnp.zeros((wide.shape[0] - 4 * slots, LANES), F32)
                for tap in range(4):
                    wide[pl.ds(tap, slots, stride=4), :] = spread[tap]
                wide[pl.ds(4, slots, stride=4), :] += spread[4]
                for block in range(blocks):
                    near = HALO - WIN // 2 + block * QB
                    wide[near : near + NEAR, :] += parts[lane * blocks + block][side]
                out_ref[0, :, lanes] = wide[...].astype(BF16)
        return carry

    lax.fori_loop(0, q_ref.shape[2] // (LANES * GROUP_BACK), body, 0)
    dw_ref[0, 10:, :] = jnp.zeros((dw_ref.shape[1] - 10, dw_ref.shape[2]), F32)


def by_seq(*shape, first=0):
    return pl.BlockSpec((1,) + shape, lambda s: (s + first,) + (0,) * len(shape))


def attention_specs(ext, group, slots, width, first=0):
    return [
        by_seq(group, width, first=first),
        by_seq(ext, width, first=first),
        by_seq(ext, width, first=first),
        pl.BlockSpec((16, width), lambda s: (0, 0)),
        by_seq(5, slots, LANES, first=first),
        by_seq(group // QB, KEYS, LANES, first=first),
    ]


def attention_forward(queries, keys, values, taps, same, bias):
    seqs, group, width = queries.shape
    ext = keys.shape[1]
    slots = same.shape[2]
    pairs = width // LANES
    blocks = group // QB
    wide = pltpu.VMEM((GROUP, ext, LANES), F32)
    pooled = pltpu.VMEM((GROUP, slots, LANES), BF16)
    return pl.pallas_call(
        attn_fwd_kernel,
        grid=(seqs,),
        in_specs=attention_specs(ext, group, slots, width),
        out_specs=[by_seq(group, width), by_seq(pairs, blocks, 2 * QB)],
        out_shape=[
            jax.ShapeDtypeStruct((seqs, group, width), BF16),
            jax.ShapeDtypeStruct((seqs, pairs, blocks, 2 * QB), F32),
        ],
        scratch_shapes=[wide, wide, pooled, pooled],
        compiler_params=pltpu.CompilerParams(vmem_limit_bytes=48 << 20),
        cost_estimate=QUICK,
        name="attn_fwd",
    )(queries, keys, values, taps, same, bias)


def attention_backward(queries, keys, values, taps, same, bias, lse, d_mixed, first, count, earlier):
    seqs, group, width = queries.shape
    ext = keys.shape[1]
    slots = same.shape[2]
    pairs = width // LANES
    blocks = group // QB
    wide = pltpu.VMEM((GROUP_BACK, ext, LANES), F32)
    pooled = pltpu.VMEM((GROUP_BACK, slots, LANES), BF16)
    d_pooled = pltpu.VMEM((GROUP_BACK, slots, LANES), F32)
    args = (queries, keys, values, taps, same, bias, lse, d_mixed)

    def kernel(*refs):
        attn_bwd_kernel(*refs[: len(args)], *refs[len(args) + len(earlier) :])

    return pl.pallas_call(
        kernel,
        grid=(count,),
        in_specs=attention_specs(ext, group, slots, width, first)
        + [by_seq(pairs, blocks, 2 * QB, first=first), by_seq(group, width, first=first)]
        + [pl.BlockSpec(memory_space=pl.ANY)] * len(earlier),
        out_specs=[
            by_seq(*shape, first=first)
            for shape in ((group, width), (ext, width), (ext, width), (16, width))
        ],
        out_shape=[
            jax.ShapeDtypeStruct((seqs, group, width), BF16),
            jax.ShapeDtypeStruct((seqs, ext, width), BF16),
            jax.ShapeDtypeStruct((seqs, ext, width), BF16),
            jax.ShapeDtypeStruct((seqs, 16, width), F32),
        ],
        input_output_aliases={len(args) + i: i for i in range(len(earlier))},
        scratch_shapes=[wide, wide, pooled, pooled, d_pooled, d_pooled],
        compiler_params=pltpu.CompilerParams(vmem_limit_bytes=48 << 20),
        cost_estimate=QUICK,
        name="attn_bwd",
    )(*args, *earlier)


ROWS = 1024
HALF_PI = 0.3989422804014327


def row_sum(value):
    return jnp.sum(value, axis=0, keepdims=True)


def row_mean(value):
    return jnp.mean(value, axis=1, keepdims=True)


def normalize(value):
    centered = value - row_mean(value)
    inv = lax.rsqrt(row_mean(centered * centered) + EPS)
    return centered * inv, inv


def normalize_back(grad, normed, inv):
    return inv * (grad - row_mean(grad) - normed * row_mean(grad * normed))


def split_cores(value, core, per_core):
    both = value.reshape(-1, 2, per_core, value.shape[1])
    mine = jnp.where(core == 0, both[:, 0], both[:, 1])
    other = jnp.where(core == 0, both[:, 1], both[:, 0])
    return mine.astype(BF16), other.astype(BF16)


def ffn_kernel(
    panels,
    core_ref,
    x_ref,
    mixed_ref,
    cot_ref,
    wo_ref,
    small_ref,
    bias_ref,
    w_in_ref,
    w_out_ref,
    y_ref,
    d_first_ref,
    d_mixed_ref,
    d_small_ref,
    d_bias_ref,
    d_wo_ref,
    d_wo_other_ref,
    d_in_ref,
    d_in_other_ref,
    d_out_ref,
    d_out_other_ref,
    n_one,
    inv_one,
    low,
    hidden,
    slope,
    d_inner,
):
    step = pl.program_id(0)
    tokens, width = x_ref.shape
    chunks = tokens // ROWS
    acc, d_outer = d_first_ref, d_mixed_ref
    core = core_ref[0]
    rows_in, rows_out = d_in_ref.shape[2], d_out_ref.shape[1]

    def square(ref):
        return ref[...].reshape(width, width)

    gain_one, shift_one, outer_bias, gain_two, shift_two = (
        small_ref[i : i + 1, :] for i in range(5)
    )

    @pl.when(step == 0)
    def _():
        def body(i, carry):
            rows = pl.ds(pl.multiple_of(i * ROWS, ROWS), ROWS)
            first = x_ref[rows, :].astype(F32) + nn(mixed_ref[rows, :], square(wo_ref))
            normed, inv = normalize(first)
            n_one[rows, :] = normed
            inv_one[rows, :] = jnp.broadcast_to(inv, (ROWS, LANES))
            out = normed * gain_one + shift_one
            low[rows, :] = out.astype(BF16)
            acc[rows, :] = out + outer_bias
            return carry

        lax.fori_loop(0, chunks, body, 0)

    @pl.when(step < panels)
    def _():
        def body(i, carry):
            rows = pl.ds(pl.multiple_of(i * ROWS, ROWS), ROWS)
            inner = nn(low[rows, :], square(w_in_ref)) + bias_ref[0]
            cdf = 0.5 * (1.0 + lax.erf(inner * 0.7071067811865476))
            pdf = HALF_PI * jnp.exp(-0.5 * inner * inner)
            out = (inner * cdf).astype(BF16)
            hidden[step, rows, :] = out
            slope[step, rows, :] = cdf + inner * pdf
            acc[rows, :] += nn(out, square(w_out_ref))
            return carry

        lax.fori_loop(0, chunks, body, 0)

    @pl.when(step == panels)
    def _():
        def body(i, carry):
            d_gain, d_shift, d_bias = carry
            rows = pl.ds(pl.multiple_of(i * ROWS, ROWS), ROWS)
            normed, inv = normalize(acc[rows, :])
            y_ref[rows, :] = (normed * gain_two + shift_two).astype(BF16)
            grad = cot_ref[rows, :].astype(F32)
            d_second = normalize_back(grad * gain_two, normed, inv)
            low_grad = d_second.astype(BF16)
            acc[rows, :] = d_second
            d_outer[rows, :] = low_grad
            return (
                d_gain + row_sum(grad * normed),
                d_shift + row_sum(grad),
                d_bias + row_sum(low_grad.astype(F32)),
            )

        zero = jnp.zeros((1, width), F32)
        d_gain, d_shift, d_bias = lax.fori_loop(0, chunks, body, (zero, zero, zero))
        d_small_ref[2:3, :] = d_bias
        d_small_ref[3:4, :] = d_gain
        d_small_ref[4:5, :] = d_shift
        d_small_ref[5:, :] = jnp.zeros((3, width), F32)

    @pl.when(step >= panels)
    def _():
        panel = step - panels

        def body(i, d_bias):
            rows = pl.ds(pl.multiple_of(i * ROWS, ROWS), ROWS)
            d_hidden = nt(d_outer[rows, :], square(w_out_ref))
            grad = (d_hidden * slope[panel, rows, :]).astype(BF16)
            d_inner[rows, :] = grad
            acc[rows, :] += nt(grad, square(w_in_ref))
            return d_bias + row_sum(grad.astype(F32))

        d_bias_ref[0] = lax.fori_loop(0, chunks, body, jnp.zeros(d_bias_ref.shape[1:], F32))
        d_out_ref[...], d_out_other_ref[...] = split_cores(
            tn(hidden[panel], d_outer[...]), core, rows_out
        )
        d_in_ref[:, 0], d_in_other_ref[:, 0] = split_cores(
            tn(low[...], d_inner[...]), core, rows_in
        )

    @pl.when(step == 2 * panels - 1)
    def _():
        def body(i, carry):
            d_gain, d_shift = carry
            rows = pl.ds(pl.multiple_of(i * ROWS, ROWS), ROWS)
            grad = acc[rows, :]
            normed = n_one[rows, :]
            d_first = normalize_back(grad * gain_one, normed, inv_one[rows, 0:1])
            d_first_ref[rows, :] = d_first
            low_grad = d_first.astype(BF16)
            d_inner[rows, :] = low_grad
            d_mixed_ref[rows, :] = nt(low_grad, square(wo_ref)).astype(BF16)
            return d_gain + row_sum(grad * normed), d_shift + row_sum(grad)

        zero = jnp.zeros((1, width), F32)
        d_gain, d_shift = lax.fori_loop(0, chunks, body, (zero, zero))
        d_small_ref[0:1, :] = d_gain
        d_small_ref[1:2, :] = d_shift
        d_wo_ref[...], d_wo_other_ref[...] = split_cores(
            tn(mixed_ref[...], d_inner[...]), core, rows_in
        )


def feed_forward(core, x, mixed, cot, small, bias, weights):
    tokens, width = x.shape
    units, groups, rows_in, _ = weights.shape
    panels = groups // 2
    panel = width
    chips = units // 2
    rows_out = panels * rows_in

    def whole(*shape):
        return pl.BlockSpec(
            shape, lambda j: (0,) * len(shape), pipeline_mode=pl.Buffered(buffer_count=1)
        )

    def later(j):
        return jnp.maximum(j - panels, 0)

    d_in = pl.BlockSpec((chips, 1, rows_in, width), lambda j: (0, later(j), 0, 0))
    d_out = pl.BlockSpec((chips // panels, rows_out, width), lambda j: (later(j), 0, 0))
    return pl.pallas_call(
        functools.partial(ffn_kernel, panels),
        grid=(2 * panels,),
        in_specs=[
            pl.BlockSpec(memory_space=pltpu.SMEM),
            whole(tokens, width),
            whole(tokens, width),
            whole(tokens, width),
            pl.BlockSpec(
                (units, 1, rows_in, width),
                lambda j: (0, 2 * panels, 0, 0),
                pipeline_mode=pl.Buffered(buffer_count=1),
            ),
            whole(8, width),
            pl.BlockSpec((1, 1, panel), lambda j: (lax.rem(j, panels), 0, 0)),
            pl.BlockSpec((units, 1, rows_in, width), lambda j: (0, panels + lax.rem(j, panels), 0, 0)),
            pl.BlockSpec(
                (units // panels, panels, rows_in, width), lambda j: (lax.rem(j, panels), 0, 0, 0)
            ),
        ],
        out_specs=[
            whole(tokens, width),
            whole(tokens, width),
            whole(tokens, width),
            whole(8, width),
            pl.BlockSpec((1, 1, panel), lambda j: (later(j), 0, 0)),
            whole(chips, rows_in, width),
            whole(chips, rows_in, width),
            d_in,
            d_in,
            d_out,
            d_out,
        ],
        out_shape=[
            jax.ShapeDtypeStruct((tokens, width), BF16),
            jax.ShapeDtypeStruct((tokens, width), F32),
            jax.ShapeDtypeStruct((tokens, width), BF16),
            jax.ShapeDtypeStruct((8, width), F32),
            jax.ShapeDtypeStruct((panels, 1, panel), F32),
        ]
        + [jax.ShapeDtypeStruct((chips, rows_in, width), BF16)] * 2
        + [jax.ShapeDtypeStruct((chips, panels, rows_in, width), BF16)] * 2
        + [jax.ShapeDtypeStruct((chips, rows_out, width), BF16)] * 2,
        scratch_shapes=[
            pltpu.VMEM((tokens, width), F32),
            pltpu.VMEM((tokens, LANES), F32),
            pltpu.VMEM((tokens, width), BF16),
            pltpu.VMEM((panels, tokens, panel), BF16),
            pltpu.VMEM((panels, tokens, panel), F32),
            pltpu.VMEM((tokens, panel), BF16),
        ],
        compiler_params=pltpu.CompilerParams(vmem_limit_bytes=60 << 20),
        cost_estimate=QUICK,
        name="ffn",
    )(core, x, mixed, cot, weights, small, bias, weights, weights)


def document_of(positions, lengths, seq_len):
    count = lengths.shape[1]
    order = jnp.arange(count)
    ends = jnp.sum(jnp.where(order[None, :] <= order[:, None], lengths[:, None, :], 0), axis=2)
    counted = jnp.sum((positions[None, :, None] >= ends[:, None, :]).astype(jnp.int32), axis=2)
    inside = (positions >= 0) & (positions < seq_len)
    return jnp.where(inside[None, :], counted, -1)


def masks(lengths, offset, group, seq_len):
    ext = group + 2 * HALO
    slots = ext // 4
    positions = offset - HALO + jnp.arange(ext + PAD, dtype=jnp.int32)
    doc = document_of(positions, lengths, seq_len)
    slot_doc = doc[:, 2:ext:4]
    biases = []
    for block in range(group // QB):
        near = HALO - WIN // 2 + block * QB
        far = block * QB // 4
        key_place = jnp.concatenate((jnp.arange(near, near + NEAR), 4 * jnp.arange(far, far + FAR) + 2))
        reach = jnp.concatenate((jnp.full((NEAR,), WIN // 2), jnp.full((FAR,), PWIN // 2)))
        key_doc = jnp.concatenate((doc[:, near : near + NEAR], slot_doc[:, far : far + FAR]), axis=1)
        query_place = HALO + block * QB + jnp.arange(QB)
        query_doc = doc[:, HALO + block * QB : HALO + (block + 1) * QB]
        allowed = (jnp.abs(key_place[:, None] - query_place[None, :]) <= reach[:, None])[None] & (
            key_doc[:, :, None] == query_doc[:, None, :]
        )
        biases.append(jnp.where(allowed, 0.0, MASKED).astype(F32))
    same = jnp.stack(
        [(doc[:, tap : tap + ext : 4] == slot_doc).astype(F32) for tap in range(5)], axis=1
    )
    same = jnp.broadcast_to(same[..., None], same.shape + (LANES,))
    return jnp.stack(biases, axis=1), same, slots


def steps(count):
    for k in range(1, count):
        if count & (count - 1) == 0:
            yield [(i, i ^ k) for i in range(count)], lambda me, k=k: (me ^ k, me ^ k)
        else:
            yield (
                [(i, (i + k) % count) for i in range(count)],
                lambda me, k=k: (lax.rem(me + k, count), lax.rem(me - k + count, count)),
            )


def pick(value, index, dim=0):
    return lax.dynamic_index_in_dim(value, index, dim, keepdims=False)


def gather_seq(block):
    count, me = lax.axis_size("seq"), lax.axis_index("seq")
    zeros = (0,) * block.ndim
    column = jnp.zeros((count,) + block.shape, block.dtype)
    column = lax.dynamic_update_slice(column, block[None], (me,) + zeros)
    for pairs, met in steps(count):
        came = lax.ppermute(block, "seq", pairs)
        column = lax.dynamic_update_slice(column, came[None], (met(me)[1],) + zeros)
    return column


def gather_yx(column):
    me = lax.axis_index("yx")
    pieces = [(column, me)]
    for pairs, met in steps(lax.axis_size("yx")):
        pieces.append((lax.ppermute(column, "yx", pairs), met(me)[1]))
    return pieces


def gather_core(pieces):
    count, me = lax.axis_size("core"), lax.axis_index("core")
    shape = pieces[0][0].shape
    zeros = (0,) * len(shape)
    whole = jnp.zeros((len(pieces), count) + shape, pieces[0][0].dtype)
    for piece, place in pieces:
        whole = lax.dynamic_update_slice(whole, piece[None, None], (place, me) + zeros)
        for pairs, met in steps(count):
            other = lax.ppermute(piece, "core", pairs)
            whole = lax.dynamic_update_slice(whole, other[None, None], (place, met(me)[1]) + zeros)
    return whole.reshape((-1,) + shape[1:])


def after(value, *earlier):
    return lax.optimization_barrier((value,) + earlier)[0]


def exchange_sum(pieces, axis):
    me = lax.axis_index(axis)
    total = pick(pieces, me).astype(F32)
    for pairs, met in steps(lax.axis_size(axis)):
        total = total + lax.ppermute(pick(pieces, met(me)[0]), axis, pairs).astype(F32)
    return total


def scatter_sum(value):
    total = exchange_sum(value.swapaxes(0, 1), "core").astype(BF16)
    total = exchange_sum(total, "yx").astype(BF16)
    return exchange_sum(total, "seq")


def local(
    tokens,
    doc_lengths,
    query_weight,
    key_weight,
    value_weight,
    out_weight,
    pool_weight,
    first_gain,
    first_shift,
    inner_weight,
    inner_bias,
    outer_weight,
    outer_bias,
    second_gain,
    second_shift,
    cotangent,
):
    seq_count = lax.axis_size("seq")
    yx_count = lax.axis_size("yx")
    core_count = lax.axis_size("core")
    units = yx_count * core_count
    parts = units * seq_count
    seq_place = lax.axis_index("seq")
    seqs, group, width = tokens.shape
    ff = inner_weight.shape[1]
    panels = ff // width
    share = query_weight.shape[0]
    count = seqs * group
    ext = group + 2 * HALO + PAD

    def shift(value, by):
        pairs = [(i, i + by) for i in range(seq_count) if 0 <= i + by < seq_count]
        return lax.ppermute(value, "seq", pairs)

    vectors = jnp.concatenate(
        (
            pool_weight.reshape(-1),
            first_gain,
            first_shift,
            inner_bias,
            outer_bias,
            second_gain,
            second_shift,
        )
    )
    small_rows = -(-vectors.shape[0] // width)
    small_rows += -(3 * share + small_rows) % 8
    vectors_row = jnp.pad(vectors, (0, small_rows * width - vectors.shape[0])).reshape(small_rows, width)
    early = jnp.concatenate((query_weight, key_weight, value_weight, vectors_row), axis=0)
    late = jnp.concatenate(
        (
            outer_weight,
            inner_weight.reshape(share, panels, width).transpose(1, 0, 2).reshape(-1, width),
            out_weight,
        ),
        axis=0,
    )
    early_column = gather_seq(early)
    late_column = gather_seq(after(late, early_column))
    early_pieces = gather_yx(early_column)
    early = gather_core(early_pieces)
    sent = after(tokens, late_column)
    outer_rows = panels * share
    late_column = jnp.concatenate(
        (
            late_column[:, :outer_rows].reshape(-1, width),
            late_column[:, outer_rows:]
            .reshape(seq_count, panels + 1, share, width)
            .swapaxes(0, 1)
            .reshape(-1, width),
        ),
        axis=0,
    )
    late = lax.all_gather(late_column, ("yx", "core"), axis=0)
    late = late.reshape(units, 2 * panels + 1, seq_count * share, width)
    w_query, w_key, w_value = (
        early[:, i * share : (i + 1) * share].reshape(width, width) for i in range(3)
    )
    small = early[:, 3 * share :].reshape(parts, -1)
    taps = small[:, : 10 * share].reshape(parts, 10, share).transpose(1, 0, 2).reshape(10, width)
    taps = jnp.pad(taps.astype(F32), ((0, 6), (0, 0)))
    at = 10 * share
    vector_list = []
    for size in (share, share, ff // parts, share, share, share):
        vector_list.append(small[:, at : at + size].reshape(1, -1).astype(F32))
        at += size
    gain_one, shift_one, bias_inner, bias_outer, gain_two, shift_two = vector_list
    small_rows_f32 = jnp.concatenate(
        (gain_one, shift_one, bias_outer, gain_two, shift_two, jnp.zeros((3, width), F32)), axis=0
    )
    bias_inner = bias_inner.reshape(panels, 1, width)

    from_left = shift(sent[:, group - HALO :], 1)
    from_right = shift(sent[:, :HALO], -1)
    beyond = shift(sent[:, :1], -2)
    x_ext = jnp.concatenate(
        (from_left, tokens, from_right, jnp.pad(beyond, ((0, 0), (0, PAD - 1), (0, 0)))), axis=1
    )
    flat = tokens.reshape(count, width)
    flat_ext = x_ext.reshape(seqs * ext, width)
    bias, same, slots = masks(doc_lengths, seq_place * group, group, group * seq_count)

    queries = nn(flat, w_query).astype(BF16).reshape(seqs, group, width)
    keys = nn(flat_ext, w_key).astype(BF16).reshape(seqs, ext, width)
    values = nn(flat_ext, w_value).astype(BF16).reshape(seqs, ext, width)
    mixed, lse = attention_forward(queries, keys, values, taps, same, bias)
    core = lax.axis_index("core")
    y, d_first, d_mixed, d_small, d_bias, *d_late = feed_forward(
        core.astype(jnp.int32).reshape(1),
        flat,
        mixed.reshape(count, width),
        cotangent.reshape(count, width),
        small_rows_f32,
        bias_inner,
        late,
    )
    swap = [(0, 1), (1, 0)]
    came = [lax.ppermute(part, "core", swap) for part in d_late[1::2]]
    back = (queries, keys, values, taps, same, bias, lse)
    d_mixed = d_mixed.reshape(seqs, group, width)
    half = seqs // 2
    d_half = attention_backward(*back, after(d_mixed, *d_late), 0, half, ())
    d_late = [
        (mine.astype(F32) + other.astype(F32)).astype(BF16).reshape(yx_count, -1, width)
        for mine, other in zip(d_late[0::2], after(tuple(came), *d_half))
    ]
    d_late = jnp.concatenate(d_late[::-1], axis=1)
    late_sum = lax.psum_scatter(d_late.reshape(-1, width), "yx", scatter_dimension=0, tiled=True)
    d_queries, d_keys, d_values, d_taps = attention_backward(
        *back, after(d_mixed, d_late), half, seqs - half, d_half
    )
    outer_all = seq_count * outer_rows
    late_sum = jnp.concatenate(
        (
            late_sum[:outer_all].reshape(seq_count, outer_rows, width),
            late_sum[outer_all:]
            .reshape(panels + 1, seq_count, share, width)
            .swapaxes(0, 1)
            .reshape(seq_count, (panels + 1) * share, width),
        ),
        axis=1,
    )
    late_sum = exchange_sum(late_sum, "seq")
    d_queries = d_queries.reshape(count, width)
    d_keys = d_keys.reshape(seqs * ext, width)
    d_values = d_values.reshape(seqs * ext, width)
    d_ext = (nt(d_keys, w_key) + nt(d_values, w_value)).reshape(seqs, ext, width)
    right = HALO + group
    to_left = shift(d_ext[:, :HALO].astype(BF16), -1).astype(F32)
    to_right = shift(d_ext[:, right : right + HALO].astype(BF16), 1).astype(F32)
    to_beyond = shift(d_ext[:, right + HALO : right + HALO + 1].astype(BF16), 2).astype(F32)
    d_query_weight = tn(flat, d_queries).astype(BF16)
    d_key_weight = tn(flat_ext, d_keys).astype(BF16)
    d_value_weight = tn(flat_ext, d_values).astype(BF16)
    d_own = nt(d_queries, w_query) + d_first
    d_input = d_own.reshape(seqs, group, width) + d_ext[:, HALO:right]
    d_input = d_input + jnp.pad(to_left, ((0, 0), (group - HALO, 0), (0, 0)))
    d_input = d_input + jnp.pad(to_right, ((0, 0), (0, group - HALO), (0, 0)))
    d_input = d_input + jnp.pad(to_beyond, ((0, 0), (0, group - 1), (0, 0)))

    d_taps = jnp.sum(d_taps, axis=0)[:10]
    d_vectors = jnp.concatenate(
        [d_taps.reshape(10, parts, share).transpose(1, 0, 2).reshape(parts, 10 * share)]
        + [
            piece.reshape(parts, -1)
            for piece in (d_small[0], d_small[1], d_bias, d_small[2], d_small[3], d_small[4])
        ],
        axis=1,
    )
    d_vectors = jnp.pad(d_vectors, ((0, 0), (0, small_rows * width - d_vectors.shape[1])))
    early_grads = jnp.concatenate(
        [g.reshape(parts, share, width) for g in (d_query_weight, d_key_weight, d_value_weight)]
        + [d_vectors.astype(BF16).reshape(parts, small_rows, width)],
        axis=1,
    )
    early_sum = scatter_sum(early_grads.reshape(yx_count, core_count, seq_count, -1, width))

    vector_sum = early_sum[3 * share :].reshape(-1)
    pieces = []
    at = 10 * share
    for size in (share, share, ff // parts, share, share, share):
        pieces.append(vector_sum[at : at + size])
        at += size
    return (
        y.reshape(seqs, group, width),
        d_input.astype(BF16),
        early_sum[:share],
        early_sum[share : 2 * share],
        early_sum[2 * share : 3 * share],
        late_sum[2 * outer_rows :],
        vector_sum[: 10 * share].reshape(10, share),
        pieces[0],
        pieces[1],
        late_sum[outer_rows : 2 * outer_rows]
        .reshape(panels, share, width)
        .transpose(1, 0, 2)
        .reshape(share, ff),
        pieces[2],
        late_sum[:outer_rows],
        pieces[3],
        pieces[4],
        pieces[5],
    )


def solution(mesh):
    dp, seq = mesh.devices.shape
    cores = 2 if dp % 2 == 0 else 1
    mesh = Mesh(mesh.devices.reshape(dp // cores, cores, seq), ("yx", "core", "seq"))
    every = ("yx", "core", "seq")
    rows = P(every, None)
    vector = P(every)
    whole = P(("yx", "core"), "seq", None)
    taps = P(None, every)
    weights = (rows, rows, rows, rows, taps, vector, vector, rows, vector, rows, vector, vector, vector)
    return jax.shard_map(
        local,
        mesh=mesh,
        in_specs=(whole, P(("yx", "core"), None)) + weights + (whole,),
        out_specs=(whole, whole) + weights,
        check_vma=False,
    )
```

```python
import functools

import jax
import jax.numpy as jnp
from jax import lax
from jax.experimental import pallas as pl
from jax.experimental.pallas import tpu as pltpu
from jax.sharding import Mesh
from jax.sharding import PartitionSpec as P

HEADS = 12
HEAD_DIM = 64
WIN = 128
PWIN = 512
EPS = 1e-05

LANES = 128
QB = 128
GROUP = 6
GROUP_BACK = 2
HALO = PWIN // 2
PAD = 16
NEAR = QB + WIN
FAR = (QB + PWIN) // 4
KEYS = NEAR + FAR
MASKED = -1e30
QUICK = pl.CostEstimate(flops=1 << 20, bytes_accessed=1 << 20, transcendentals=0)

F32 = jnp.float32
BF16 = jnp.bfloat16


def nt(left, right):
    return lax.dot_general(left, right, (((1,), (1,)), ((), ())), preferred_element_type=F32)


def tn(left, right):
    return lax.dot_general(left, right, (((0,), (0,)), ((), ())), preferred_element_type=F32)


def nn(left, right):
    return lax.dot_general(left, right, (((1,), (0,)), ((), ())), preferred_element_type=F32)


def slot_taps(wide, slots):
    return [wide[pl.ds(tap, slots, stride=4), :] for tap in range(5)]


def pool(taps, same_ref, w_ref, first, lanes):
    total = None
    for tap in range(5):
        term = taps[tap] * same_ref[0, tap] * w_ref[first + tap : first + tap + 1, lanes]
        total = term if total is None else total + term
    return total.astype(BF16)


def pair_stack(rows):
    lane = lax.broadcasted_iota(jnp.int32, rows.shape, 1)
    zero = jnp.zeros_like(rows)
    return jnp.concatenate(
        (jnp.where(lane < HEAD_DIM, rows, zero), jnp.where(lane < HEAD_DIM, zero, rows)), axis=0
    )


def pair_join(both):
    joined = jnp.concatenate((both[:HEAD_DIM, :QB], both[HEAD_DIM:, QB:]), axis=0)
    return joined.T


def rows_of(block):
    return slice(block * QB, (block + 1) * QB)


def keys_of(ref, pooled, block, lanes):
    near = HALO - WIN // 2 + block * QB
    far = block * QB // 4
    return jnp.concatenate((ref[0, near : near + NEAR, lanes], pooled[far : far + FAR, :]), axis=0)


def scores_of(keys, stacked, bias):
    return nt(keys, stacked) + jnp.concatenate((bias, bias), axis=1)


def attn_fwd_kernel(
    q_ref, k_ref, v_ref, w_ref, same_ref, bias_ref, out_ref, lse_ref, k_wide, v_wide, pk_ref, pv_ref
):
    slots = pk_ref.shape[1]
    scale = jnp.asarray(HEAD_DIM**-0.5, BF16)

    blocks = q_ref.shape[1] // QB

    def body(step, carry):
        jobs = []
        for lane in range(GROUP):
            pair = step * GROUP + lane
            lanes = pl.ds(pl.multiple_of(pair * LANES, LANES), LANES)
            k_wide[lane] = k_ref[0, :, lanes].astype(F32)
            v_wide[lane] = v_ref[0, :, lanes].astype(F32)
            pk_ref[lane] = pool(slot_taps(k_wide.at[lane], slots), same_ref, w_ref, 0, lanes)
            pv_ref[lane] = pool(slot_taps(v_wide.at[lane], slots), same_ref, w_ref, 5, lanes)
            jobs += [(lane, pair, lanes, block) for block in range(blocks)]
        scores = []
        for lane, pair, lanes, block in jobs:
            stacked = pair_stack(q_ref[0, rows_of(block), lanes] * scale)
            keys = keys_of(k_ref, pk_ref.at[lane], block, lanes)
            scores.append(scores_of(keys, stacked, bias_ref[0, block]))
        probs = []
        for (lane, pair, lanes, block), score in zip(jobs, scores):
            top = jnp.max(score, axis=0, keepdims=True)
            weights = jnp.exp(score - top)
            denom = jnp.sum(weights, axis=0, keepdims=True)
            probs.append((weights * (1.0 / denom)).astype(BF16))
            lse_ref[0, pair, block : block + 1, :] = top + jnp.log(denom)
        mixed = []
        for (lane, pair, lanes, block), prob in zip(jobs, probs):
            mixed.append(tn(keys_of(v_ref, pv_ref.at[lane], block, lanes), prob))
        for (lane, pair, lanes, block), value in zip(jobs, mixed):
            out_ref[0, rows_of(block), lanes] = pair_join(value).astype(BF16)
        return carry

    lax.fori_loop(0, q_ref.shape[2] // (LANES * GROUP), body, 0)


def attn_bwd_kernel(
    q_ref,
    k_ref,
    v_ref,
    w_ref,
    same_ref,
    bias_ref,
    lse_ref,
    do_ref,
    dq_ref,
    dk_ref,
    dv_ref,
    dw_ref,
    k_wide,
    v_wide,
    pk_ref,
    pv_ref,
    dpk_ref,
    dpv_ref,
):
    slots = pk_ref.shape[1]
    scale = jnp.asarray(HEAD_DIM**-0.5, BF16)
    blocks = q_ref.shape[1] // QB

    def body(step, carry):
        jobs = []
        for lane in range(GROUP_BACK):
            pair = step * GROUP_BACK + lane
            lanes = pl.ds(pl.multiple_of(pair * LANES, LANES), LANES)
            k_wide[lane] = k_ref[0, :, lanes].astype(F32)
            v_wide[lane] = v_ref[0, :, lanes].astype(F32)
            pk_ref[lane] = pool(slot_taps(k_wide.at[lane], slots), same_ref, w_ref, 0, lanes)
            pv_ref[lane] = pool(slot_taps(v_wide.at[lane], slots), same_ref, w_ref, 5, lanes)
            jobs += [(lane, pair, lanes, block) for block in range(blocks)]
        dpk_ref[...] = jnp.zeros_like(dpk_ref)
        dpv_ref[...] = jnp.zeros_like(dpv_ref)
        scores, d_probs = [], []
        for lane, pair, lanes, block in jobs:
            keys = keys_of(k_ref, pk_ref.at[lane], block, lanes)
            stacked = pair_stack(q_ref[0, rows_of(block), lanes] * scale)
            scores.append(scores_of(keys, stacked, bias_ref[0, block]))
            values = keys_of(v_ref, pv_ref.at[lane], block, lanes)
            d_probs.append(nt(values, pair_stack(do_ref[0, rows_of(block), lanes])))
        probs, d_scores = [], []
        for (lane, pair, lanes, block), score, d_prob in zip(jobs, scores, d_probs):
            prob = jnp.exp(score - lse_ref[0, pair, block : block + 1, :])
            row_dot = jnp.sum(prob * d_prob, axis=0, keepdims=True)
            d_scores.append((prob * (d_prob - row_dot)).astype(BF16))
            probs.append(prob.astype(BF16))
        parts = []
        for (lane, pair, lanes, block), prob, d_score in zip(jobs, probs, d_scores):
            d_values = nn(prob, pair_stack(do_ref[0, rows_of(block), lanes]))
            d_keys = nn(d_score, pair_stack(q_ref[0, rows_of(block), lanes] * scale))
            far = slice(block * QB // 4, block * QB // 4 + FAR)
            dpk_ref[lane, far, :] += d_keys[NEAR:]
            dpv_ref[lane, far, :] += d_values[NEAR:]
            parts.append((d_keys[:NEAR], d_values[:NEAR]))
        d_queries = []
        for (lane, pair, lanes, block), d_score in zip(jobs, d_scores):
            d_queries.append(tn(keys_of(k_ref, pk_ref.at[lane], block, lanes), d_score))
        for (lane, pair, lanes, block), value in zip(jobs, d_queries):
            dq_ref[0, rows_of(block), lanes] = (pair_join(value) * HEAD_DIM**-0.5).astype(BF16)
        for lane in range(GROUP_BACK):
            lanes = jobs[lane * blocks][2]
            for side, (wide_ref, d_pool_ref, out_ref) in enumerate(
                ((k_wide, dpk_ref, dk_ref), (v_wide, dpv_ref, dv_ref))
            ):
                wide = wide_ref.at[lane]
                d_pool = d_pool_ref[lane]
                taps = slot_taps(wide, slots)
                masked = [d_pool * same_ref[0, tap] for tap in range(5)]
                places = [5 * side + tap for tap in range(5)]
                for tap, row in enumerate(places):
                    dw_ref[0, row : row + 1, lanes] = jnp.sum(
                        masked[tap] * taps[tap], axis=0, keepdims=True
                    )
                spread = [
                    masked[tap] * w_ref[row : row + 1, lanes] for tap, row in enumerate(places)
                ]
                wide[4 * slots :, :] = jnp.zeros((wide.shape[0] - 4 * slots, LANES), F32)
                for tap in range(4):
                    wide[pl.ds(tap, slots, stride=4), :] = spread[tap]
                wide[pl.ds(4, slots, stride=4), :] += spread[4]
                for block in range(blocks):
                    near = HALO - WIN // 2 + block * QB
                    wide[near : near + NEAR, :] += parts[lane * blocks + block][side]
                out_ref[0, :, lanes] = wide[...].astype(BF16)
        return carry

    lax.fori_loop(0, q_ref.shape[2] // (LANES * GROUP_BACK), body, 0)
    dw_ref[0, 10:, :] = jnp.zeros((dw_ref.shape[1] - 10, dw_ref.shape[2]), F32)


def by_seq(*shape, first=0):
    return pl.BlockSpec((1,) + shape, lambda s: (s + first,) + (0,) * len(shape))


def attention_specs(ext, group, slots, width, first=0):
    return [
        by_seq(group, width, first=first),
        by_seq(ext, width, first=first),
        by_seq(ext, width, first=first),
        pl.BlockSpec((16, width), lambda s: (0, 0)),
        by_seq(5, slots, LANES, first=first),
        by_seq(group // QB, KEYS, LANES, first=first),
    ]


def attention_forward(queries, keys, values, taps, same, bias):
    seqs, group, width = queries.shape
    ext = keys.shape[1]
    slots = same.shape[2]
    pairs = width // LANES
    blocks = group // QB
    wide = pltpu.VMEM((GROUP, ext, LANES), F32)
    pooled = pltpu.VMEM((GROUP, slots, LANES), BF16)
    return pl.pallas_call(
        attn_fwd_kernel,
        grid=(seqs,),
        in_specs=attention_specs(ext, group, slots, width),
        out_specs=[by_seq(group, width), by_seq(pairs, blocks, 2 * QB)],
        out_shape=[
            jax.ShapeDtypeStruct((seqs, group, width), BF16),
            jax.ShapeDtypeStruct((seqs, pairs, blocks, 2 * QB), F32),
        ],
        scratch_shapes=[wide, wide, pooled, pooled],
        compiler_params=pltpu.CompilerParams(vmem_limit_bytes=60 << 20),
        cost_estimate=QUICK,
        name="attn_fwd",
    )(queries, keys, values, taps, same, bias)


def attention_backward(queries, keys, values, taps, same, bias, lse, d_mixed, first, count, earlier):
    seqs, group, width = queries.shape
    ext = keys.shape[1]
    slots = same.shape[2]
    pairs = width // LANES
    blocks = group // QB
    wide = pltpu.VMEM((GROUP_BACK, ext, LANES), F32)
    pooled = pltpu.VMEM((GROUP_BACK, slots, LANES), BF16)
    d_pooled = pltpu.VMEM((GROUP_BACK, slots, LANES), F32)
    args = (queries, keys, values, taps, same, bias, lse, d_mixed)

    def kernel(*refs):
        attn_bwd_kernel(*refs[: len(args)], *refs[len(args) + len(earlier) :])

    return pl.pallas_call(
        kernel,
        grid=(count,),
        in_specs=attention_specs(ext, group, slots, width, first)
        + [by_seq(pairs, blocks, 2 * QB, first=first), by_seq(group, width, first=first)]
        + [pl.BlockSpec(memory_space=pl.ANY)] * len(earlier),
        out_specs=[
            by_seq(*shape, first=first)
            for shape in ((group, width), (ext, width), (ext, width), (16, width))
        ],
        out_shape=[
            jax.ShapeDtypeStruct((seqs, group, width), BF16),
            jax.ShapeDtypeStruct((seqs, ext, width), BF16),
            jax.ShapeDtypeStruct((seqs, ext, width), BF16),
            jax.ShapeDtypeStruct((seqs, 16, width), F32),
        ],
        input_output_aliases={len(args) + i: i for i in range(len(earlier))},
        scratch_shapes=[wide, wide, pooled, pooled, d_pooled, d_pooled],
        compiler_params=pltpu.CompilerParams(vmem_limit_bytes=60 << 20),
        cost_estimate=QUICK,
        name="attn_bwd",
    )(*args, *earlier)


ROWS = 1024
HALF_PI = 0.3989422804014327


def row_sum(value):
    return jnp.sum(value, axis=0, keepdims=True)


def row_mean(value):
    return jnp.mean(value, axis=1, keepdims=True)


def normalize(value):
    centered = value - row_mean(value)
    inv = lax.rsqrt(row_mean(centered * centered) + EPS)
    return centered * inv, inv


def normalize_back(grad, normed, inv):
    return inv * (grad - row_mean(grad) - normed * row_mean(grad * normed))


def ffn_kernel(
    panels,
    x_ref,
    mixed_ref,
    cot_ref,
    wo_ref,
    small_ref,
    bias_ref,
    w_in_ref,
    w_out_ref,
    y_ref,
    d_first_ref,
    d_mixed_ref,
    d_small_ref,
    d_bias_ref,
    d_weights_ref,
    n_one,
    inv_one,
    low,
    hidden,
    slope,
    d_inner,
    d_in_stage,
    d_out_stage,
    in_sems,
    out_sems,
):
    step = pl.program_id(0)
    tokens, width = x_ref.shape
    chunks = tokens // ROWS
    acc, d_outer = d_first_ref, d_mixed_ref
    units = d_weights_ref.shape[0]
    some = units // panels

    def in_copy(panel, slot):
        return pltpu.make_async_copy(
            d_in_stage.at[slot], d_weights_ref.at[:, panels + panel], in_sems.at[slot]
        )

    def out_copy(panel, slot):
        return pltpu.make_async_copy(
            d_out_stage.at[slot],
            d_weights_ref.at[pl.ds(panel * some, some), pl.ds(0, panels)],
            out_sems.at[slot],
        )

    def square(ref):
        return ref[...].reshape(width, width)

    gain_one, shift_one, outer_bias, gain_two, shift_two = (
        small_ref[i : i + 1, :] for i in range(5)
    )

    @pl.when(step == 0)
    def _():
        def body(i, carry):
            rows = pl.ds(pl.multiple_of(i * ROWS, ROWS), ROWS)
            first = x_ref[rows, :].astype(F32) + nn(mixed_ref[rows, :], square(wo_ref))
            normed, inv = normalize(first)
            n_one[rows, :] = normed
            inv_one[rows, :] = jnp.broadcast_to(inv, (ROWS, LANES))
            out = normed * gain_one + shift_one
            low[rows, :] = out.astype(BF16)
            acc[rows, :] = out + outer_bias
            return carry

        lax.fori_loop(0, chunks, body, 0)

    @pl.when(step < panels)
    def _():
        def body(i, carry):
            rows = pl.ds(pl.multiple_of(i * ROWS, ROWS), ROWS)
            inner = nn(low[rows, :], square(w_in_ref)) + bias_ref[0]
            cdf = 0.5 * (1.0 + lax.erf(inner * 0.7071067811865476))
            pdf = HALF_PI * jnp.exp(-0.5 * inner * inner)
            out = (inner * cdf).astype(BF16)
            hidden[step, rows, :] = out
            slope[step, rows, :] = cdf + inner * pdf
            acc[rows, :] += nn(out, square(w_out_ref))
            return carry

        lax.fori_loop(0, chunks, body, 0)

    @pl.when(step == panels)
    def _():
        def body(i, carry):
            d_gain, d_shift, d_bias = carry
            rows = pl.ds(pl.multiple_of(i * ROWS, ROWS), ROWS)
            normed, inv = normalize(acc[rows, :])
            y_ref[rows, :] = (normed * gain_two + shift_two).astype(BF16)
            grad = cot_ref[rows, :].astype(F32)
            d_second = normalize_back(grad * gain_two, normed, inv)
            low_grad = d_second.astype(BF16)
            acc[rows, :] = d_second
            d_outer[rows, :] = low_grad
            return (
                d_gain + row_sum(grad * normed),
                d_shift + row_sum(grad),
                d_bias + row_sum(low_grad.astype(F32)),
            )

        zero = jnp.zeros((1, width), F32)
        d_gain, d_shift, d_bias = lax.fori_loop(0, chunks, body, (zero, zero, zero))
        d_small_ref[2:3, :] = d_bias
        d_small_ref[3:4, :] = d_gain
        d_small_ref[4:5, :] = d_shift
        d_small_ref[5:, :] = jnp.zeros((3, width), F32)

    @pl.when(step >= panels)
    def _():
        panel = step - panels

        def body(i, d_bias):
            rows = pl.ds(pl.multiple_of(i * ROWS, ROWS), ROWS)
            d_hidden = nt(d_outer[rows, :], square(w_out_ref))
            grad = (d_hidden * slope[panel, rows, :]).astype(BF16)
            d_inner[rows, :] = grad
            acc[rows, :] += nt(grad, square(w_in_ref))
            return d_bias + row_sum(grad.astype(F32))

        d_bias_ref[0] = lax.fori_loop(0, chunks, body, jnp.zeros(d_bias_ref.shape[1:], F32))
        slot = lax.rem(panel, 2)

        @pl.when(panel >= 2)
        def _():
            in_copy(panel - 2, slot).wait()
            out_copy(panel - 2, slot).wait()

        d_out_stage[slot] = tn(hidden[panel], d_outer[...]).astype(BF16).reshape(d_out_stage.shape[1:])
        out_copy(panel, slot).start()
        d_in_stage[slot] = tn(low[...], d_inner[...]).astype(BF16).reshape(d_in_stage.shape[1:])
        in_copy(panel, slot).start()

    @pl.when(step == 2 * panels - 1)
    def _():
        def body(i, carry):
            d_gain, d_shift = carry
            rows = pl.ds(pl.multiple_of(i * ROWS, ROWS), ROWS)
            grad = acc[rows, :]
            normed = n_one[rows, :]
            d_first = normalize_back(grad * gain_one, normed, inv_one[rows, 0:1])
            d_first_ref[rows, :] = d_first
            low_grad = d_first.astype(BF16)
            d_inner[rows, :] = low_grad
            d_mixed_ref[rows, :] = nt(low_grad, square(wo_ref)).astype(BF16)
            return d_gain + row_sum(grad * normed), d_shift + row_sum(grad)

        zero = jnp.zeros((1, width), F32)
        d_gain, d_shift = lax.fori_loop(0, chunks, body, (zero, zero))
        d_small_ref[0:1, :] = d_gain
        d_small_ref[1:2, :] = d_shift
        slot = panels % 2
        in_copy(panels - 2, slot).wait()
        d_wo = tn(mixed_ref[...], d_inner[...])
        d_in_stage[slot] = d_wo.astype(BF16).reshape(d_in_stage.shape[1:])
        in_copy(panels, slot).start()
        out_copy(panels - 2, slot).wait()
        in_copy(panels - 1, 1 - slot).wait()
        out_copy(panels - 1, 1 - slot).wait()
        in_copy(panels, slot).wait()


def feed_forward(x, mixed, cot, small, bias, weights):
    tokens, width = x.shape
    units, groups, rows_in, _ = weights.shape
    panels = groups // 2
    panel = width

    def whole(*shape):
        return pl.BlockSpec(
            shape, lambda j: (0,) * len(shape), pipeline_mode=pl.Buffered(buffer_count=1)
        )

    def later(j):
        return jnp.maximum(j - panels, 0)

    return pl.pallas_call(
        functools.partial(ffn_kernel, panels),
        grid=(2 * panels,),
        in_specs=[
            whole(tokens, width),
            whole(tokens, width),
            whole(tokens, width),
            pl.BlockSpec(
                (units, 1, rows_in, width),
                lambda j: (0, 2 * panels, 0, 0),
                pipeline_mode=pl.Buffered(buffer_count=1),
            ),
            whole(8, width),
            pl.BlockSpec((1, 1, panel), lambda j: (lax.rem(j, panels), 0, 0)),
            pl.BlockSpec((units, 1, rows_in, width), lambda j: (0, panels + lax.rem(j, panels), 0, 0)),
            pl.BlockSpec(
                (units // panels, panels, rows_in, width), lambda j: (lax.rem(j, panels), 0, 0, 0)
            ),
        ],
        out_specs=[
            whole(tokens, width),
            whole(tokens, width),
            whole(tokens, width),
            whole(8, width),
            pl.BlockSpec((1, 1, panel), lambda j: (later(j), 0, 0)),
            pl.BlockSpec(memory_space=pl.ANY),
        ],
        out_shape=[
            jax.ShapeDtypeStruct((tokens, width), BF16),
            jax.ShapeDtypeStruct((tokens, width), F32),
            jax.ShapeDtypeStruct((tokens, width), BF16),
            jax.ShapeDtypeStruct((8, width), F32),
            jax.ShapeDtypeStruct((panels, 1, panel), F32),
            jax.ShapeDtypeStruct(weights.shape, BF16),
        ],
        scratch_shapes=[
            pltpu.VMEM((tokens, width), F32),
            pltpu.VMEM((tokens, LANES), F32),
            pltpu.VMEM((tokens, width), BF16),
            pltpu.VMEM((panels, tokens, panel), BF16),
            pltpu.VMEM((panels, tokens, panel), F32),
            pltpu.VMEM((tokens, panel), BF16),
            pltpu.VMEM((2, units, rows_in, width), BF16),
            pltpu.VMEM((2, units // panels, panels, rows_in, width), BF16),
            pltpu.SemaphoreType.DMA((2,)),
            pltpu.SemaphoreType.DMA((2,)),
        ],
        compiler_params=pltpu.CompilerParams(vmem_limit_bytes=60 << 20),
        cost_estimate=QUICK,
        name="ffn",
    )(x, mixed, cot, weights, small, bias, weights, weights)


def pack_kernel(outer_ref, inner_ref, out_ref, packed_ref):
    rows, width = outer_ref.shape
    share = out_ref.shape[0]
    packed_ref[:rows, :] = outer_ref[...]
    for panel in range(inner_ref.shape[1] // width):
        at = rows + panel * share
        packed_ref[at : at + share, :] = inner_ref[:, panel * width : (panel + 1) * width]
    packed_ref[packed_ref.shape[0] - share :, :] = out_ref[...]


def pack(outer, inner, out):
    share, width = out.shape
    panels = inner.shape[1] // width
    if share % 8:
        inner = inner.reshape(share, panels, width).swapaxes(0, 1).reshape(-1, width)
        return jnp.concatenate((outer, inner, out), axis=0)
    rows = outer.shape[0] + (panels + 1) * share
    return pl.pallas_call(
        pack_kernel,
        out_shape=jax.ShapeDtypeStruct((rows, width), BF16),
        cost_estimate=QUICK,
        name="pack",
    )(outer, inner, out)


SMALL = 16


def small_block(taps, vectors, bias, width):
    share = taps.shape[1]
    rows = jnp.concatenate([taps.astype(F32)] + [v.astype(F32) for v in vectors], axis=0)
    rows = jnp.concatenate((rows, jnp.zeros((rows.shape[0], width - share), F32)), axis=1)
    bias = bias.astype(F32)
    last = jnp.concatenate((bias, jnp.zeros((1, width - bias.shape[1]), F32)), axis=1)
    return jnp.concatenate((rows, last), axis=0).astype(BF16)


def stack_kernel(q_ref, k_ref, v_ref, taps_ref, a_ref, b_ref, c_ref, d_ref, e_ref, bias_ref, out_ref):
    share, width = q_ref.shape
    for place, ref in enumerate((q_ref, k_ref, v_ref)):
        out_ref[place * share : (place + 1) * share, :] = ref[...]
    vectors = [ref[...] for ref in (a_ref, b_ref, c_ref, d_ref, e_ref)]
    out_ref[3 * share :, :] = small_block(taps_ref[...], vectors, bias_ref[...], width)


def stack(query, key, value, taps, vectors, bias):
    share, width = query.shape
    vectors = [v.reshape(1, -1) for v in vectors]
    bias = bias.reshape(1, -1)
    if share % 8:
        return jnp.concatenate((query, key, value, small_block(taps, vectors, bias, width)), axis=0)
    return pl.pallas_call(
        stack_kernel,
        out_shape=jax.ShapeDtypeStruct((3 * share + SMALL, width), BF16),
        cost_estimate=QUICK,
        name="stack",
    )(query, key, value, taps, *vectors, bias)


def square_of(w_ref, place):
    units, _, width = w_ref.shape
    part = width // units
    return w_ref[:, place * part : (place + 1) * part, :].reshape(width, width)


def project_kernel(
    x_ref, left_ref, right_ref, near_left_ref, far_right_ref, far_ref, w_ref, q_ref, k_ref, v_ref, ext_ref
):
    half = HALO // 2
    group, width = x_ref.shape[1:]
    right = HALO + group
    ext_ref[0, :half, :] = left_ref[0]
    ext_ref[0, half:HALO, :] = near_left_ref[0]
    ext_ref[0, HALO:right, :] = x_ref[0]
    ext_ref[0, right : right + half, :] = right_ref[0]
    ext_ref[0, right + half : right + HALO, :] = far_right_ref[0]
    row = lax.broadcasted_iota(jnp.int32, (PAD, width), 0)
    far = jnp.where(row == 0, jnp.broadcast_to(far_ref[0].astype(F32), (PAD, width)), 0.0)
    ext_ref[0, right + HALO :, :] = far.astype(BF16)
    q_ref[0] = nn(x_ref[0], square_of(w_ref, 0)).astype(BF16)
    k_ref[0] = nn(ext_ref[0], square_of(w_ref, 1)).astype(BF16)
    v_ref[0] = nn(ext_ref[0], square_of(w_ref, 2)).astype(BF16)


def resident(*shape):
    return pl.BlockSpec(
        shape, lambda s: (0,) * len(shape), pipeline_mode=pl.Buffered(buffer_count=1)
    )


def project(x, left, right, near_left, far_right, far, weights):
    seqs, group, width = x.shape
    ext = group + 2 * HALO + PAD
    extended = jax.ShapeDtypeStruct((seqs, ext, width), BF16)
    return pl.pallas_call(
        project_kernel,
        grid=(seqs,),
        in_specs=[
            by_seq(group, width),
            by_seq(HALO // 2, width),
            by_seq(HALO // 2, width),
            by_seq(HALO // 2, width),
            by_seq(HALO // 2, width),
            by_seq(1, width),
            resident(*weights.shape),
        ],
        out_specs=[by_seq(group, width)] + [by_seq(ext, width)] * 3,
        out_shape=[jax.ShapeDtypeStruct(x.shape, BF16), extended, extended, extended],
        compiler_params=pltpu.CompilerParams(vmem_limit_bytes=60 << 20),
        cost_estimate=QUICK,
        name="project",
    )(x, left, right, near_left, far_right, far, weights)


def input_grad_kernel(
    dq_ref, dk_ref, dv_ref, first_ref, w_ref, a_ref, b_ref, c_ref, d_ref, far_ref, own_ref
):
    half = HALO // 2
    right = HALO + dq_ref.shape[1]
    grad = nt(dk_ref[0], square_of(w_ref, 1)) + nt(dv_ref[0], square_of(w_ref, 2))
    for ref, at in ((a_ref, 0), (b_ref, right), (c_ref, half), (d_ref, right + half)):
        ref[0] = grad[at : at + half].astype(BF16)
    far_ref[0] = grad[right + HALO : right + HALO + 1].astype(BF16)
    own_ref[0] = grad[HALO:right] + nt(dq_ref[0], square_of(w_ref, 0)) + first_ref[0]


def input_grads(d_queries, d_keys, d_values, d_first, weights):
    seqs, group, width = d_queries.shape
    ext = d_keys.shape[1]
    halo = jax.ShapeDtypeStruct((seqs, HALO // 2, width), BF16)
    return pl.pallas_call(
        input_grad_kernel,
        grid=(seqs,),
        in_specs=[
            by_seq(group, width),
            by_seq(ext, width),
            by_seq(ext, width),
            by_seq(group, width),
            resident(*weights.shape),
        ],
        out_specs=[by_seq(HALO // 2, width)] * 4 + [by_seq(1, width), by_seq(group, width)],
        out_shape=[
            halo,
            halo,
            halo,
            halo,
            jax.ShapeDtypeStruct((seqs, 1, width), BF16),
            jax.ShapeDtypeStruct((seqs, group, width), F32),
        ],
        compiler_params=pltpu.CompilerParams(vmem_limit_bytes=60 << 20),
        cost_estimate=QUICK,
        name="input_grads",
    )(d_queries, d_keys, d_values, d_first, weights)


def weight_grad_kernel(
    x_ref, dq_ref, dk_ref, dv_ref, small_ref, out_ref, acc, x_tail, dk_tail, dv_tail
):
    seq = pl.program_id(0)
    group, width = dq_ref.shape[1:]
    units = out_ref.shape[0]
    part = width // units
    main = 2 * HALO + group

    @pl.when(seq == 0)
    def _():
        acc[...] = jnp.zeros_like(acc)

    rows = pl.ds(pl.multiple_of(seq * PAD, PAD), PAD)
    for tail, ref in ((x_tail, x_ref), (dk_tail, dk_ref), (dv_tail, dv_ref)):
        tail[rows, :] = ref[0, main:, :]
    acc[0] += tn(x_ref[0, HALO : HALO + group, :], dq_ref[0])
    acc[1] += tn(x_ref[0, :main, :], dk_ref[0, :main, :])
    acc[2] += tn(x_ref[0, :main, :], dv_ref[0, :main, :])

    @pl.when(seq == pl.num_programs(0) - 1)
    def _():
        ends = (None, tn(x_tail[...], dk_tail[...]), tn(x_tail[...], dv_tail[...]))
        for place, end in enumerate(ends):
            total = acc[place] if end is None else acc[place] + end
            out_ref[:, place * part : (place + 1) * part, :] = total.astype(BF16).reshape(
                units, part, width
            )
        out_ref[:, 3 * part :, :] = small_ref[...]


def weight_grads(x_ext, d_queries, d_keys, d_values, small):
    seqs, group, width = d_queries.shape
    ext = x_ext.shape[1]
    units, small_rows, _ = small.shape
    shape = (units, 3 * (width // units) + small_rows, width)
    tail = pltpu.VMEM((seqs * PAD, width), BF16)
    return pl.pallas_call(
        weight_grad_kernel,
        grid=(seqs,),
        in_specs=[
            by_seq(ext, width),
            by_seq(group, width),
            by_seq(ext, width),
            by_seq(ext, width),
            resident(*small.shape),
        ],
        out_specs=resident(*shape),
        out_shape=jax.ShapeDtypeStruct(shape, BF16),
        scratch_shapes=[pltpu.VMEM((3, width, width), F32), tail, tail, tail],
        compiler_params=pltpu.CompilerParams(vmem_limit_bytes=60 << 20),
        cost_estimate=QUICK,
        name="weight_grads",
    )(x_ext, d_queries, d_keys, d_values, small)


def document_of(positions, lengths, seq_len):
    count = lengths.shape[1]
    order = jnp.arange(count)
    ends = jnp.sum(jnp.where(order[None, :] <= order[:, None], lengths[:, None, :], 0), axis=2)
    counted = jnp.sum((positions[None, :, None] >= ends[:, None, :]).astype(jnp.int32), axis=2)
    inside = (positions >= 0) & (positions < seq_len)
    return jnp.where(inside[None, :], counted, -1)


def masks(lengths, offset, group, seq_len):
    ext = group + 2 * HALO
    slots = ext // 4
    positions = offset - HALO + jnp.arange(ext + PAD, dtype=jnp.int32)
    doc = document_of(positions, lengths, seq_len)
    slot_doc = doc[:, 2:ext:4]
    biases = []
    for block in range(group // QB):
        near = HALO - WIN // 2 + block * QB
        far = block * QB // 4
        key_place = jnp.concatenate((jnp.arange(near, near + NEAR), 4 * jnp.arange(far, far + FAR) + 2))
        reach = jnp.concatenate((jnp.full((NEAR,), WIN // 2), jnp.full((FAR,), PWIN // 2)))
        key_doc = jnp.concatenate((doc[:, near : near + NEAR], slot_doc[:, far : far + FAR]), axis=1)
        query_place = HALO + block * QB + jnp.arange(QB)
        query_doc = doc[:, HALO + block * QB : HALO + (block + 1) * QB]
        allowed = (jnp.abs(key_place[:, None] - query_place[None, :]) <= reach[:, None])[None] & (
            key_doc[:, :, None] == query_doc[:, None, :]
        )
        biases.append(jnp.where(allowed, 0.0, MASKED).astype(F32))
    same = jnp.stack(
        [(doc[:, tap : tap + ext : 4] == slot_doc).astype(F32) for tap in range(5)], axis=1
    )
    same = jnp.broadcast_to(same[..., None], same.shape + (LANES,))
    return jnp.stack(biases, axis=1), same, slots


def steps(count):
    for k in range(1, count):
        if count & (count - 1) == 0:
            yield [(i, i ^ k) for i in range(count)], lambda me, k=k: (me ^ k, me ^ k)
        else:
            yield (
                [(i, (i + k) % count) for i in range(count)],
                lambda me, k=k: (lax.rem(me + k, count), lax.rem(me - k + count, count)),
            )


def pick(value, index, dim=0):
    return lax.dynamic_index_in_dim(value, index, dim, keepdims=False)


def gather_seq(block, *earlier):
    count, me = lax.axis_size("seq"), lax.axis_index("seq")
    zeros = (0,) * block.ndim
    came_all = after(tuple(lax.ppermute(block, "seq", pairs) for pairs, _ in steps(count)), *earlier)
    column = jnp.zeros((count,) + block.shape, block.dtype)
    column = lax.dynamic_update_slice(column, block[None], (me,) + zeros)
    for came, (_, met) in zip(came_all, steps(count)):
        column = lax.dynamic_update_slice(column, came[None], (met(me)[1],) + zeros)
    return column


def gather_yx(column):
    me = lax.axis_index("yx")
    pieces = [(column, me)]
    for pairs, met in steps(lax.axis_size("yx")):
        pieces.append((lax.ppermute(column, "yx", pairs), met(me)[1]))
    return pieces


def gather_core(pieces):
    count, me = lax.axis_size("core"), lax.axis_index("core")
    shape = pieces[0][0].shape
    zeros = (0,) * len(shape)
    whole = jnp.zeros((len(pieces), count) + shape, pieces[0][0].dtype)
    for piece, place in pieces:
        whole = lax.dynamic_update_slice(whole, piece[None, None], (place, me) + zeros)
        for pairs, met in steps(count):
            other = lax.ppermute(piece, "core", pairs)
            whole = lax.dynamic_update_slice(whole, other[None, None], (place, met(me)[1]) + zeros)
    return whole.reshape((-1,) + shape)


def after(value, *earlier):
    return lax.optimization_barrier((value, earlier))[0] if earlier else lax.optimization_barrier(value)


def exchange_sum(pieces, axis):
    me = lax.axis_index(axis)
    total = pick(pieces, me).astype(F32)
    for pairs, met in steps(lax.axis_size(axis)):
        total = total + lax.ppermute(pick(pieces, met(me)[0]), axis, pairs).astype(F32)
    return total


def local(
    tokens,
    doc_lengths,
    query_weight,
    key_weight,
    value_weight,
    out_weight,
    pool_weight,
    first_gain,
    first_shift,
    inner_weight,
    inner_bias,
    outer_weight,
    outer_bias,
    second_gain,
    second_shift,
    cotangent,
):
    seq_count = lax.axis_size("seq")
    yx_count = lax.axis_size("yx")
    core_count = lax.axis_size("core")
    units = yx_count * core_count
    parts = units * seq_count
    seq_place = lax.axis_index("seq")
    seqs, group, width = tokens.shape
    ff = inner_weight.shape[1]
    panels = ff // width
    share = query_weight.shape[0]
    count = seqs * group

    def shift(value, by):
        pairs = [(i, i + by) for i in range(seq_count) if 0 <= i + by < seq_count]
        return lax.ppermute(value, "seq", pairs)

    early = stack(
        query_weight,
        key_weight,
        value_weight,
        pool_weight,
        (first_gain, first_shift, outer_bias, second_gain, second_shift),
        inner_bias,
    )
    late = pack(outer_weight, inner_weight, out_weight)
    early_column = gather_seq(early)
    sent = after(tokens, early_column)
    half = HALO // 2
    came = (
        shift(sent[:, group - HALO : group - half], 1),
        shift(sent[:, :half], -1),
    )
    later_came = (
        shift(sent[:, group - half :], 1),
        shift(sent[:, half:HALO], -1),
        shift(sent[:, :1], -2),
    )
    early_column = jnp.concatenate(
        [early_column[:, i * share : (i + 1) * share].reshape(-1, width) for i in range(3)]
        + [early_column[:, 3 * share :].reshape(-1, width)],
        axis=0,
    )
    early_pieces = gather_yx(early_column)
    early = gather_core(early_pieces)
    late_column = lax.all_gather(late, "seq", axis=0)
    late_column, came = after((late_column, came), [piece for piece, _ in early_pieces[1:]])
    outer_rows = panels * share
    late_column = jnp.concatenate(
        (
            late_column[:, :outer_rows].reshape(-1, width),
            late_column[:, outer_rows:]
            .reshape(seq_count, panels + 1, share, width)
            .swapaxes(0, 1)
            .reshape(-1, width),
        ),
        axis=0,
    )
    late = lax.all_gather(late_column, ("yx", "core"), axis=0)
    late = late.reshape(units, 2 * panels + 1, seq_count * share, width)
    small = early[:, 3 * seq_count * share :].reshape(parts, SMALL, width)
    vectors = small[:, : SMALL - 1, :share].transpose(1, 0, 2).reshape(SMALL - 1, width).astype(F32)
    taps = jnp.pad(vectors[:10], ((0, 6), (0, 0)))
    small_rows_f32 = jnp.pad(vectors[10:], ((0, 3), (0, 0)))
    bias_inner = small[:, SMALL - 1, : ff // parts].reshape(panels, 1, width).astype(F32)

    flat = tokens.reshape(count, width)
    bias, same, slots = masks(doc_lengths, seq_place * group, group, group * seq_count)

    queries, keys, values, x_ext = project(tokens, *came, *later_came, early)
    mixed, lse = attention_forward(queries, keys, values, taps, same, bias)
    y, d_first, d_mixed, d_small, d_bias, d_late = feed_forward(
        flat,
        mixed.reshape(count, width),
        cotangent.reshape(count, width),
        small_rows_f32,
        bias_inner,
        late,
    )
    late_sum = lax.psum_scatter(
        d_late.reshape(-1, width), ("yx", "core"), scatter_dimension=0, tiled=True
    )
    d_queries, d_keys, d_values, d_taps = attention_backward(
        queries,
        keys,
        values,
        taps,
        same,
        bias,
        lse,
        d_mixed.reshape(seqs, group, width),
        0,
        seqs,
        (),
    )
    left_a, right_a, left_b, right_b, far, own = input_grads(
        d_queries, d_keys, d_values, d_first.reshape(seqs, group, width), early
    )
    came = (shift(left_a, -1), shift(right_a, 1))
    later_came = (shift(left_b, -1), shift(right_b, 1), shift(far, 2))

    d_taps = jnp.sum(d_taps, axis=0)[:10]
    d_vectors = jnp.concatenate((d_taps, d_small[:5]), axis=0)
    d_vectors = d_vectors.reshape(SMALL - 1, parts, share).transpose(1, 0, 2)
    d_vectors = jnp.pad(d_vectors, ((0, 0), (0, 0), (0, width - share)))
    d_bias = jnp.pad(d_bias.reshape(parts, 1, -1), ((0, 0), (0, 0), (0, width - ff // parts)))
    d_vectors = jnp.concatenate((d_vectors, d_bias), axis=1).astype(BF16)
    d_vectors = d_vectors.reshape(units, seq_count * SMALL, width)
    early_sum = weight_grads(after(x_ext, own), d_queries, d_keys, d_values, d_vectors)
    early_sum = early_sum.reshape(yx_count, core_count, -1, width)
    early_sum = exchange_sum(early_sum.swapaxes(0, 1), "core").astype(BF16)
    early_sum, came = after((early_sum, came))
    early_sum = exchange_sum(early_sum, "yx").astype(BF16)
    early_sum, later_came, late_sum = after((early_sum, later_came, late_sum))
    outer_all = seq_count * outer_rows
    late_sum = jnp.concatenate(
        (
            late_sum[:outer_all].reshape(seq_count, outer_rows, width),
            late_sum[outer_all:]
            .reshape(panels + 1, seq_count, share, width)
            .swapaxes(0, 1)
            .reshape(seq_count, (panels + 1) * share, width),
        ),
        axis=1,
    )
    late_sum = exchange_sum(late_sum, "seq")
    whole = 3 * seq_count * share
    early_sum = jnp.concatenate(
        [
            early_sum[:whole]
            .reshape(3, seq_count, share, width)
            .swapaxes(0, 1)
            .reshape(seq_count, 3 * share, width),
            early_sum[whole:].reshape(seq_count, SMALL, width),
        ],
        axis=1,
    )
    early_sum = exchange_sum(early_sum, "seq")

    edge = group - HALO
    from_left = jnp.concatenate((came[1], later_came[1]), axis=1).astype(F32)
    from_right = jnp.concatenate((came[0], later_came[0]), axis=1).astype(F32)
    d_input = own + jnp.pad(from_right, ((0, 0), (edge, 0), (0, 0)))
    d_input = d_input + jnp.pad(from_left, ((0, 0), (0, edge), (0, 0)))
    d_input = d_input + jnp.pad(later_came[2].astype(F32), ((0, 0), (0, group - 1), (0, 0)))

    vector_sum = early_sum[3 * share :]
    pieces = [vector_sum[10 + i, :share] for i in range(5)]
    return (
        y.reshape(seqs, group, width),
        d_input.astype(BF16),
        early_sum[:share],
        early_sum[share : 2 * share],
        early_sum[2 * share : 3 * share],
        late_sum[2 * outer_rows :],
        vector_sum[:10, :share],
        pieces[0],
        pieces[1],
        late_sum[outer_rows : 2 * outer_rows]
        .reshape(panels, share, width)
        .transpose(1, 0, 2)
        .reshape(share, ff),
        vector_sum[SMALL - 1, : ff // parts],
        late_sum[:outer_rows],
        pieces[2],
        pieces[3],
        pieces[4],
    )


def solution(mesh):
    dp, seq = mesh.devices.shape
    cores = 2 if dp % 2 == 0 else 1
    mesh = Mesh(mesh.devices.reshape(dp // cores, cores, seq), ("yx", "core", "seq"))
    every = ("yx", "core", "seq")
    rows = P(every, None)
    vector = P(every)
    whole = P(("yx", "core"), "seq", None)
    taps = P(None, every)
    weights = (rows, rows, rows, rows, taps, vector, vector, rows, vector, rows, vector, vector, vector)
    return jax.shard_map(
        local,
        mesh=mesh,
        in_specs=(whole, P(("yx", "core"), None)) + weights + (whole,),
        out_specs=(whole, whole) + weights,
        check_vma=False,
    )
```

```python
import functools

import jax
import jax.numpy as jnp
from jax import lax
from jax.experimental import pallas as pl
from jax.experimental.pallas import tpu as pltpu
from jax.sharding import Mesh
from jax.sharding import PartitionSpec as P

HEADS = 12
HEAD_DIM = 64
WIN = 128
PWIN = 512
EPS = 1e-05

LANES = 128
QB = 128
GROUP = 6
GROUP_BACK = 2
HALO = PWIN // 2
PAD = 16
NEAR = QB + WIN
FAR = (QB + PWIN) // 4
KEYS = NEAR + FAR
MASKED = -1e30
QUICK = pl.CostEstimate(flops=1 << 20, bytes_accessed=1 << 20, transcendentals=0)

F32 = jnp.float32
BF16 = jnp.bfloat16


def nt(left, right):
    return lax.dot_general(left, right, (((1,), (1,)), ((), ())), preferred_element_type=F32)


def tn(left, right):
    return lax.dot_general(left, right, (((0,), (0,)), ((), ())), preferred_element_type=F32)


def nn(left, right):
    return lax.dot_general(left, right, (((1,), (0,)), ((), ())), preferred_element_type=F32)


def slot_taps(wide, slots):
    return [wide[pl.ds(tap, slots, stride=4), :] for tap in range(5)]


def pool(taps, same_ref, w_ref, first, lanes):
    total = None
    for tap in range(5):
        term = taps[tap] * same_ref[0, tap] * w_ref[first + tap : first + tap + 1, lanes]
        total = term if total is None else total + term
    return total.astype(BF16)


def pair_stack(rows):
    lane = lax.broadcasted_iota(jnp.int32, rows.shape, 1)
    zero = jnp.zeros_like(rows)
    return jnp.concatenate(
        (jnp.where(lane < HEAD_DIM, rows, zero), jnp.where(lane < HEAD_DIM, zero, rows)), axis=0
    )


def pair_join(both):
    joined = jnp.concatenate((both[:HEAD_DIM, :QB], both[HEAD_DIM:, QB:]), axis=0)
    return joined.T


def rows_of(block):
    return slice(block * QB, (block + 1) * QB)


def keys_of(ref, pooled, block, lanes):
    near = HALO - WIN // 2 + block * QB
    far = block * QB // 4
    return jnp.concatenate((ref[0, near : near + NEAR, lanes], pooled[far : far + FAR, :]), axis=0)


def scores_of(keys, stacked, bias):
    return nt(keys, stacked) + jnp.concatenate((bias, bias), axis=1)


def attn_fwd_kernel(
    q_ref, k_ref, v_ref, w_ref, same_ref, bias_ref, out_ref, lse_ref, k_wide, v_wide, pk_ref, pv_ref
):
    slots = pk_ref.shape[1]
    scale = jnp.asarray(HEAD_DIM**-0.5, BF16)

    blocks = q_ref.shape[1] // QB

    def body(step, carry):
        jobs = []
        for lane in range(GROUP):
            pair = step * GROUP + lane
            lanes = pl.ds(pl.multiple_of(pair * LANES, LANES), LANES)
            k_wide[lane] = k_ref[0, :, lanes].astype(F32)
            v_wide[lane] = v_ref[0, :, lanes].astype(F32)
            pk_ref[lane] = pool(slot_taps(k_wide.at[lane], slots), same_ref, w_ref, 0, lanes)
            pv_ref[lane] = pool(slot_taps(v_wide.at[lane], slots), same_ref, w_ref, 5, lanes)
            jobs += [(lane, pair, lanes, block) for block in range(blocks)]
        scores = []
        for lane, pair, lanes, block in jobs:
            stacked = pair_stack(q_ref[0, rows_of(block), lanes] * scale)
            keys = keys_of(k_ref, pk_ref.at[lane], block, lanes)
            scores.append(scores_of(keys, stacked, bias_ref[0, block]))
        probs = []
        for (lane, pair, lanes, block), score in zip(jobs, scores):
            top = jnp.max(score, axis=0, keepdims=True)
            weights = jnp.exp(score - top)
            denom = jnp.sum(weights, axis=0, keepdims=True)
            probs.append((weights * (1.0 / denom)).astype(BF16))
            lse_ref[0, pair, block : block + 1, :] = top + jnp.log(denom)
        mixed = []
        for (lane, pair, lanes, block), prob in zip(jobs, probs):
            mixed.append(tn(keys_of(v_ref, pv_ref.at[lane], block, lanes), prob))
        for (lane, pair, lanes, block), value in zip(jobs, mixed):
            out_ref[0, rows_of(block), lanes] = pair_join(value).astype(BF16)
        return carry

    lax.fori_loop(0, q_ref.shape[2] // (LANES * GROUP), body, 0)


def attn_bwd_kernel(
    q_ref,
    k_ref,
    v_ref,
    w_ref,
    same_ref,
    bias_ref,
    lse_ref,
    do_ref,
    dq_ref,
    dk_ref,
    dv_ref,
    dw_ref,
    k_wide,
    v_wide,
    pk_ref,
    pv_ref,
    dpk_ref,
    dpv_ref,
):
    slots = pk_ref.shape[1]
    scale = jnp.asarray(HEAD_DIM**-0.5, BF16)
    blocks = q_ref.shape[1] // QB

    def body(step, carry):
        jobs = []
        for lane in range(GROUP_BACK):
            pair = step * GROUP_BACK + lane
            lanes = pl.ds(pl.multiple_of(pair * LANES, LANES), LANES)
            k_wide[lane] = k_ref[0, :, lanes].astype(F32)
            v_wide[lane] = v_ref[0, :, lanes].astype(F32)
            pk_ref[lane] = pool(slot_taps(k_wide.at[lane], slots), same_ref, w_ref, 0, lanes)
            pv_ref[lane] = pool(slot_taps(v_wide.at[lane], slots), same_ref, w_ref, 5, lanes)
            jobs += [(lane, pair, lanes, block) for block in range(blocks)]
        dpk_ref[...] = jnp.zeros_like(dpk_ref)
        dpv_ref[...] = jnp.zeros_like(dpv_ref)
        scores, d_probs = [], []
        for lane, pair, lanes, block in jobs:
            keys = keys_of(k_ref, pk_ref.at[lane], block, lanes)
            stacked = pair_stack(q_ref[0, rows_of(block), lanes] * scale)
            scores.append(scores_of(keys, stacked, bias_ref[0, block]))
            values = keys_of(v_ref, pv_ref.at[lane], block, lanes)
            d_probs.append(nt(values, pair_stack(do_ref[0, rows_of(block), lanes])))
        probs, d_scores = [], []
        for (lane, pair, lanes, block), score, d_prob in zip(jobs, scores, d_probs):
            prob = jnp.exp(score - lse_ref[0, pair, block : block + 1, :])
            row_dot = jnp.sum(prob * d_prob, axis=0, keepdims=True)
            d_scores.append((prob * (d_prob - row_dot)).astype(BF16))
            probs.append(prob.astype(BF16))
        parts = []
        for (lane, pair, lanes, block), prob, d_score in zip(jobs, probs, d_scores):
            d_values = nn(prob, pair_stack(do_ref[0, rows_of(block), lanes]))
            d_keys = nn(d_score, pair_stack(q_ref[0, rows_of(block), lanes] * scale))
            far = slice(block * QB // 4, block * QB // 4 + FAR)
            dpk_ref[lane, far, :] += d_keys[NEAR:]
            dpv_ref[lane, far, :] += d_values[NEAR:]
            parts.append((d_keys[:NEAR], d_values[:NEAR]))
        d_queries = []
        for (lane, pair, lanes, block), d_score in zip(jobs, d_scores):
            d_queries.append(tn(keys_of(k_ref, pk_ref.at[lane], block, lanes), d_score))
        for (lane, pair, lanes, block), value in zip(jobs, d_queries):
            dq_ref[0, rows_of(block), lanes] = (pair_join(value) * HEAD_DIM**-0.5).astype(BF16)
        for lane in range(GROUP_BACK):
            lanes = jobs[lane * blocks][2]
            for side, (wide_ref, d_pool_ref, out_ref) in enumerate(
                ((k_wide, dpk_ref, dk_ref), (v_wide, dpv_ref, dv_ref))
            ):
                wide = wide_ref.at[lane]
                d_pool = d_pool_ref[lane]
                taps = slot_taps(wide, slots)
                masked = [d_pool * same_ref[0, tap] for tap in range(5)]
                places = [5 * side + tap for tap in range(5)]
                for tap, row in enumerate(places):
                    dw_ref[0, row : row + 1, lanes] = jnp.sum(
                        masked[tap] * taps[tap], axis=0, keepdims=True
                    )
                spread = [
                    masked[tap] * w_ref[row : row + 1, lanes] for tap, row in enumerate(places)
                ]
                wide[4 * slots :, :] = jnp.zeros((wide.shape[0] - 4 * slots, LANES), F32)
                for tap in range(4):
                    wide[pl.ds(tap, slots, stride=4), :] = spread[tap]
                wide[pl.ds(4, slots, stride=4), :] += spread[4]
                for block in range(blocks):
                    near = HALO - WIN // 2 + block * QB
                    wide[near : near + NEAR, :] += parts[lane * blocks + block][side]
                out_ref[0, :, lanes] = wide[...].astype(BF16)
        return carry

    lax.fori_loop(0, q_ref.shape[2] // (LANES * GROUP_BACK), body, 0)
    dw_ref[0, 10:, :] = jnp.zeros((dw_ref.shape[1] - 10, dw_ref.shape[2]), F32)


def by_seq(*shape, first=0):
    return pl.BlockSpec((1,) + shape, lambda s: (s + first,) + (0,) * len(shape))


def attention_specs(ext, group, slots, width, first=0):
    return [
        by_seq(group, width, first=first),
        by_seq(ext, width, first=first),
        by_seq(ext, width, first=first),
        pl.BlockSpec((16, width), lambda s: (0, 0)),
        by_seq(5, slots, LANES, first=first),
        by_seq(group // QB, KEYS, LANES, first=first),
    ]


def attention_forward(queries, keys, values, taps, same, bias):
    seqs, group, width = queries.shape
    ext = keys.shape[1]
    slots = same.shape[2]
    pairs = width // LANES
    blocks = group // QB
    wide = pltpu.VMEM((GROUP, ext, LANES), F32)
    pooled = pltpu.VMEM((GROUP, slots, LANES), BF16)
    return pl.pallas_call(
        attn_fwd_kernel,
        grid=(seqs,),
        in_specs=attention_specs(ext, group, slots, width),
        out_specs=[by_seq(group, width), by_seq(pairs, blocks, 2 * QB)],
        out_shape=[
            jax.ShapeDtypeStruct((seqs, group, width), BF16),
            jax.ShapeDtypeStruct((seqs, pairs, blocks, 2 * QB), F32),
        ],
        scratch_shapes=[wide, wide, pooled, pooled],
        compiler_params=pltpu.CompilerParams(vmem_limit_bytes=60 << 20),
        cost_estimate=QUICK,
        name="attn_fwd",
    )(queries, keys, values, taps, same, bias)


def attention_backward(queries, keys, values, taps, same, bias, lse, d_mixed, first, count, earlier):
    seqs, group, width = queries.shape
    ext = keys.shape[1]
    slots = same.shape[2]
    pairs = width // LANES
    blocks = group // QB
    wide = pltpu.VMEM((GROUP_BACK, ext, LANES), F32)
    pooled = pltpu.VMEM((GROUP_BACK, slots, LANES), BF16)
    d_pooled = pltpu.VMEM((GROUP_BACK, slots, LANES), F32)
    args = (queries, keys, values, taps, same, bias, lse, d_mixed)

    def kernel(*refs):
        attn_bwd_kernel(*refs[: len(args)], *refs[len(args) + len(earlier) :])

    return pl.pallas_call(
        kernel,
        grid=(count,),
        in_specs=attention_specs(ext, group, slots, width, first)
        + [by_seq(pairs, blocks, 2 * QB, first=first), by_seq(group, width, first=first)]
        + [pl.BlockSpec(memory_space=pl.ANY)] * len(earlier),
        out_specs=[
            by_seq(*shape, first=first)
            for shape in ((group, width), (ext, width), (ext, width), (16, width))
        ],
        out_shape=[
            jax.ShapeDtypeStruct((seqs, group, width), BF16),
            jax.ShapeDtypeStruct((seqs, ext, width), BF16),
            jax.ShapeDtypeStruct((seqs, ext, width), BF16),
            jax.ShapeDtypeStruct((seqs, 16, width), F32),
        ],
        input_output_aliases={len(args) + i: i for i in range(len(earlier))},
        scratch_shapes=[wide, wide, pooled, pooled, d_pooled, d_pooled],
        compiler_params=pltpu.CompilerParams(vmem_limit_bytes=60 << 20),
        cost_estimate=QUICK,
        name="attn_bwd",
    )(*args, *earlier)


ROWS = 512
HALF_PI = 0.3989422804014327


def row_sum(value):
    return jnp.sum(value, axis=0, keepdims=True)


def row_mean(value):
    return jnp.mean(value, axis=1, keepdims=True)


def normalize(value):
    centered = value - row_mean(value)
    inv = lax.rsqrt(row_mean(centered * centered) + EPS)
    return centered * inv, inv


def normalize_back(grad, normed, inv):
    return inv * (grad - row_mean(grad) - normed * row_mean(grad * normed))


def ffn_kernel(
    panels,
    x_ref,
    mixed_ref,
    cot_ref,
    wo_ref,
    small_ref,
    bias_ref,
    w_in_ref,
    w_out_ref,
    y_ref,
    d_first_ref,
    d_mixed_ref,
    d_small_ref,
    d_bias_ref,
    d_weights_ref,
    n_one,
    inv_one,
    low,
    hidden,
    slope,
    d_inner,
    d_in_stage,
    d_out_stage,
    in_sems,
    out_sems,
):
    step = pl.program_id(0)
    tokens, width = x_ref.shape
    chunks = tokens // ROWS
    acc, d_outer = d_first_ref, d_mixed_ref
    units = d_weights_ref.shape[0]
    some = units // panels

    def in_copy(panel, slot):
        return pltpu.make_async_copy(
            d_in_stage.at[slot], d_weights_ref.at[:, panels + panel], in_sems.at[slot]
        )

    def out_copy(panel, slot):
        return pltpu.make_async_copy(
            d_out_stage.at[slot],
            d_weights_ref.at[pl.ds(panel * some, some), pl.ds(0, panels)],
            out_sems.at[slot],
        )

    def square(ref):
        return ref[...].reshape(width, width)

    gain_one, shift_one, outer_bias, gain_two, shift_two = (
        small_ref[i : i + 1, :] for i in range(5)
    )

    @pl.when(step == 0)
    def _():
        def body(i, carry):
            rows = pl.ds(pl.multiple_of(i * ROWS, ROWS), ROWS)
            first = x_ref[rows, :].astype(F32) + nn(mixed_ref[rows, :], square(wo_ref))
            normed, inv = normalize(first)
            n_one[rows, :] = normed
            inv_one[rows, :] = jnp.broadcast_to(inv, (ROWS, LANES))
            out = normed * gain_one + shift_one
            low[rows, :] = out.astype(BF16)
            acc[rows, :] = out + outer_bias
            return carry

        lax.fori_loop(0, chunks, body, 0)

    @pl.when(step < panels)
    def _():
        def body(i, carry):
            rows = pl.ds(pl.multiple_of(i * ROWS, ROWS), ROWS)
            inner = nn(low[rows, :], square(w_in_ref)) + bias_ref[0]
            cdf = 0.5 * (1.0 + lax.erf(inner * 0.7071067811865476))
            pdf = HALF_PI * jnp.exp(-0.5 * inner * inner)
            out = (inner * cdf).astype(BF16)
            hidden[step, rows, :] = out
            slope[step, rows, :] = cdf + inner * pdf
            acc[rows, :] += nn(out, square(w_out_ref))
            return carry

        lax.fori_loop(0, chunks, body, 0)

    @pl.when(step == panels)
    def _():
        def body(i, carry):
            d_gain, d_shift, d_bias = carry
            rows = pl.ds(pl.multiple_of(i * ROWS, ROWS), ROWS)
            normed, inv = normalize(acc[rows, :])
            y_ref[rows, :] = (normed * gain_two + shift_two).astype(BF16)
            grad = cot_ref[rows, :].astype(F32)
            d_second = normalize_back(grad * gain_two, normed, inv)
            low_grad = d_second.astype(BF16)
            acc[rows, :] = d_second
            d_outer[rows, :] = low_grad
            return (
                d_gain + row_sum(grad * normed),
                d_shift + row_sum(grad),
                d_bias + row_sum(low_grad.astype(F32)),
            )

        zero = jnp.zeros((1, width), F32)
        d_gain, d_shift, d_bias = lax.fori_loop(0, chunks, body, (zero, zero, zero))
        d_small_ref[2:3, :] = d_bias
        d_small_ref[3:4, :] = d_gain
        d_small_ref[4:5, :] = d_shift
        d_small_ref[5:, :] = jnp.zeros((3, width), F32)

    @pl.when(step >= panels)
    def _():
        panel = step - panels

        def body(i, d_bias):
            rows = pl.ds(pl.multiple_of(i * ROWS, ROWS), ROWS)
            d_hidden = nt(d_outer[rows, :], square(w_out_ref))
            grad = (d_hidden * slope[panel, rows, :]).astype(BF16)
            d_inner[rows, :] = grad
            acc[rows, :] += nt(grad, square(w_in_ref))
            return d_bias + row_sum(grad.astype(F32))

        d_bias_ref[0] = lax.fori_loop(0, chunks, body, jnp.zeros(d_bias_ref.shape[1:], F32))
        slot = lax.rem(panel, 2)

        @pl.when(panel >= 2)
        def _():
            in_copy(panel - 2, slot).wait()
            out_copy(panel - 2, slot).wait()

        d_out_stage[slot] = tn(hidden[panel], d_outer[...]).astype(BF16).reshape(d_out_stage.shape[1:])
        out_copy(panel, slot).start()
        d_in_stage[slot] = tn(low[...], d_inner[...]).astype(BF16).reshape(d_in_stage.shape[1:])
        in_copy(panel, slot).start()

    @pl.when(step == 2 * panels - 1)
    def _():
        def body(i, carry):
            d_gain, d_shift = carry
            rows = pl.ds(pl.multiple_of(i * ROWS, ROWS), ROWS)
            grad = acc[rows, :]
            normed = n_one[rows, :]
            d_first = normalize_back(grad * gain_one, normed, inv_one[rows, 0:1])
            d_first_ref[rows, :] = d_first
            low_grad = d_first.astype(BF16)
            d_inner[rows, :] = low_grad
            d_mixed_ref[rows, :] = nt(low_grad, square(wo_ref)).astype(BF16)
            return d_gain + row_sum(grad * normed), d_shift + row_sum(grad)

        zero = jnp.zeros((1, width), F32)
        d_gain, d_shift = lax.fori_loop(0, chunks, body, (zero, zero))
        d_small_ref[0:1, :] = d_gain
        d_small_ref[1:2, :] = d_shift
        slot = panels % 2
        in_copy(panels - 2, slot).wait()
        d_wo = tn(mixed_ref[...], d_inner[...])
        d_in_stage[slot] = d_wo.astype(BF16).reshape(d_in_stage.shape[1:])
        in_copy(panels, slot).start()
        out_copy(panels - 2, slot).wait()
        in_copy(panels - 1, 1 - slot).wait()
        out_copy(panels - 1, 1 - slot).wait()
        in_copy(panels, slot).wait()


def feed_forward(x, mixed, cot, small, bias, weights):
    tokens, width = x.shape
    units, groups, rows_in, _ = weights.shape
    panels = groups // 2
    panel = width

    def whole(*shape):
        return pl.BlockSpec(
            shape, lambda j: (0,) * len(shape), pipeline_mode=pl.Buffered(buffer_count=1)
        )

    def later(j):
        return jnp.maximum(j - panels, 0)

    return pl.pallas_call(
        functools.partial(ffn_kernel, panels),
        grid=(2 * panels,),
        in_specs=[
            whole(tokens, width),
            whole(tokens, width),
            whole(tokens, width),
            pl.BlockSpec(
                (units, 1, rows_in, width),
                lambda j: (0, 2 * panels, 0, 0),
                pipeline_mode=pl.Buffered(buffer_count=1),
            ),
            whole(8, width),
            pl.BlockSpec((1, 1, panel), lambda j: (lax.rem(j, panels), 0, 0)),
            pl.BlockSpec((units, 1, rows_in, width), lambda j: (0, panels + lax.rem(j, panels), 0, 0)),
            pl.BlockSpec(
                (units // panels, panels, rows_in, width), lambda j: (lax.rem(j, panels), 0, 0, 0)
            ),
        ],
        out_specs=[
            whole(tokens, width),
            whole(tokens, width),
            whole(tokens, width),
            whole(8, width),
            pl.BlockSpec((1, 1, panel), lambda j: (later(j), 0, 0)),
            pl.BlockSpec(memory_space=pl.ANY),
        ],
        out_shape=[
            jax.ShapeDtypeStruct((tokens, width), BF16),
            jax.ShapeDtypeStruct((tokens, width), F32),
            jax.ShapeDtypeStruct((tokens, width), BF16),
            jax.ShapeDtypeStruct((8, width), F32),
            jax.ShapeDtypeStruct((panels, 1, panel), F32),
            jax.ShapeDtypeStruct(weights.shape, BF16),
        ],
        scratch_shapes=[
            pltpu.VMEM((tokens, width), F32),
            pltpu.VMEM((tokens, LANES), F32),
            pltpu.VMEM((tokens, width), BF16),
            pltpu.VMEM((panels, tokens, panel), BF16),
            pltpu.VMEM((panels, tokens, panel), F32),
            pltpu.VMEM((tokens, panel), BF16),
            pltpu.VMEM((2, units, rows_in, width), BF16),
            pltpu.VMEM((2, units // panels, panels, rows_in, width), BF16),
            pltpu.SemaphoreType.DMA((2,)),
            pltpu.SemaphoreType.DMA((2,)),
        ],
        compiler_params=pltpu.CompilerParams(vmem_limit_bytes=60 << 20),
        cost_estimate=QUICK,
        name="ffn",
    )(x, mixed, cot, weights, small, bias, weights, weights)


def pack_kernel(outer_ref, inner_ref, out_ref, packed_ref):
    rows, width = outer_ref.shape
    share = out_ref.shape[0]
    packed_ref[:rows, :] = outer_ref[...]
    for panel in range(inner_ref.shape[1] // width):
        at = rows + panel * share
        packed_ref[at : at + share, :] = inner_ref[:, panel * width : (panel + 1) * width]
    packed_ref[packed_ref.shape[0] - share :, :] = out_ref[...]


def pack(outer, inner, out):
    share, width = out.shape
    panels = inner.shape[1] // width
    if share % 8:
        inner = inner.reshape(share, panels, width).swapaxes(0, 1).reshape(-1, width)
        return jnp.concatenate((outer, inner, out), axis=0)
    rows = outer.shape[0] + (panels + 1) * share
    return pl.pallas_call(
        pack_kernel,
        out_shape=jax.ShapeDtypeStruct((rows, width), BF16),
        cost_estimate=QUICK,
        name="pack",
    )(outer, inner, out)


SOON = 160
SMALL = 16


def small_block(taps, vectors, bias, width):
    share = taps.shape[1]
    rows = jnp.concatenate([taps.astype(F32)] + [v.astype(F32) for v in vectors], axis=0)
    rows = jnp.concatenate((rows, jnp.zeros((rows.shape[0], width - share), F32)), axis=1)
    bias = bias.astype(F32)
    last = jnp.concatenate((bias, jnp.zeros((1, width - bias.shape[1]), F32)), axis=1)
    return jnp.concatenate((rows, last), axis=0).astype(BF16)


def stack_kernel(q_ref, k_ref, v_ref, taps_ref, a_ref, b_ref, c_ref, d_ref, e_ref, bias_ref, out_ref):
    share, width = q_ref.shape
    for place, ref in enumerate((q_ref, k_ref, v_ref)):
        out_ref[place * share : (place + 1) * share, :] = ref[...]
    vectors = [ref[...] for ref in (a_ref, b_ref, c_ref, d_ref, e_ref)]
    out_ref[3 * share :, :] = small_block(taps_ref[...], vectors, bias_ref[...], width)


def stack(query, key, value, taps, vectors, bias):
    share, width = query.shape
    vectors = [v.reshape(1, -1) for v in vectors]
    bias = bias.reshape(1, -1)
    if share % 8:
        return jnp.concatenate((query, key, value, small_block(taps, vectors, bias, width)), axis=0)
    return pl.pallas_call(
        stack_kernel,
        out_shape=jax.ShapeDtypeStruct((3 * share + SMALL, width), BF16),
        cost_estimate=QUICK,
        name="stack",
    )(query, key, value, taps, *vectors, bias)


def square_of(w_ref, place):
    units, _, width = w_ref.shape
    part = width // units
    return w_ref[:, place * part : (place + 1) * part, :].reshape(width, width)


def project_own_kernel(x_ref, w_ref, q_ref, k_ref, v_ref):
    for place, ref in enumerate((q_ref, k_ref, v_ref)):
        ref[0] = nn(x_ref[0], square_of(w_ref, place)).astype(BF16)


def project_halos_kernel(
    x_ref, own_k_ref, own_v_ref, left_ref, right_ref, far_ref, w_ref, k_ref, v_ref, ext_ref
):
    group, width = x_ref.shape[1:]
    right = HALO + group
    ext_ref[0, :HALO, :] = left_ref[0]
    ext_ref[0, HALO:right, :] = x_ref[0]
    ext_ref[0, right : right + HALO, :] = right_ref[0]
    row = lax.broadcasted_iota(jnp.int32, (PAD, width), 0)
    far = jnp.where(row == 0, jnp.broadcast_to(far_ref[0].astype(F32), (PAD, width)), 0.0)
    ext_ref[0, right + HALO :, :] = far.astype(BF16)
    halos = jnp.concatenate((ext_ref[0, :HALO, :], ext_ref[0, right:, :]), axis=0)
    for place, own_ref, ref in ((1, own_k_ref, k_ref), (2, own_v_ref, v_ref)):
        rows = nn(halos, square_of(w_ref, place)).astype(BF16)
        ref[0, :HALO, :] = rows[:HALO]
        ref[0, HALO:right, :] = own_ref[0]
        ref[0, right:, :] = rows[HALO:]


def resident(*shape):
    return pl.BlockSpec(
        shape, lambda s: (0,) * len(shape), pipeline_mode=pl.Buffered(buffer_count=1)
    )


def project_own(x, weights):
    seqs, group, width = x.shape
    return pl.pallas_call(
        project_own_kernel,
        grid=(seqs,),
        in_specs=[by_seq(group, width), resident(*weights.shape)],
        out_specs=[by_seq(group, width)] * 3,
        out_shape=[jax.ShapeDtypeStruct(x.shape, BF16)] * 3,
        compiler_params=pltpu.CompilerParams(vmem_limit_bytes=60 << 20),
        cost_estimate=QUICK,
        name="project_own",
    )(x, weights)


def project_halos(x, own_keys, own_values, left, right, far, weights):
    seqs, group, width = x.shape
    ext = group + 2 * HALO + PAD
    return pl.pallas_call(
        project_halos_kernel,
        grid=(seqs,),
        in_specs=[by_seq(group, width)] * 3
        + [by_seq(HALO, width), by_seq(HALO, width), by_seq(1, width), resident(*weights.shape)],
        out_specs=[by_seq(ext, width)] * 3,
        out_shape=[jax.ShapeDtypeStruct((seqs, ext, width), BF16)] * 3,
        compiler_params=pltpu.CompilerParams(vmem_limit_bytes=60 << 20),
        cost_estimate=QUICK,
        name="project_halos",
    )(x, own_keys, own_values, left, right, far, weights)


def input_grad_kernel(
    dq_ref, dk_ref, dv_ref, first_ref, w_ref, a_ref, b_ref, c_ref, d_ref, far_ref, own_ref
):
    right = HALO + dq_ref.shape[1]
    grad = nt(dk_ref[0], square_of(w_ref, 1)) + nt(dv_ref[0], square_of(w_ref, 2))
    for ref, at in ((a_ref, 0), (b_ref, right), (c_ref, SOON), (d_ref, right + SOON)):
        ref[0] = grad[at : at + ref.shape[1]].astype(BF16)
    far_ref[0] = grad[right + HALO : right + HALO + 1].astype(BF16)
    own_ref[0] = grad[HALO:right] + nt(dq_ref[0], square_of(w_ref, 0)) + first_ref[0]


def input_grads(d_queries, d_keys, d_values, d_first, weights):
    seqs, group, width = d_queries.shape
    ext = d_keys.shape[1]
    rows = (SOON, SOON, HALO - SOON, HALO - SOON)
    return pl.pallas_call(
        input_grad_kernel,
        grid=(seqs,),
        in_specs=[
            by_seq(group, width),
            by_seq(ext, width),
            by_seq(ext, width),
            by_seq(group, width),
            resident(*weights.shape),
        ],
        out_specs=[by_seq(n, width) for n in rows + (1, group)],
        out_shape=[jax.ShapeDtypeStruct((seqs, n, width), BF16) for n in rows + (1,)]
        + [jax.ShapeDtypeStruct((seqs, group, width), F32)],
        compiler_params=pltpu.CompilerParams(vmem_limit_bytes=60 << 20),
        cost_estimate=QUICK,
        name="input_grads",
    )(d_queries, d_keys, d_values, d_first, weights)


def weight_grad_kernel(
    x_ref, dq_ref, dk_ref, dv_ref, small_ref, out_ref, acc, x_tail, dk_tail, dv_tail
):
    seq = pl.program_id(0)
    group, width = dq_ref.shape[1:]
    units = out_ref.shape[0]
    part = width // units
    main = 2 * HALO + group

    @pl.when(seq == 0)
    def _():
        acc[...] = jnp.zeros_like(acc)

    rows = pl.ds(pl.multiple_of(seq * PAD, PAD), PAD)
    for tail, ref in ((x_tail, x_ref), (dk_tail, dk_ref), (dv_tail, dv_ref)):
        tail[rows, :] = ref[0, main:, :]
    acc[0] += tn(x_ref[0, HALO : HALO + group, :], dq_ref[0])
    acc[1] += tn(x_ref[0, :main, :], dk_ref[0, :main, :])
    acc[2] += tn(x_ref[0, :main, :], dv_ref[0, :main, :])

    @pl.when(seq == pl.num_programs(0) - 1)
    def _():
        ends = (None, tn(x_tail[...], dk_tail[...]), tn(x_tail[...], dv_tail[...]))
        for place, end in enumerate(ends):
            total = acc[place] if end is None else acc[place] + end
            out_ref[:, place * part : (place + 1) * part, :] = total.astype(BF16).reshape(
                units, part, width
            )
        out_ref[:, 3 * part :, :] = small_ref[...]


def weight_grads(x_ext, d_queries, d_keys, d_values, small):
    seqs, group, width = d_queries.shape
    ext = x_ext.shape[1]
    units, small_rows, _ = small.shape
    shape = (units, 3 * (width // units) + small_rows, width)
    tail = pltpu.VMEM((seqs * PAD, width), BF16)
    return pl.pallas_call(
        weight_grad_kernel,
        grid=(seqs,),
        in_specs=[
            by_seq(ext, width),
            by_seq(group, width),
            by_seq(ext, width),
            by_seq(ext, width),
            resident(*small.shape),
        ],
        out_specs=resident(*shape),
        out_shape=jax.ShapeDtypeStruct(shape, BF16),
        scratch_shapes=[pltpu.VMEM((3, width, width), F32), tail, tail, tail],
        compiler_params=pltpu.CompilerParams(vmem_limit_bytes=60 << 20),
        cost_estimate=QUICK,
        name="weight_grads",
    )(x_ext, d_queries, d_keys, d_values, small)


def document_of(positions, lengths, seq_len):
    count = lengths.shape[1]
    order = jnp.arange(count)
    ends = jnp.sum(jnp.where(order[None, :] <= order[:, None], lengths[:, None, :], 0), axis=2)
    counted = jnp.sum((positions[None, :, None] >= ends[:, None, :]).astype(jnp.int32), axis=2)
    inside = (positions >= 0) & (positions < seq_len)
    return jnp.where(inside[None, :], counted, -1)


def masks(lengths, offset, group, seq_len):
    ext = group + 2 * HALO
    slots = ext // 4
    positions = offset - HALO + jnp.arange(ext + PAD, dtype=jnp.int32)
    doc = document_of(positions, lengths, seq_len)
    slot_doc = doc[:, 2:ext:4]
    biases = []
    for block in range(group // QB):
        near = HALO - WIN // 2 + block * QB
        far = block * QB // 4
        key_place = jnp.concatenate((jnp.arange(near, near + NEAR), 4 * jnp.arange(far, far + FAR) + 2))
        reach = jnp.concatenate((jnp.full((NEAR,), WIN // 2), jnp.full((FAR,), PWIN // 2)))
        key_doc = jnp.concatenate((doc[:, near : near + NEAR], slot_doc[:, far : far + FAR]), axis=1)
        query_place = HALO + block * QB + jnp.arange(QB)
        query_doc = doc[:, HALO + block * QB : HALO + (block + 1) * QB]
        allowed = (jnp.abs(key_place[:, None] - query_place[None, :]) <= reach[:, None])[None] & (
            key_doc[:, :, None] == query_doc[:, None, :]
        )
        biases.append(jnp.where(allowed, 0.0, MASKED).astype(F32))
    same = jnp.stack(
        [(doc[:, tap : tap + ext : 4] == slot_doc).astype(F32) for tap in range(5)], axis=1
    )
    same = jnp.broadcast_to(same[..., None], same.shape + (LANES,))
    return jnp.stack(biases, axis=1), same, slots


def steps(count):
    for k in range(1, count):
        if count & (count - 1) == 0:
            yield [(i, i ^ k) for i in range(count)], lambda me, k=k: (me ^ k, me ^ k)
        else:
            yield (
                [(i, (i + k) % count) for i in range(count)],
                lambda me, k=k: (lax.rem(me + k, count), lax.rem(me - k + count, count)),
            )


def pick(value, index, dim=0):
    return lax.dynamic_index_in_dim(value, index, dim, keepdims=False)


def gather_seq(block, *earlier):
    count, me = lax.axis_size("seq"), lax.axis_index("seq")
    zeros = (0,) * block.ndim
    came_all = after(tuple(lax.ppermute(block, "seq", pairs) for pairs, _ in steps(count)), *earlier)
    column = jnp.zeros((count,) + block.shape, block.dtype)
    column = lax.dynamic_update_slice(column, block[None], (me,) + zeros)
    for came, (_, met) in zip(came_all, steps(count)):
        column = lax.dynamic_update_slice(column, came[None], (met(me)[1],) + zeros)
    return column


def gather_yx(column):
    me = lax.axis_index("yx")
    pieces = [(column, me)]
    for pairs, met in steps(lax.axis_size("yx")):
        pieces.append((lax.ppermute(column, "yx", pairs), met(me)[1]))
    return pieces


def assemble_kernel(count, *refs):
    places, parts, whole, sems = refs[0], refs[1 : 1 + count], refs[-2], refs[-1]
    copies = [
        pltpu.make_async_copy(part, whole.at[places[i]], sems.at[i]) for i, part in enumerate(parts)
    ]
    for copy in copies:
        copy.start()
    for copy in copies:
        copy.wait()


def gather_core(pieces):
    count, me = lax.axis_size("core"), lax.axis_index("core")
    parts, places = [], []
    for piece, place in pieces:
        parts.append(piece)
        places.append(place * count + me)
        for pairs, met in steps(count):
            parts.append(lax.ppermute(piece, "core", pairs))
            places.append(place * count + met(me)[1])
    return pl.pallas_call(
        functools.partial(assemble_kernel, len(parts)),
        in_specs=[pl.BlockSpec(memory_space=pltpu.SMEM)]
        + [pl.BlockSpec(memory_space=pltpu.VMEM)] * len(parts),
        out_specs=pl.BlockSpec(memory_space=pl.ANY),
        out_shape=jax.ShapeDtypeStruct((len(parts),) + parts[0].shape, BF16),
        compiler_params=pltpu.CompilerParams(vmem_limit_bytes=60 << 20),
        scratch_shapes=[pltpu.SemaphoreType.DMA((len(parts),))],
        cost_estimate=QUICK,
        name="assemble",
    )(jnp.stack(places).astype(jnp.int32), *parts)


def after(value, *earlier):
    return lax.optimization_barrier((value, earlier))[0] if earlier else lax.optimization_barrier(value)


def exchange_sum(pieces, axis, *earlier):
    me = lax.axis_index(axis)
    came = [
        lax.ppermute(pick(pieces, met(me)[0]), axis, pairs)
        for pairs, met in steps(lax.axis_size(axis))
    ]
    total = pick(pieces, me).astype(F32)
    for part in after(came, *earlier):
        total = total + part.astype(F32)
    return total


def local(
    tokens,
    doc_lengths,
    query_weight,
    key_weight,
    value_weight,
    out_weight,
    pool_weight,
    first_gain,
    first_shift,
    inner_weight,
    inner_bias,
    outer_weight,
    outer_bias,
    second_gain,
    second_shift,
    cotangent,
):
    seq_count = lax.axis_size("seq")
    yx_count = lax.axis_size("yx")
    core_count = lax.axis_size("core")
    units = yx_count * core_count
    parts = units * seq_count
    seq_place = lax.axis_index("seq")
    seqs, group, width = tokens.shape
    ff = inner_weight.shape[1]
    panels = ff // width
    share = query_weight.shape[0]
    count = seqs * group

    def shift(value, by):
        pairs = [(i, i + by) for i in range(seq_count) if 0 <= i + by < seq_count]
        return lax.ppermute(value, "seq", pairs)

    early = stack(
        query_weight,
        key_weight,
        value_weight,
        pool_weight,
        (first_gain, first_shift, outer_bias, second_gain, second_shift),
        inner_bias,
    )
    late = pack(outer_weight, inner_weight, out_weight)
    bias, same, _ = masks(doc_lengths, seq_place * group, group, group * seq_count)
    early_column, bias, same = after((gather_seq(early), bias, same))
    sent = after(tokens, early_column)
    came = (
        shift(sent[:, group - HALO :], 1),
        shift(sent[:, :HALO], -1),
        shift(sent[:, :1], -2),
    )
    early_column = jnp.concatenate(
        [early_column[:, i * share : (i + 1) * share].reshape(-1, width) for i in range(3)]
        + [early_column[:, 3 * share :].reshape(-1, width)],
        axis=0,
    )
    early_pieces = gather_yx(early_column)
    early = gather_core(early_pieces)
    late_column = lax.all_gather(late, "seq", axis=0)
    late_column = after(late_column, [piece for piece, _ in early_pieces[1:]])
    outer_rows = panels * share
    late_column = jnp.concatenate(
        (
            late_column[:, :outer_rows].reshape(-1, width),
            late_column[:, outer_rows:]
            .reshape(seq_count, panels + 1, share, width)
            .swapaxes(0, 1)
            .reshape(-1, width),
        ),
        axis=0,
    )
    late = lax.all_gather(late_column, ("yx", "core"), axis=0)
    late = late.reshape(units, 2 * panels + 1, seq_count * share, width)
    small = early[:, 3 * seq_count * share :].reshape(parts, SMALL, width)
    vectors = small[:, : SMALL - 1, :share].transpose(1, 0, 2).reshape(SMALL - 1, width).astype(F32)
    taps = jnp.pad(vectors[:10], ((0, 6), (0, 0)))
    small_rows_f32 = jnp.pad(vectors[10:], ((0, 3), (0, 0)))
    bias_inner = small[:, SMALL - 1, : ff // parts].reshape(panels, 1, width).astype(F32)

    flat = tokens.reshape(count, width)

    queries, own_keys, own_values = project_own(tokens, early)
    keys, values, x_ext = project_halos(tokens, own_keys, own_values, *came, early)
    mixed, lse = attention_forward(queries, keys, values, taps, same, bias)
    y, d_first, d_mixed, d_small, d_bias, d_late = feed_forward(
        flat,
        mixed.reshape(count, width),
        cotangent.reshape(count, width),
        small_rows_f32,
        bias_inner,
        late,
    )
    late_sum = lax.psum_scatter(
        d_late.reshape(-1, width), ("yx", "core"), scatter_dimension=0, tiled=True
    )
    d_queries, d_keys, d_values, d_taps = attention_backward(
        queries,
        keys,
        values,
        taps,
        same,
        bias,
        lse,
        d_mixed.reshape(seqs, group, width),
        0,
        seqs,
        (),
    )
    left_a, right_a, left_b, right_b, far, own = input_grads(
        d_queries, d_keys, d_values, d_first.reshape(seqs, group, width), early
    )
    came = (shift(left_a, -1), shift(right_a, 1))
    later_came = (shift(left_b, -1), shift(right_b, 1), shift(far, 2))

    d_taps = jnp.sum(d_taps, axis=0)[:10]
    d_vectors = jnp.concatenate((d_taps, d_small[:5]), axis=0)
    d_vectors = d_vectors.reshape(SMALL - 1, parts, share).transpose(1, 0, 2)
    d_vectors = jnp.pad(d_vectors, ((0, 0), (0, 0), (0, width - share)))
    d_bias = jnp.pad(d_bias.reshape(parts, 1, -1), ((0, 0), (0, 0), (0, width - ff // parts)))
    d_vectors = jnp.concatenate((d_vectors, d_bias), axis=1).astype(BF16)
    d_vectors = d_vectors.reshape(units, seq_count * SMALL, width)
    early_sum = weight_grads(after(x_ext, own), d_queries, d_keys, d_values, d_vectors)
    early_sum = early_sum.reshape(yx_count, core_count, -1, width)
    early_sum, came = after((early_sum, came))
    early_sum = exchange_sum(early_sum.swapaxes(0, 1), "core").astype(BF16)
    outer_all = seq_count * outer_rows
    late_sum = jnp.concatenate(
        (
            late_sum[:outer_all].reshape(seq_count, outer_rows, width),
            late_sum[outer_all:]
            .reshape(panels + 1, seq_count, share, width)
            .swapaxes(0, 1)
            .reshape(seq_count, (panels + 1) * share, width),
        ),
        axis=1,
    )
    late_sum = exchange_sum(late_sum, "seq")
    early_sum = exchange_sum(early_sum, "yx", late_sum, later_came).astype(BF16)
    whole = 3 * seq_count * share
    early_sum = jnp.concatenate(
        [
            early_sum[:whole]
            .reshape(3, seq_count, share, width)
            .swapaxes(0, 1)
            .reshape(seq_count, 3 * share, width),
            early_sum[whole:].reshape(seq_count, SMALL, width),
        ],
        axis=1,
    )
    early_sum = exchange_sum(early_sum, "seq")

    edge = group - HALO
    from_right, from_left = (
        jnp.concatenate(parts, axis=1).astype(F32) for parts in zip(came, later_came)
    )
    from_far = later_came[2].astype(F32)
    d_input = own + jnp.pad(from_right, ((0, 0), (edge, 0), (0, 0)))
    d_input = d_input + jnp.pad(from_left, ((0, 0), (0, edge), (0, 0)))
    d_input = d_input + jnp.pad(from_far, ((0, 0), (0, group - 1), (0, 0)))

    vector_sum = early_sum[3 * share :]
    pieces = [vector_sum[10 + i, :share] for i in range(5)]
    return (
        y.reshape(seqs, group, width),
        d_input.astype(BF16),
        early_sum[:share],
        early_sum[share : 2 * share],
        early_sum[2 * share : 3 * share],
        late_sum[2 * outer_rows :],
        vector_sum[:10, :share],
        pieces[0],
        pieces[1],
        late_sum[outer_rows : 2 * outer_rows]
        .reshape(panels, share, width)
        .transpose(1, 0, 2)
        .reshape(share, ff),
        vector_sum[SMALL - 1, : ff // parts],
        late_sum[:outer_rows],
        pieces[2],
        pieces[3],
        pieces[4],
    )


def solution(mesh):
    dp, seq = mesh.devices.shape
    cores = 2 if dp % 2 == 0 else 1
    mesh = Mesh(mesh.devices.reshape(dp // cores, cores, seq), ("yx", "core", "seq"))
    every = ("yx", "core", "seq")
    rows = P(every, None)
    vector = P(every)
    whole = P(("yx", "core"), "seq", None)
    taps = P(None, every)
    weights = (rows, rows, rows, rows, taps, vector, vector, rows, vector, rows, vector, vector, vector)
    return jax.shard_map(
        local,
        mesh=mesh,
        in_specs=(whole, P(("yx", "core"), None)) + weights + (whole,),
        out_specs=(whole, whole) + weights,
        check_vma=False,
    )
```

```python
import functools

import jax
import jax.numpy as jnp
from jax import lax
from jax.experimental import pallas as pl
from jax.experimental.pallas import tpu as pltpu
from jax.sharding import Mesh
from jax.sharding import PartitionSpec as P

HEADS = 12
HEAD_DIM = 64
WIN = 128
PWIN = 512
EPS = 1e-05

LANES = 128
QB = 128
GROUP = 6
GROUP_BACK = 2
HALO = PWIN // 2
PAD = 16
NEAR = QB + WIN
FAR = (QB + PWIN) // 4
KEYS = NEAR + FAR
MASKED = -1e30
QUICK = pl.CostEstimate(flops=1 << 20, bytes_accessed=1 << 20, transcendentals=0)

F32 = jnp.float32
BF16 = jnp.bfloat16


def nt(left, right):
    return lax.dot_general(left, right, (((1,), (1,)), ((), ())), preferred_element_type=F32)


def tn(left, right):
    return lax.dot_general(left, right, (((0,), (0,)), ((), ())), preferred_element_type=F32)


def nn(left, right):
    return lax.dot_general(left, right, (((1,), (0,)), ((), ())), preferred_element_type=F32)


def slot_taps(wide, slots):
    return [wide[pl.ds(tap, slots, stride=4), :] for tap in range(5)]


def pool(taps, same_ref, w_ref, first, lanes):
    total = None
    for tap in range(5):
        term = taps[tap] * same_ref[0, tap] * w_ref[first + tap : first + tap + 1, lanes]
        total = term if total is None else total + term
    return total.astype(BF16)


def pair_stack(rows):
    lane = lax.broadcasted_iota(jnp.int32, rows.shape, 1)
    zero = jnp.zeros_like(rows)
    return jnp.concatenate(
        (jnp.where(lane < HEAD_DIM, rows, zero), jnp.where(lane < HEAD_DIM, zero, rows)), axis=0
    )


def pair_join(both):
    joined = jnp.concatenate((both[:HEAD_DIM, :QB], both[HEAD_DIM:, QB:]), axis=0)
    return joined.T


def rows_of(block):
    return slice(block * QB, (block + 1) * QB)


def keys_of(ref, pooled, block, lanes):
    near = HALO - WIN // 2 + block * QB
    far = block * QB // 4
    return jnp.concatenate((ref[0, near : near + NEAR, lanes], pooled[far : far + FAR, :]), axis=0)


def scores_of(keys, stacked, bias):
    return nt(keys, stacked) + jnp.concatenate((bias, bias), axis=1)


def attn_fwd_kernel(
    q_ref, k_ref, v_ref, w_ref, same_ref, bias_ref, out_ref, lse_ref, k_wide, v_wide, pk_ref, pv_ref
):
    slots = pk_ref.shape[1]
    scale = jnp.asarray(HEAD_DIM**-0.5, BF16)

    blocks = q_ref.shape[1] // QB

    def body(step, carry):
        jobs = []
        for lane in range(GROUP):
            pair = step * GROUP + lane
            lanes = pl.ds(pl.multiple_of(pair * LANES, LANES), LANES)
            k_wide[lane] = k_ref[0, :, lanes].astype(F32)
            v_wide[lane] = v_ref[0, :, lanes].astype(F32)
            pk_ref[lane] = pool(slot_taps(k_wide.at[lane], slots), same_ref, w_ref, 0, lanes)
            pv_ref[lane] = pool(slot_taps(v_wide.at[lane], slots), same_ref, w_ref, 5, lanes)
            jobs += [(lane, pair, lanes, block) for block in range(blocks)]
        scores = []
        for lane, pair, lanes, block in jobs:
            stacked = pair_stack(q_ref[0, rows_of(block), lanes] * scale)
            keys = keys_of(k_ref, pk_ref.at[lane], block, lanes)
            scores.append(scores_of(keys, stacked, bias_ref[0, block]))
        probs = []
        for (lane, pair, lanes, block), score in zip(jobs, scores):
            top = jnp.max(score, axis=0, keepdims=True)
            weights = jnp.exp(score - top)
            denom = jnp.sum(weights, axis=0, keepdims=True)
            probs.append((weights * (1.0 / denom)).astype(BF16))
            lse_ref[0, pair, block : block + 1, :] = top + jnp.log(denom)
        mixed = []
        for (lane, pair, lanes, block), prob in zip(jobs, probs):
            mixed.append(tn(keys_of(v_ref, pv_ref.at[lane], block, lanes), prob))
        for (lane, pair, lanes, block), value in zip(jobs, mixed):
            out_ref[0, rows_of(block), lanes] = pair_join(value).astype(BF16)
        return carry

    lax.fori_loop(0, q_ref.shape[2] // (LANES * GROUP), body, 0)


def attn_bwd_kernel(
    q_ref,
    k_ref,
    v_ref,
    w_ref,
    same_ref,
    bias_ref,
    lse_ref,
    do_ref,
    dq_ref,
    dk_ref,
    dv_ref,
    dw_ref,
    k_wide,
    v_wide,
    pk_ref,
    pv_ref,
    dpk_ref,
    dpv_ref,
):
    slots = pk_ref.shape[1]
    scale = jnp.asarray(HEAD_DIM**-0.5, BF16)
    blocks = q_ref.shape[1] // QB

    def body(step, carry):
        jobs = []
        for lane in range(GROUP_BACK):
            pair = step * GROUP_BACK + lane
            lanes = pl.ds(pl.multiple_of(pair * LANES, LANES), LANES)
            k_wide[lane] = k_ref[0, :, lanes].astype(F32)
            v_wide[lane] = v_ref[0, :, lanes].astype(F32)
            pk_ref[lane] = pool(slot_taps(k_wide.at[lane], slots), same_ref, w_ref, 0, lanes)
            pv_ref[lane] = pool(slot_taps(v_wide.at[lane], slots), same_ref, w_ref, 5, lanes)
            jobs += [(lane, pair, lanes, block) for block in range(blocks)]
        dpk_ref[...] = jnp.zeros_like(dpk_ref)
        dpv_ref[...] = jnp.zeros_like(dpv_ref)
        scores, d_probs = [], []
        for lane, pair, lanes, block in jobs:
            keys = keys_of(k_ref, pk_ref.at[lane], block, lanes)
            stacked = pair_stack(q_ref[0, rows_of(block), lanes] * scale)
            scores.append(scores_of(keys, stacked, bias_ref[0, block]))
            values = keys_of(v_ref, pv_ref.at[lane], block, lanes)
            d_probs.append(nt(values, pair_stack(do_ref[0, rows_of(block), lanes])))
        probs, d_scores = [], []
        for (lane, pair, lanes, block), score, d_prob in zip(jobs, scores, d_probs):
            prob = jnp.exp(score - lse_ref[0, pair, block : block + 1, :])
            row_dot = jnp.sum(prob * d_prob, axis=0, keepdims=True)
            d_scores.append((prob * (d_prob - row_dot)).astype(BF16))
            probs.append(prob.astype(BF16))
        parts = []
        for (lane, pair, lanes, block), prob, d_score in zip(jobs, probs, d_scores):
            d_values = nn(prob, pair_stack(do_ref[0, rows_of(block), lanes]))
            d_keys = nn(d_score, pair_stack(q_ref[0, rows_of(block), lanes] * scale))
            far = slice(block * QB // 4, block * QB // 4 + FAR)
            dpk_ref[lane, far, :] += d_keys[NEAR:]
            dpv_ref[lane, far, :] += d_values[NEAR:]
            parts.append((d_keys[:NEAR], d_values[:NEAR]))
        d_queries = []
        for (lane, pair, lanes, block), d_score in zip(jobs, d_scores):
            d_queries.append(tn(keys_of(k_ref, pk_ref.at[lane], block, lanes), d_score))
        for (lane, pair, lanes, block), value in zip(jobs, d_queries):
            dq_ref[0, rows_of(block), lanes] = (pair_join(value) * HEAD_DIM**-0.5).astype(BF16)
        for lane in range(GROUP_BACK):
            lanes = jobs[lane * blocks][2]
            for side, (wide_ref, d_pool_ref, out_ref) in enumerate(
                ((k_wide, dpk_ref, dk_ref), (v_wide, dpv_ref, dv_ref))
            ):
                wide = wide_ref.at[lane]
                d_pool = d_pool_ref[lane]
                taps = slot_taps(wide, slots)
                masked = [d_pool * same_ref[0, tap] for tap in range(5)]
                places = [5 * side + tap for tap in range(5)]
                for tap, row in enumerate(places):
                    dw_ref[0, row : row + 1, lanes] = jnp.sum(
                        masked[tap] * taps[tap], axis=0, keepdims=True
                    )
                spread = [
                    masked[tap] * w_ref[row : row + 1, lanes] for tap, row in enumerate(places)
                ]
                wide[4 * slots :, :] = jnp.zeros((wide.shape[0] - 4 * slots, LANES), F32)
                for tap in range(4):
                    wide[pl.ds(tap, slots, stride=4), :] = spread[tap]
                wide[pl.ds(4, slots, stride=4), :] += spread[4]
                for block in range(blocks):
                    near = HALO - WIN // 2 + block * QB
                    wide[near : near + NEAR, :] += parts[lane * blocks + block][side]
                out_ref[0, :, lanes] = wide[...].astype(BF16)
        return carry

    lax.fori_loop(0, q_ref.shape[2] // (LANES * GROUP_BACK), body, 0)
    dw_ref[0, 10:, :] = jnp.zeros((dw_ref.shape[1] - 10, dw_ref.shape[2]), F32)


def by_seq(*shape, first=0):
    return pl.BlockSpec((1,) + shape, lambda s: (s + first,) + (0,) * len(shape))


def attention_specs(ext, group, slots, width, first=0):
    return [
        by_seq(group, width, first=first),
        by_seq(ext, width, first=first),
        by_seq(ext, width, first=first),
        pl.BlockSpec((16, width), lambda s: (0, 0)),
        by_seq(5, slots, LANES, first=first),
        by_seq(group // QB, KEYS, LANES, first=first),
    ]


def attention_forward(queries, keys, values, taps, same, bias):
    seqs, group, width = queries.shape
    ext = keys.shape[1]
    slots = same.shape[2]
    pairs = width // LANES
    blocks = group // QB
    wide = pltpu.VMEM((GROUP, ext, LANES), F32)
    pooled = pltpu.VMEM((GROUP, slots, LANES), BF16)
    return pl.pallas_call(
        attn_fwd_kernel,
        grid=(seqs,),
        in_specs=attention_specs(ext, group, slots, width),
        out_specs=[by_seq(group, width), by_seq(pairs, blocks, 2 * QB)],
        out_shape=[
            jax.ShapeDtypeStruct((seqs, group, width), BF16),
            jax.ShapeDtypeStruct((seqs, pairs, blocks, 2 * QB), F32),
        ],
        scratch_shapes=[wide, wide, pooled, pooled],
        compiler_params=pltpu.CompilerParams(vmem_limit_bytes=60 << 20),
        cost_estimate=QUICK,
        name="attn_fwd",
    )(queries, keys, values, taps, same, bias)


def attention_backward(queries, keys, values, taps, same, bias, lse, d_mixed, first, count, earlier):
    seqs, group, width = queries.shape
    ext = keys.shape[1]
    slots = same.shape[2]
    pairs = width // LANES
    blocks = group // QB
    wide = pltpu.VMEM((GROUP_BACK, ext, LANES), F32)
    pooled = pltpu.VMEM((GROUP_BACK, slots, LANES), BF16)
    d_pooled = pltpu.VMEM((GROUP_BACK, slots, LANES), F32)
    args = (queries, keys, values, taps, same, bias, lse, d_mixed)

    def kernel(*refs):
        attn_bwd_kernel(*refs[: len(args)], *refs[len(args) + len(earlier) :])

    return pl.pallas_call(
        kernel,
        grid=(count,),
        in_specs=attention_specs(ext, group, slots, width, first)
        + [by_seq(pairs, blocks, 2 * QB, first=first), by_seq(group, width, first=first)]
        + [pl.BlockSpec(memory_space=pl.ANY)] * len(earlier),
        out_specs=[
            by_seq(*shape, first=first)
            for shape in ((group, width), (ext, width), (ext, width), (16, width))
        ],
        out_shape=[
            jax.ShapeDtypeStruct((seqs, group, width), BF16),
            jax.ShapeDtypeStruct((seqs, ext, width), BF16),
            jax.ShapeDtypeStruct((seqs, ext, width), BF16),
            jax.ShapeDtypeStruct((seqs, 16, width), F32),
        ],
        input_output_aliases={len(args) + i: i for i in range(len(earlier))},
        scratch_shapes=[wide, wide, pooled, pooled, d_pooled, d_pooled],
        compiler_params=pltpu.CompilerParams(vmem_limit_bytes=60 << 20),
        cost_estimate=QUICK,
        name="attn_bwd",
    )(*args, *earlier)


ROWS = 512
HALF_PI = 0.3989422804014327


def row_sum(value):
    return jnp.sum(value, axis=0, keepdims=True)


def row_mean(value):
    return jnp.mean(value, axis=1, keepdims=True)


def normalize(value):
    centered = value - row_mean(value)
    inv = lax.rsqrt(row_mean(centered * centered) + EPS)
    return centered * inv, inv


def normalize_back(grad, normed, inv):
    return inv * (grad - row_mean(grad) - normed * row_mean(grad * normed))


def ffn_kernel(
    panels,
    x_ref,
    mixed_ref,
    cot_ref,
    wo_ref,
    small_ref,
    bias_ref,
    w_in_ref,
    w_out_ref,
    y_ref,
    d_first_ref,
    d_mixed_ref,
    d_small_ref,
    d_bias_ref,
    d_weights_ref,
    n_one,
    inv_one,
    low,
    hidden,
    slope,
    d_inner,
    d_in_stage,
    d_out_stage,
    in_sems,
    out_sems,
):
    step = pl.program_id(0)
    tokens, width = x_ref.shape
    chunks = tokens // ROWS
    acc, d_outer = d_first_ref, d_mixed_ref
    units = d_weights_ref.shape[0]
    some = units // panels

    def in_copy(panel, slot):
        return pltpu.make_async_copy(
            d_in_stage.at[slot], d_weights_ref.at[:, panels + panel], in_sems.at[slot]
        )

    def out_copy(panel, slot):
        return pltpu.make_async_copy(
            d_out_stage.at[slot],
            d_weights_ref.at[pl.ds(panel * some, some), pl.ds(0, panels)],
            out_sems.at[slot],
        )

    def square(ref):
        return ref[...].reshape(width, width)

    gain_one, shift_one, outer_bias, gain_two, shift_two = (
        small_ref[i : i + 1, :] for i in range(5)
    )

    @pl.when(step == 0)
    def _():
        def body(i, carry):
            rows = pl.ds(pl.multiple_of(i * ROWS, ROWS), ROWS)
            first = x_ref[rows, :].astype(F32) + nn(mixed_ref[rows, :], square(wo_ref))
            normed, inv = normalize(first)
            n_one[rows, :] = normed
            inv_one[rows, :] = jnp.broadcast_to(inv, (ROWS, LANES))
            out = normed * gain_one + shift_one
            low[rows, :] = out.astype(BF16)
            acc[rows, :] = out + outer_bias
            return carry

        lax.fori_loop(0, chunks, body, 0)

    @pl.when(step < panels)
    def _():
        def body(i, carry):
            rows = pl.ds(pl.multiple_of(i * ROWS, ROWS), ROWS)
            inner = nn(low[rows, :], square(w_in_ref)) + bias_ref[0]
            cdf = 0.5 * (1.0 + lax.erf(inner * 0.7071067811865476))
            pdf = HALF_PI * jnp.exp(-0.5 * inner * inner)
            out = (inner * cdf).astype(BF16)
            hidden[step, rows, :] = out
            slope[step, rows, :] = cdf + inner * pdf
            acc[rows, :] += nn(out, square(w_out_ref))
            return carry

        lax.fori_loop(0, chunks, body, 0)

    @pl.when(step == panels)
    def _():
        def body(i, carry):
            d_gain, d_shift, d_bias = carry
            rows = pl.ds(pl.multiple_of(i * ROWS, ROWS), ROWS)
            normed, inv = normalize(acc[rows, :])
            y_ref[rows, :] = (normed * gain_two + shift_two).astype(BF16)
            grad = cot_ref[rows, :].astype(F32)
            d_second = normalize_back(grad * gain_two, normed, inv)
            low_grad = d_second.astype(BF16)
            acc[rows, :] = d_second
            d_outer[rows, :] = low_grad
            return (
                d_gain + row_sum(grad * normed),
                d_shift + row_sum(grad),
                d_bias + row_sum(low_grad.astype(F32)),
            )

        zero = jnp.zeros((1, width), F32)
        d_gain, d_shift, d_bias = lax.fori_loop(0, chunks, body, (zero, zero, zero))
        d_small_ref[2:3, :] = d_bias
        d_small_ref[3:4, :] = d_gain
        d_small_ref[4:5, :] = d_shift
        d_small_ref[5:, :] = jnp.zeros((3, width), F32)

    @pl.when(step >= panels)
    def _():
        panel = step - panels

        def body(i, d_bias):
            rows = pl.ds(pl.multiple_of(i * ROWS, ROWS), ROWS)
            d_hidden = nt(d_outer[rows, :], square(w_out_ref))
            grad = (d_hidden * slope[panel, rows, :]).astype(BF16)
            d_inner[rows, :] = grad
            acc[rows, :] += nt(grad, square(w_in_ref))
            return d_bias + row_sum(grad.astype(F32))

        d_bias_ref[0] = lax.fori_loop(0, chunks, body, jnp.zeros(d_bias_ref.shape[1:], F32))
        slot = lax.rem(panel, 2)

        @pl.when(panel >= 2)
        def _():
            in_copy(panel - 2, slot).wait()
            out_copy(panel - 2, slot).wait()

        d_out_stage[slot] = tn(hidden[panel], d_outer[...]).astype(BF16).reshape(d_out_stage.shape[1:])
        out_copy(panel, slot).start()
        d_in_stage[slot] = tn(low[...], d_inner[...]).astype(BF16).reshape(d_in_stage.shape[1:])
        in_copy(panel, slot).start()

    @pl.when(step == 2 * panels - 1)
    def _():
        def body(i, carry):
            d_gain, d_shift = carry
            rows = pl.ds(pl.multiple_of(i * ROWS, ROWS), ROWS)
            grad = acc[rows, :]
            normed = n_one[rows, :]
            d_first = normalize_back(grad * gain_one, normed, inv_one[rows, 0:1])
            d_first_ref[rows, :] = d_first
            low_grad = d_first.astype(BF16)
            d_inner[rows, :] = low_grad
            d_mixed_ref[rows, :] = nt(low_grad, square(wo_ref)).astype(BF16)
            return d_gain + row_sum(grad * normed), d_shift + row_sum(grad)

        zero = jnp.zeros((1, width), F32)
        d_gain, d_shift = lax.fori_loop(0, chunks, body, (zero, zero))
        d_small_ref[0:1, :] = d_gain
        d_small_ref[1:2, :] = d_shift
        slot = panels % 2
        in_copy(panels - 2, slot).wait()
        d_wo = tn(mixed_ref[...], d_inner[...])
        d_in_stage[slot] = d_wo.astype(BF16).reshape(d_in_stage.shape[1:])
        in_copy(panels, slot).start()
        out_copy(panels - 2, slot).wait()
        in_copy(panels - 1, 1 - slot).wait()
        out_copy(panels - 1, 1 - slot).wait()
        in_copy(panels, slot).wait()


def feed_forward(x, mixed, cot, small, bias, weights):
    tokens, width = x.shape
    units, groups, rows_in, _ = weights.shape
    panels = groups // 2
    panel = width

    def whole(*shape):
        return pl.BlockSpec(
            shape, lambda j: (0,) * len(shape), pipeline_mode=pl.Buffered(buffer_count=1)
        )

    def later(j):
        return jnp.maximum(j - panels, 0)

    return pl.pallas_call(
        functools.partial(ffn_kernel, panels),
        grid=(2 * panels,),
        in_specs=[
            whole(tokens, width),
            whole(tokens, width),
            whole(tokens, width),
            pl.BlockSpec(
                (units, 1, rows_in, width),
                lambda j: (0, 2 * panels, 0, 0),
                pipeline_mode=pl.Buffered(buffer_count=1),
            ),
            whole(8, width),
            pl.BlockSpec((1, 1, panel), lambda j: (lax.rem(j, panels), 0, 0)),
            pl.BlockSpec((units, 1, rows_in, width), lambda j: (0, panels + lax.rem(j, panels), 0, 0)),
            pl.BlockSpec(
                (units // panels, panels, rows_in, width), lambda j: (lax.rem(j, panels), 0, 0, 0)
            ),
        ],
        out_specs=[
            whole(tokens, width),
            whole(tokens, width),
            whole(tokens, width),
            whole(8, width),
            pl.BlockSpec((1, 1, panel), lambda j: (later(j), 0, 0)),
            pl.BlockSpec(memory_space=pl.ANY),
        ],
        out_shape=[
            jax.ShapeDtypeStruct((tokens, width), BF16),
            jax.ShapeDtypeStruct((tokens, width), F32),
            jax.ShapeDtypeStruct((tokens, width), BF16),
            jax.ShapeDtypeStruct((8, width), F32),
            jax.ShapeDtypeStruct((panels, 1, panel), F32),
            jax.ShapeDtypeStruct(weights.shape, BF16),
        ],
        scratch_shapes=[
            pltpu.VMEM((tokens, width), F32),
            pltpu.VMEM((tokens, LANES), F32),
            pltpu.VMEM((tokens, width), BF16),
            pltpu.VMEM((panels, tokens, panel), BF16),
            pltpu.VMEM((panels, tokens, panel), F32),
            pltpu.VMEM((tokens, panel), BF16),
            pltpu.VMEM((2, units, rows_in, width), BF16),
            pltpu.VMEM((2, units // panels, panels, rows_in, width), BF16),
            pltpu.SemaphoreType.DMA((2,)),
            pltpu.SemaphoreType.DMA((2,)),
        ],
        compiler_params=pltpu.CompilerParams(vmem_limit_bytes=60 << 20),
        cost_estimate=QUICK,
        name="ffn",
    )(x, mixed, cot, weights, small, bias, weights, weights)


def pack_kernel(outer_ref, inner_ref, out_ref, packed_ref):
    rows, width = outer_ref.shape
    share = out_ref.shape[0]
    packed_ref[:rows, :] = outer_ref[...]
    for panel in range(inner_ref.shape[1] // width):
        at = rows + panel * share
        packed_ref[at : at + share, :] = inner_ref[:, panel * width : (panel + 1) * width]
    packed_ref[packed_ref.shape[0] - share :, :] = out_ref[...]


def pack(outer, inner, out):
    share, width = out.shape
    panels = inner.shape[1] // width
    if share % 8:
        inner = inner.reshape(share, panels, width).swapaxes(0, 1).reshape(-1, width)
        return jnp.concatenate((outer, inner, out), axis=0)
    rows = outer.shape[0] + (panels + 1) * share
    return pl.pallas_call(
        pack_kernel,
        out_shape=jax.ShapeDtypeStruct((rows, width), BF16),
        cost_estimate=QUICK,
        name="pack",
    )(outer, inner, out)


SMALL = 16


def small_block(taps, vectors, bias, width):
    share = taps.shape[1]
    rows = jnp.concatenate([taps.astype(F32)] + [v.astype(F32) for v in vectors], axis=0)
    rows = jnp.concatenate((rows, jnp.zeros((rows.shape[0], width - share), F32)), axis=1)
    bias = bias.astype(F32)
    last = jnp.concatenate((bias, jnp.zeros((1, width - bias.shape[1]), F32)), axis=1)
    return jnp.concatenate((rows, last), axis=0).astype(BF16)


def stack_kernel(q_ref, k_ref, v_ref, taps_ref, a_ref, b_ref, c_ref, d_ref, e_ref, bias_ref, out_ref):
    share, width = q_ref.shape
    for place, ref in enumerate((q_ref, k_ref, v_ref)):
        out_ref[place * share : (place + 1) * share, :] = ref[...]
    vectors = [ref[...] for ref in (a_ref, b_ref, c_ref, d_ref, e_ref)]
    out_ref[3 * share :, :] = small_block(taps_ref[...], vectors, bias_ref[...], width)


def stack(query, key, value, taps, vectors, bias):
    share, width = query.shape
    vectors = [v.reshape(1, -1) for v in vectors]
    bias = bias.reshape(1, -1)
    if share % 8:
        return jnp.concatenate((query, key, value, small_block(taps, vectors, bias, width)), axis=0)
    return pl.pallas_call(
        stack_kernel,
        out_shape=jax.ShapeDtypeStruct((3 * share + SMALL, width), BF16),
        cost_estimate=QUICK,
        name="stack",
    )(query, key, value, taps, *vectors, bias)


def square_of(w_ref, place):
    units, _, width = w_ref.shape
    part = width // units
    return w_ref[:, place * part : (place + 1) * part, :].reshape(width, width)


def project_own_kernel(x_ref, w_ref, q_ref, k_ref, v_ref):
    for place, ref in enumerate((q_ref, k_ref, v_ref)):
        ref[0] = nn(x_ref[0], square_of(w_ref, place)).astype(BF16)


def project_halos_kernel(
    own_k_ref, own_v_ref, left_ref, right_ref, far_ref, w_ref, k_ref, v_ref, halos
):
    group, width = own_k_ref.shape[1:]
    right = HALO + group
    halos[:HALO, :] = left_ref[0]
    halos[HALO : 2 * HALO, :] = right_ref[0]
    halos[2 * HALO :, :] = padded(far_ref)
    for place, own_ref, ref in ((1, own_k_ref, k_ref), (2, own_v_ref, v_ref)):
        rows = nn(halos[...], square_of(w_ref, place)).astype(BF16)
        ref[0, :HALO, :] = rows[:HALO]
        ref[0, HALO:right, :] = own_ref[0]
        ref[0, right:, :] = rows[HALO:]


def padded(far_ref):
    width = far_ref.shape[2]
    row = lax.broadcasted_iota(jnp.int32, (PAD, width), 0)
    far = jnp.broadcast_to(far_ref[0].astype(F32), (PAD, width))
    return jnp.where(row == 0, far, 0.0).astype(BF16)


def resident(*shape):
    return pl.BlockSpec(
        shape, lambda s: (0,) * len(shape), pipeline_mode=pl.Buffered(buffer_count=1)
    )


def project_own(x, weights):
    seqs, group, width = x.shape
    return pl.pallas_call(
        project_own_kernel,
        grid=(seqs,),
        in_specs=[by_seq(group, width), resident(*weights.shape)],
        out_specs=[by_seq(group, width)] * 3,
        out_shape=[jax.ShapeDtypeStruct(x.shape, BF16)] * 3,
        compiler_params=pltpu.CompilerParams(vmem_limit_bytes=60 << 20),
        cost_estimate=QUICK,
        name="project_own",
    )(x, weights)


def project_halos(own_keys, own_values, left, right, far, weights):
    seqs, group, width = own_keys.shape
    ext = group + 2 * HALO + PAD
    return pl.pallas_call(
        project_halos_kernel,
        grid=(seqs,),
        in_specs=[by_seq(group, width)] * 2
        + [by_seq(HALO, width), by_seq(HALO, width), by_seq(1, width), resident(*weights.shape)],
        out_specs=[by_seq(ext, width)] * 2,
        out_shape=[jax.ShapeDtypeStruct((seqs, ext, width), BF16)] * 2,
        scratch_shapes=[pltpu.VMEM((2 * HALO + PAD, width), BF16)],
        compiler_params=pltpu.CompilerParams(vmem_limit_bytes=60 << 20),
        cost_estimate=QUICK,
        name="project_halos",
    )(own_keys, own_values, left, right, far, weights)


def input_grad_kernel(
    dq_ref, dk_ref, dv_ref, first_ref, w_ref, left_ref, right_ref, far_ref, own_ref
):
    right = HALO + dq_ref.shape[1]
    grad = nt(dk_ref[0], square_of(w_ref, 1)) + nt(dv_ref[0], square_of(w_ref, 2))
    left_ref[0] = grad[:HALO].astype(BF16)
    right_ref[0] = grad[right : right + HALO].astype(BF16)
    far_ref[0] = grad[right + HALO : right + HALO + 1].astype(BF16)
    own_ref[0] = grad[HALO:right] + nt(dq_ref[0], square_of(w_ref, 0)) + first_ref[0]


def input_grads(d_queries, d_keys, d_values, d_first, weights):
    seqs, group, width = d_queries.shape
    ext = d_keys.shape[1]
    rows = (HALO, HALO)
    return pl.pallas_call(
        input_grad_kernel,
        grid=(seqs,),
        in_specs=[
            by_seq(group, width),
            by_seq(ext, width),
            by_seq(ext, width),
            by_seq(group, width),
            resident(*weights.shape),
        ],
        out_specs=[by_seq(n, width) for n in rows + (1, group)],
        out_shape=[jax.ShapeDtypeStruct((seqs, n, width), BF16) for n in rows + (1,)]
        + [jax.ShapeDtypeStruct((seqs, group, width), F32)],
        compiler_params=pltpu.CompilerParams(vmem_limit_bytes=60 << 20),
        cost_estimate=QUICK,
        name="input_grads",
    )(d_queries, d_keys, d_values, d_first, weights)


def split_cores(value, core):
    both = value.reshape((-1, 2) + value.shape[1:])
    mine, other = both[:, 0], both[:, 1]
    return jnp.where(core == 0, mine, other), jnp.where(core == 0, other, mine)


def weight_grad_kernel(
    core_ref,
    x_ref,
    left_ref,
    right_ref,
    far_ref,
    dq_ref,
    dk_ref,
    dv_ref,
    small_ref,
    mine_ref,
    other_ref,
    acc,
    rows,
    x_tail,
    dk_tail,
    dv_tail,
):
    seq = pl.program_id(0)
    core = core_ref[0]
    group, width = dq_ref.shape[1:]
    units = 2 * mine_ref.shape[0]
    part = width // units
    main = 2 * HALO + group

    @pl.when(seq == 0)
    def _():
        acc[...] = jnp.zeros_like(acc)

    rows[:HALO, :] = left_ref[0]
    rows[HALO : HALO + group, :] = x_ref[0]
    rows[HALO + group :, :] = right_ref[0]
    tail = pl.ds(pl.multiple_of(seq * PAD, PAD), PAD)
    x_tail[tail, :] = padded(far_ref)
    dk_tail[tail, :] = dk_ref[0, main:, :]
    dv_tail[tail, :] = dv_ref[0, main:, :]
    acc[0] += tn(x_ref[0], dq_ref[0])
    acc[1] += tn(rows[...], dk_ref[0, :main, :])
    acc[2] += tn(rows[...], dv_ref[0, :main, :])

    @pl.when(seq == pl.num_programs(0) - 1)
    def _():
        ends = (None, tn(x_tail[...], dk_tail[...]), tn(x_tail[...], dv_tail[...]))
        for place, end in enumerate(ends):
            total = acc[place] if end is None else acc[place] + end
            mine, other = split_cores(total.reshape(units, part, width), core)
            at = slice(place * part, (place + 1) * part)
            mine_ref[:, at, :] = mine.astype(BF16)
            other_ref[:, at, :] = other.astype(BF16)
        mine, other = split_cores(small_ref[...], core)
        mine_ref[:, 3 * part :, :] = mine.astype(BF16)
        other_ref[:, 3 * part :, :] = other.astype(BF16)


def weight_grads(core, x, left, right, far, d_queries, d_keys, d_values, small):
    seqs, group, width = d_queries.shape
    ext = d_keys.shape[1]
    units, small_rows, _ = small.shape
    shape = (units // 2, 3 * (width // units) + small_rows, width)
    tail = pltpu.VMEM((seqs * PAD, width), BF16)
    return pl.pallas_call(
        weight_grad_kernel,
        grid=(seqs,),
        in_specs=[
            pl.BlockSpec(memory_space=pltpu.SMEM),
            by_seq(group, width),
            by_seq(HALO, width),
            by_seq(HALO, width),
            by_seq(1, width),
            by_seq(group, width),
            by_seq(ext, width),
            by_seq(ext, width),
            resident(*small.shape),
        ],
        out_specs=[resident(*shape)] * 2,
        out_shape=[jax.ShapeDtypeStruct(shape, BF16)] * 2,
        scratch_shapes=[
            pltpu.VMEM((3, width, width), F32),
            pltpu.VMEM((2 * HALO + group, width), BF16),
            tail,
            tail,
            tail,
        ],
        compiler_params=pltpu.CompilerParams(vmem_limit_bytes=60 << 20),
        cost_estimate=QUICK,
        name="weight_grads",
    )(core, x, left, right, far, d_queries, d_keys, d_values, small)


def document_of(positions, lengths, seq_len):
    count = lengths.shape[1]
    order = jnp.arange(count)
    ends = jnp.sum(jnp.where(order[None, :] <= order[:, None], lengths[:, None, :], 0), axis=2)
    counted = jnp.sum((positions[None, :, None] >= ends[:, None, :]).astype(jnp.int32), axis=2)
    inside = (positions >= 0) & (positions < seq_len)
    return jnp.where(inside[None, :], counted, -1)


def masks(lengths, offset, group, seq_len):
    ext = group + 2 * HALO
    slots = ext // 4
    positions = offset - HALO + jnp.arange(ext + PAD, dtype=jnp.int32)
    doc = document_of(positions, lengths, seq_len)
    slot_doc = doc[:, 2:ext:4]
    biases = []
    for block in range(group // QB):
        near = HALO - WIN // 2 + block * QB
        far = block * QB // 4
        key_place = jnp.concatenate((jnp.arange(near, near + NEAR), 4 * jnp.arange(far, far + FAR) + 2))
        reach = jnp.concatenate((jnp.full((NEAR,), WIN // 2), jnp.full((FAR,), PWIN // 2)))
        key_doc = jnp.concatenate((doc[:, near : near + NEAR], slot_doc[:, far : far + FAR]), axis=1)
        query_place = HALO + block * QB + jnp.arange(QB)
        query_doc = doc[:, HALO + block * QB : HALO + (block + 1) * QB]
        allowed = (jnp.abs(key_place[:, None] - query_place[None, :]) <= reach[:, None])[None] & (
            key_doc[:, :, None] == query_doc[:, None, :]
        )
        biases.append(jnp.where(allowed, 0.0, MASKED).astype(F32))
    same = jnp.stack(
        [(doc[:, tap : tap + ext : 4] == slot_doc).astype(F32) for tap in range(5)], axis=1
    )
    same = jnp.broadcast_to(same[..., None], same.shape + (LANES,))
    return jnp.stack(biases, axis=1), same, slots


def steps(count):
    for k in range(1, count):
        if count & (count - 1) == 0:
            yield [(i, i ^ k) for i in range(count)], lambda me, k=k: (me ^ k, me ^ k)
        else:
            yield (
                [(i, (i + k) % count) for i in range(count)],
                lambda me, k=k: (lax.rem(me + k, count), lax.rem(me - k + count, count)),
            )


def pick(value, index, dim=0):
    return lax.dynamic_index_in_dim(value, index, dim, keepdims=False)


def gather_seq(block, *earlier):
    count, me = lax.axis_size("seq"), lax.axis_index("seq")
    zeros = (0,) * block.ndim
    came_all = after(tuple(lax.ppermute(block, "seq", pairs) for pairs, _ in steps(count)), *earlier)
    column = jnp.zeros((count,) + block.shape, block.dtype)
    column = lax.dynamic_update_slice(column, block[None], (me,) + zeros)
    for came, (_, met) in zip(came_all, steps(count)):
        column = lax.dynamic_update_slice(column, came[None], (met(me)[1],) + zeros)
    return column


def gather_yx(column):
    me = lax.axis_index("yx")
    pieces = [(column, me)]
    for pairs, met in steps(lax.axis_size("yx")):
        pieces.append((lax.ppermute(column, "yx", pairs), met(me)[1]))
    return pieces


def assemble_kernel(count, *refs):
    places, parts, whole, sems = refs[0], refs[1 : 1 + count], refs[-2], refs[-1]
    copies = [
        pltpu.make_async_copy(part, whole.at[places[i]], sems.at[i]) for i, part in enumerate(parts)
    ]
    for copy in copies:
        copy.start()
    for copy in copies:
        copy.wait()


def gather_core(pieces):
    count, me = lax.axis_size("core"), lax.axis_index("core")
    parts, places = [], []
    for piece, place in pieces:
        parts.append(piece)
        places.append(place * count + me)
        for pairs, met in steps(count):
            parts.append(lax.ppermute(piece, "core", pairs))
            places.append(place * count + met(me)[1])
    return pl.pallas_call(
        functools.partial(assemble_kernel, len(parts)),
        in_specs=[pl.BlockSpec(memory_space=pltpu.SMEM)]
        + [pl.BlockSpec(memory_space=pltpu.VMEM)] * len(parts),
        out_specs=pl.BlockSpec(memory_space=pl.ANY),
        out_shape=jax.ShapeDtypeStruct((len(parts),) + parts[0].shape, BF16),
        compiler_params=pltpu.CompilerParams(vmem_limit_bytes=60 << 20),
        scratch_shapes=[pltpu.SemaphoreType.DMA((len(parts),))],
        cost_estimate=QUICK,
        name="assemble",
    )(jnp.stack(places).astype(jnp.int32), *parts)


def after(value, *earlier):
    return lax.optimization_barrier((value, earlier))[0] if earlier else lax.optimization_barrier(value)


def exchange_sum(pieces, axis, *earlier):
    me = lax.axis_index(axis)
    came = [
        lax.ppermute(pick(pieces, met(me)[0]), axis, pairs)
        for pairs, met in steps(lax.axis_size(axis))
    ]
    total = pick(pieces, me).astype(F32)
    for part in after(came, *earlier):
        total = total + part.astype(F32)
    return total


def local(
    tokens,
    doc_lengths,
    query_weight,
    key_weight,
    value_weight,
    out_weight,
    pool_weight,
    first_gain,
    first_shift,
    inner_weight,
    inner_bias,
    outer_weight,
    outer_bias,
    second_gain,
    second_shift,
    cotangent,
):
    seq_count = lax.axis_size("seq")
    yx_count = lax.axis_size("yx")
    core_count = lax.axis_size("core")
    units = yx_count * core_count
    parts = units * seq_count
    core = lax.axis_index("core")
    seq_place = lax.axis_index("seq")
    seqs, group, width = tokens.shape
    ff = inner_weight.shape[1]
    panels = ff // width
    share = query_weight.shape[0]
    count = seqs * group

    def shift(value, by):
        pairs = [(i, i + by) for i in range(seq_count) if 0 <= i + by < seq_count]
        return lax.ppermute(value, "seq", pairs)

    early = stack(
        query_weight,
        key_weight,
        value_weight,
        pool_weight,
        (first_gain, first_shift, outer_bias, second_gain, second_shift),
        inner_bias,
    )
    late = pack(outer_weight, inner_weight, out_weight)
    bias, same, _ = masks(doc_lengths, seq_place * group, group, group * seq_count)
    early_column, bias, same = after((gather_seq(early), bias, same))
    sent = after(tokens, early_column)
    came = (
        shift(sent[:, group - HALO :], 1),
        shift(sent[:, :HALO], -1),
        shift(sent[:, :1], -2),
    )
    early_column = jnp.concatenate(
        [early_column[:, i * share : (i + 1) * share].reshape(-1, width) for i in range(3)]
        + [early_column[:, 3 * share :].reshape(-1, width)],
        axis=0,
    )
    early_pieces = gather_yx(early_column)
    early = gather_core(early_pieces)
    late_column = lax.all_gather(late, "seq", axis=0)
    late_column = after(late_column, [piece for piece, _ in early_pieces[1:]])
    outer_rows = panels * share
    late_column = jnp.concatenate(
        (
            late_column[:, :outer_rows].reshape(-1, width),
            late_column[:, outer_rows:]
            .reshape(seq_count, panels + 1, share, width)
            .swapaxes(0, 1)
            .reshape(-1, width),
        ),
        axis=0,
    )
    late = lax.all_gather(late_column, ("yx", "core"), axis=0)
    late = late.reshape(units, 2 * panels + 1, seq_count * share, width)
    small = early[:, 3 * seq_count * share :].reshape(parts, SMALL, width)
    vectors = small[:, : SMALL - 1, :share].transpose(1, 0, 2).reshape(SMALL - 1, width).astype(F32)
    taps = jnp.pad(vectors[:10], ((0, 6), (0, 0)))
    small_rows_f32 = jnp.pad(vectors[10:], ((0, 3), (0, 0)))
    bias_inner = small[:, SMALL - 1, : ff // parts].reshape(panels, 1, width).astype(F32)

    flat = tokens.reshape(count, width)

    queries, own_keys, own_values = project_own(tokens, early)
    keys, values = project_halos(own_keys, own_values, *came, early)
    mixed, lse = attention_forward(queries, keys, values, taps, same, bias)
    y, d_first, d_mixed, d_small, d_bias, d_late = feed_forward(
        flat,
        mixed.reshape(count, width),
        cotangent.reshape(count, width),
        small_rows_f32,
        bias_inner,
        late,
    )
    late_sum = lax.psum_scatter(
        d_late.reshape(-1, width), ("yx", "core"), scatter_dimension=0, tiled=True
    )
    d_queries, d_keys, d_values, d_taps = attention_backward(
        queries,
        keys,
        values,
        taps,
        same,
        bias,
        lse,
        d_mixed.reshape(seqs, group, width),
        0,
        seqs,
        (),
    )
    left, right, far, own = input_grads(
        d_queries, d_keys, d_values, d_first.reshape(seqs, group, width), early
    )
    back = (shift(left, -1), shift(right, 1), shift(far, 2))

    d_taps = jnp.sum(d_taps, axis=0)[:10]
    d_vectors = jnp.concatenate((d_taps, d_small[:5]), axis=0)
    d_vectors = d_vectors.reshape(SMALL - 1, parts, share).transpose(1, 0, 2)
    d_vectors = jnp.pad(d_vectors, ((0, 0), (0, 0), (0, width - share)))
    d_bias = jnp.pad(d_bias.reshape(parts, 1, -1), ((0, 0), (0, 0), (0, width - ff // parts)))
    d_vectors = jnp.concatenate((d_vectors, d_bias), axis=1).astype(BF16)
    d_vectors = d_vectors.reshape(units, seq_count * SMALL, width)
    mine, other = weight_grads(
        core.astype(jnp.int32).reshape(1),
        after(tokens, own),
        *came,
        d_queries,
        d_keys,
        d_values,
        d_vectors,
    )
    (mine, other), back = after(((mine, other), back))
    swapped = lax.ppermute(other, "core", [(0, 1), (1, 0)])
    early_sum = (mine.astype(F32) + swapped.astype(F32)).astype(BF16)
    outer_all = seq_count * outer_rows
    late_sum = jnp.concatenate(
        (
            late_sum[:outer_all].reshape(seq_count, outer_rows, width),
            late_sum[outer_all:]
            .reshape(panels + 1, seq_count, share, width)
            .swapaxes(0, 1)
            .reshape(seq_count, (panels + 1) * share, width),
        ),
        axis=1,
    )
    late_sum = exchange_sum(late_sum, "seq")
    early_sum = exchange_sum(early_sum, "yx", late_sum).astype(BF16)
    whole = 3 * seq_count * share
    early_sum = jnp.concatenate(
        [
            early_sum[:whole]
            .reshape(3, seq_count, share, width)
            .swapaxes(0, 1)
            .reshape(seq_count, 3 * share, width),
            early_sum[whole:].reshape(seq_count, SMALL, width),
        ],
        axis=1,
    )
    early_sum = exchange_sum(early_sum, "seq")

    edge = group - HALO
    from_right, from_left, from_far = (part.astype(F32) for part in back)
    d_input = own + jnp.pad(from_right, ((0, 0), (edge, 0), (0, 0)))
    d_input = d_input + jnp.pad(from_left, ((0, 0), (0, edge), (0, 0)))
    d_input = d_input + jnp.pad(from_far, ((0, 0), (0, group - 1), (0, 0)))

    vector_sum = early_sum[3 * share :]
    pieces = [vector_sum[10 + i, :share] for i in range(5)]
    return (
        y.reshape(seqs, group, width),
        d_input.astype(BF16),
        early_sum[:share],
        early_sum[share : 2 * share],
        early_sum[2 * share : 3 * share],
        late_sum[2 * outer_rows :],
        vector_sum[:10, :share],
        pieces[0],
        pieces[1],
        late_sum[outer_rows : 2 * outer_rows]
        .reshape(panels, share, width)
        .transpose(1, 0, 2)
        .reshape(share, ff),
        vector_sum[SMALL - 1, : ff // parts],
        late_sum[:outer_rows],
        pieces[2],
        pieces[3],
        pieces[4],
    )


def solution(mesh):
    dp, seq = mesh.devices.shape
    cores = 2 if dp % 2 == 0 else 1
    mesh = Mesh(mesh.devices.reshape(dp // cores, cores, seq), ("yx", "core", "seq"))
    every = ("yx", "core", "seq")
    rows = P(every, None)
    vector = P(every)
    whole = P(("yx", "core"), "seq", None)
    taps = P(None, every)
    weights = (rows, rows, rows, rows, taps, vector, vector, rows, vector, rows, vector, vector, vector)
    return jax.shard_map(
        local,
        mesh=mesh,
        in_specs=(whole, P(("yx", "core"), None)) + weights + (whole,),
        out_specs=(whole, whole) + weights,
        check_vma=False,
    )
```

```python
import functools

import jax
import jax.numpy as jnp
from jax import lax
from jax.experimental import pallas as pl
from jax.experimental.pallas import tpu as pltpu
from jax.sharding import Mesh
from jax.sharding import PartitionSpec as P

HEADS = 12
HEAD_DIM = 64
WIN = 128
PWIN = 512
EPS = 1e-05

LANES = 128
QB = 128
GROUP = 6
GROUP_BACK = 2
HALO = PWIN // 2
PAD = 16
NEAR = QB + WIN
FAR = (QB + PWIN) // 4
KEYS = NEAR + FAR
MASKED = -1e30
QUICK = pl.CostEstimate(flops=1 << 20, bytes_accessed=1 << 20, transcendentals=0)

F32 = jnp.float32
BF16 = jnp.bfloat16


def nt(left, right):
    return lax.dot_general(left, right, (((1,), (1,)), ((), ())), preferred_element_type=F32)


def tn(left, right):
    return lax.dot_general(left, right, (((0,), (0,)), ((), ())), preferred_element_type=F32)


def nn(left, right):
    return lax.dot_general(left, right, (((1,), (0,)), ((), ())), preferred_element_type=F32)


def slot_taps(wide, slots):
    return [wide[pl.ds(tap, slots, stride=4), :] for tap in range(5)]


def pool(taps, same_ref, w_ref, first, lanes):
    total = None
    for tap in range(5):
        term = taps[tap] * same_ref[0, tap] * w_ref[first + tap : first + tap + 1, lanes]
        total = term if total is None else total + term
    return total.astype(BF16)


def pair_stack(rows):
    lane = lax.broadcasted_iota(jnp.int32, rows.shape, 1)
    zero = jnp.zeros_like(rows)
    return jnp.concatenate(
        (jnp.where(lane < HEAD_DIM, rows, zero), jnp.where(lane < HEAD_DIM, zero, rows)), axis=0
    )


def pair_join(both):
    joined = jnp.concatenate((both[:HEAD_DIM, :QB], both[HEAD_DIM:, QB:]), axis=0)
    return joined.T


def rows_of(block):
    return slice(block * QB, (block + 1) * QB)


def keys_of(ref, pooled, block, lanes):
    near = HALO - WIN // 2 + block * QB
    far = block * QB // 4
    return jnp.concatenate((ref[0, near : near + NEAR, lanes], pooled[far : far + FAR, :]), axis=0)


def scores_of(keys, stacked, bias):
    return nt(keys, stacked) + jnp.concatenate((bias, bias), axis=1)


def attn_fwd_kernel(
    q_ref, k_ref, v_ref, w_ref, same_ref, bias_ref, out_ref, lse_ref, k_wide, v_wide, pk_ref, pv_ref
):
    slots = pk_ref.shape[1]
    scale = jnp.asarray(HEAD_DIM**-0.5, BF16)

    blocks = q_ref.shape[1] // QB

    def body(step, carry):
        jobs = []
        for lane in range(GROUP):
            pair = step * GROUP + lane
            lanes = pl.ds(pl.multiple_of(pair * LANES, LANES), LANES)
            k_wide[lane] = k_ref[0, :, lanes].astype(F32)
            v_wide[lane] = v_ref[0, :, lanes].astype(F32)
            pk_ref[lane] = pool(slot_taps(k_wide.at[lane], slots), same_ref, w_ref, 0, lanes)
            pv_ref[lane] = pool(slot_taps(v_wide.at[lane], slots), same_ref, w_ref, 5, lanes)
            jobs += [(lane, pair, lanes, block) for block in range(blocks)]
        scores = []
        for lane, pair, lanes, block in jobs:
            stacked = pair_stack(q_ref[0, rows_of(block), lanes] * scale)
            keys = keys_of(k_ref, pk_ref.at[lane], block, lanes)
            scores.append(scores_of(keys, stacked, bias_ref[0, block]))
        probs = []
        for (lane, pair, lanes, block), score in zip(jobs, scores):
            top = jnp.max(score, axis=0, keepdims=True)
            weights = jnp.exp(score - top)
            denom = jnp.sum(weights, axis=0, keepdims=True)
            probs.append((weights * (1.0 / denom)).astype(BF16))
            lse_ref[0, pair, block : block + 1, :] = top + jnp.log(denom)
        mixed = []
        for (lane, pair, lanes, block), prob in zip(jobs, probs):
            mixed.append(tn(keys_of(v_ref, pv_ref.at[lane], block, lanes), prob))
        for (lane, pair, lanes, block), value in zip(jobs, mixed):
            out_ref[0, rows_of(block), lanes] = pair_join(value).astype(BF16)
        return carry

    lax.fori_loop(0, q_ref.shape[2] // (LANES * GROUP), body, 0)


def attn_bwd_kernel(
    q_ref,
    k_ref,
    v_ref,
    w_ref,
    same_ref,
    bias_ref,
    lse_ref,
    do_ref,
    dq_ref,
    dk_ref,
    dv_ref,
    dw_ref,
    k_wide,
    v_wide,
    pk_ref,
    pv_ref,
    dpk_ref,
    dpv_ref,
):
    slots = pk_ref.shape[1]
    scale = jnp.asarray(HEAD_DIM**-0.5, BF16)
    blocks = q_ref.shape[1] // QB

    def body(step, carry):
        jobs = []
        for lane in range(GROUP_BACK):
            pair = step * GROUP_BACK + lane
            lanes = pl.ds(pl.multiple_of(pair * LANES, LANES), LANES)
            k_wide[lane] = k_ref[0, :, lanes].astype(F32)
            v_wide[lane] = v_ref[0, :, lanes].astype(F32)
            pk_ref[lane] = pool(slot_taps(k_wide.at[lane], slots), same_ref, w_ref, 0, lanes)
            pv_ref[lane] = pool(slot_taps(v_wide.at[lane], slots), same_ref, w_ref, 5, lanes)
            jobs += [(lane, pair, lanes, block) for block in range(blocks)]
        dpk_ref[...] = jnp.zeros_like(dpk_ref)
        dpv_ref[...] = jnp.zeros_like(dpv_ref)
        scores, d_probs = [], []
        for lane, pair, lanes, block in jobs:
            keys = keys_of(k_ref, pk_ref.at[lane], block, lanes)
            stacked = pair_stack(q_ref[0, rows_of(block), lanes] * scale)
            scores.append(scores_of(keys, stacked, bias_ref[0, block]))
            values = keys_of(v_ref, pv_ref.at[lane], block, lanes)
            d_probs.append(nt(values, pair_stack(do_ref[0, rows_of(block), lanes])))
        probs, d_scores = [], []
        for (lane, pair, lanes, block), score, d_prob in zip(jobs, scores, d_probs):
            prob = jnp.exp(score - lse_ref[0, pair, block : block + 1, :])
            row_dot = jnp.sum(prob * d_prob, axis=0, keepdims=True)
            d_scores.append((prob * (d_prob - row_dot)).astype(BF16))
            probs.append(prob.astype(BF16))
        parts = []
        for (lane, pair, lanes, block), prob, d_score in zip(jobs, probs, d_scores):
            d_values = nn(prob, pair_stack(do_ref[0, rows_of(block), lanes]))
            d_keys = nn(d_score, pair_stack(q_ref[0, rows_of(block), lanes] * scale))
            far = slice(block * QB // 4, block * QB // 4 + FAR)
            dpk_ref[lane, far, :] += d_keys[NEAR:]
            dpv_ref[lane, far, :] += d_values[NEAR:]
            parts.append((d_keys[:NEAR], d_values[:NEAR]))
        d_queries = []
        for (lane, pair, lanes, block), d_score in zip(jobs, d_scores):
            d_queries.append(tn(keys_of(k_ref, pk_ref.at[lane], block, lanes), d_score))
        for (lane, pair, lanes, block), value in zip(jobs, d_queries):
            dq_ref[0, rows_of(block), lanes] = (pair_join(value) * HEAD_DIM**-0.5).astype(BF16)
        for lane in range(GROUP_BACK):
            lanes = jobs[lane * blocks][2]
            for side, (wide_ref, d_pool_ref, out_ref) in enumerate(
                ((k_wide, dpk_ref, dk_ref), (v_wide, dpv_ref, dv_ref))
            ):
                wide = wide_ref.at[lane]
                d_pool = d_pool_ref[lane]
                taps = slot_taps(wide, slots)
                masked = [d_pool * same_ref[0, tap] for tap in range(5)]
                places = [5 * side + tap for tap in range(5)]
                for tap, row in enumerate(places):
                    dw_ref[0, row : row + 1, lanes] = jnp.sum(
                        masked[tap] * taps[tap], axis=0, keepdims=True
                    )
                spread = [
                    masked[tap] * w_ref[row : row + 1, lanes] for tap, row in enumerate(places)
                ]
                wide[4 * slots :, :] = jnp.zeros((wide.shape[0] - 4 * slots, LANES), F32)
                for tap in range(4):
                    wide[pl.ds(tap, slots, stride=4), :] = spread[tap]
                wide[pl.ds(4, slots, stride=4), :] += spread[4]
                for block in range(blocks):
                    near = HALO - WIN // 2 + block * QB
                    wide[near : near + NEAR, :] += parts[lane * blocks + block][side]
                out_ref[0, :, lanes] = wide[...].astype(BF16)
        return carry

    lax.fori_loop(0, q_ref.shape[2] // (LANES * GROUP_BACK), body, 0)
    dw_ref[0, 10:, :] = jnp.zeros((dw_ref.shape[1] - 10, dw_ref.shape[2]), F32)


def by_seq(*shape, first=0):
    return pl.BlockSpec((1,) + shape, lambda s: (s + first,) + (0,) * len(shape))


def attention_specs(ext, group, slots, width, first=0):
    return [
        by_seq(group, width, first=first),
        by_seq(ext, width, first=first),
        by_seq(ext, width, first=first),
        pl.BlockSpec((16, width), lambda s: (0, 0)),
        by_seq(5, slots, LANES, first=first),
        by_seq(group // QB, KEYS, LANES, first=first),
    ]


def attention_forward(queries, keys, values, taps, same, bias):
    seqs, group, width = queries.shape
    ext = keys.shape[1]
    slots = same.shape[2]
    pairs = width // LANES
    blocks = group // QB
    wide = pltpu.VMEM((GROUP, ext, LANES), F32)
    pooled = pltpu.VMEM((GROUP, slots, LANES), BF16)
    return pl.pallas_call(
        attn_fwd_kernel,
        grid=(seqs,),
        in_specs=attention_specs(ext, group, slots, width),
        out_specs=[by_seq(group, width), by_seq(pairs, blocks, 2 * QB)],
        out_shape=[
            jax.ShapeDtypeStruct((seqs, group, width), BF16),
            jax.ShapeDtypeStruct((seqs, pairs, blocks, 2 * QB), F32),
        ],
        scratch_shapes=[wide, wide, pooled, pooled],
        compiler_params=pltpu.CompilerParams(vmem_limit_bytes=60 << 20),
        cost_estimate=QUICK,
        name="attn_fwd",
    )(queries, keys, values, taps, same, bias)


def attention_backward(queries, keys, values, taps, same, bias, lse, d_mixed, first, count, earlier):
    seqs, group, width = queries.shape
    ext = keys.shape[1]
    slots = same.shape[2]
    pairs = width // LANES
    blocks = group // QB
    wide = pltpu.VMEM((GROUP_BACK, ext, LANES), F32)
    pooled = pltpu.VMEM((GROUP_BACK, slots, LANES), BF16)
    d_pooled = pltpu.VMEM((GROUP_BACK, slots, LANES), F32)
    args = (queries, keys, values, taps, same, bias, lse, d_mixed)

    def kernel(*refs):
        attn_bwd_kernel(*refs[: len(args)], *refs[len(args) + len(earlier) :])

    return pl.pallas_call(
        kernel,
        grid=(count,),
        in_specs=attention_specs(ext, group, slots, width, first)
        + [by_seq(pairs, blocks, 2 * QB, first=first), by_seq(group, width, first=first)]
        + [pl.BlockSpec(memory_space=pl.ANY)] * len(earlier),
        out_specs=[
            by_seq(*shape, first=first)
            for shape in ((group, width), (ext, width), (ext, width), (16, width))
        ],
        out_shape=[
            jax.ShapeDtypeStruct((seqs, group, width), BF16),
            jax.ShapeDtypeStruct((seqs, ext, width), BF16),
            jax.ShapeDtypeStruct((seqs, ext, width), BF16),
            jax.ShapeDtypeStruct((seqs, 16, width), F32),
        ],
        input_output_aliases={len(args) + i: i for i in range(len(earlier))},
        scratch_shapes=[wide, wide, pooled, pooled, d_pooled, d_pooled],
        compiler_params=pltpu.CompilerParams(vmem_limit_bytes=60 << 20),
        cost_estimate=QUICK,
        name="attn_bwd",
    )(*args, *earlier)


ROWS = 512
HALF_PI = 0.3989422804014327


def row_sum(value):
    return jnp.sum(value, axis=0, keepdims=True)


def row_mean(value):
    return jnp.mean(value, axis=1, keepdims=True)


def normalize(value):
    centered = value - row_mean(value)
    inv = lax.rsqrt(row_mean(centered * centered) + EPS)
    return centered * inv, inv


def normalize_back(grad, normed, inv):
    return inv * (grad - row_mean(grad) - normed * row_mean(grad * normed))


def ffn_kernel(
    panels,
    x_ref,
    mixed_ref,
    cot_ref,
    wo_ref,
    small_ref,
    bias_ref,
    w_in_ref,
    w_out_ref,
    y_ref,
    d_first_ref,
    d_mixed_ref,
    d_small_ref,
    d_bias_ref,
    d_weights_ref,
    n_one,
    inv_one,
    low,
    hidden,
    slope,
    d_inner,
    d_in_stage,
    d_out_stage,
    in_sems,
    out_sems,
):
    step = pl.program_id(0)
    tokens, width = x_ref.shape
    chunks = tokens // ROWS
    acc, d_outer = d_first_ref, d_mixed_ref
    units = d_weights_ref.shape[0]
    some = units // panels

    def in_copy(panel, slot):
        return pltpu.make_async_copy(
            d_in_stage.at[slot], d_weights_ref.at[:, :, panels + panel], in_sems.at[slot]
        )

    def out_copy(panel, slot):
        return pltpu.make_async_copy(
            d_out_stage.at[slot],
            d_weights_ref.at[pl.ds(panel * some, some), :, pl.ds(0, panels)],
            out_sems.at[slot],
        )

    def square(ref):
        return ref[...].reshape(width, width)

    gain_one, shift_one, outer_bias, gain_two, shift_two = (
        small_ref[i : i + 1, :] for i in range(5)
    )

    @pl.when(step == 0)
    def _():
        def body(i, carry):
            rows = pl.ds(pl.multiple_of(i * ROWS, ROWS), ROWS)
            first = x_ref[rows, :].astype(F32) + nn(mixed_ref[rows, :], square(wo_ref))
            normed, inv = normalize(first)
            n_one[rows, :] = normed
            inv_one[rows, :] = jnp.broadcast_to(inv, (ROWS, LANES))
            out = normed * gain_one + shift_one
            low[rows, :] = out.astype(BF16)
            acc[rows, :] = out + outer_bias
            return carry

        lax.fori_loop(0, chunks, body, 0)

    @pl.when(step < panels)
    def _():
        def body(i, carry):
            rows = pl.ds(pl.multiple_of(i * ROWS, ROWS), ROWS)
            inner = nn(low[rows, :], square(w_in_ref)) + bias_ref[0]
            cdf = 0.5 * (1.0 + lax.erf(inner * 0.7071067811865476))
            pdf = HALF_PI * jnp.exp(-0.5 * inner * inner)
            out = (inner * cdf).astype(BF16)
            hidden[step, rows, :] = out
            slope[step, rows, :] = cdf + inner * pdf
            acc[rows, :] += nn(out, square(w_out_ref))
            return carry

        lax.fori_loop(0, chunks, body, 0, unroll=True)

    @pl.when(step == panels)
    def _():
        def body(i, carry):
            d_gain, d_shift, d_bias = carry
            rows = pl.ds(pl.multiple_of(i * ROWS, ROWS), ROWS)
            normed, inv = normalize(acc[rows, :])
            y_ref[rows, :] = (normed * gain_two + shift_two).astype(BF16)
            grad = cot_ref[rows, :].astype(F32)
            d_second = normalize_back(grad * gain_two, normed, inv)
            low_grad = d_second.astype(BF16)
            acc[rows, :] = d_second
            d_outer[rows, :] = low_grad
            return (
                d_gain + row_sum(grad * normed),
                d_shift + row_sum(grad),
                d_bias + row_sum(low_grad.astype(F32)),
            )

        zero = jnp.zeros((1, width), F32)
        d_gain, d_shift, d_bias = lax.fori_loop(0, chunks, body, (zero, zero, zero))
        d_small_ref[2:3, :] = d_bias
        d_small_ref[3:4, :] = d_gain
        d_small_ref[4:5, :] = d_shift
        d_small_ref[5:, :] = jnp.zeros((3, width), F32)

    @pl.when(step >= panels)
    def _():
        panel = step - panels

        def body(i, d_bias):
            rows = pl.ds(pl.multiple_of(i * ROWS, ROWS), ROWS)
            d_hidden = nt(d_outer[rows, :], square(w_out_ref))
            grad = (d_hidden * slope[panel, rows, :]).astype(BF16)
            d_inner[rows, :] = grad
            acc[rows, :] += nt(grad, square(w_in_ref))
            return d_bias + row_sum(grad.astype(F32))

        d_bias_ref[0] = lax.fori_loop(0, chunks, body, jnp.zeros(d_bias_ref.shape[1:], F32))
        slot = lax.rem(panel, 2)

        @pl.when(panel >= 2)
        def _():
            in_copy(panel - 2, slot).wait()
            out_copy(panel - 2, slot).wait()

        d_out_stage[slot] = tn(hidden[panel], d_outer[...]).astype(BF16).reshape(d_out_stage.shape[1:])
        out_copy(panel, slot).start()
        d_in_stage[slot] = tn(low[...], d_inner[...]).astype(BF16).reshape(d_in_stage.shape[1:])
        in_copy(panel, slot).start()

    @pl.when(step == 2 * panels - 1)
    def _():
        def body(i, carry):
            d_gain, d_shift = carry
            rows = pl.ds(pl.multiple_of(i * ROWS, ROWS), ROWS)
            grad = acc[rows, :]
            normed = n_one[rows, :]
            d_first = normalize_back(grad * gain_one, normed, inv_one[rows, 0:1])
            d_first_ref[rows, :] = d_first
            low_grad = d_first.astype(BF16)
            d_inner[rows, :] = low_grad
            d_mixed_ref[rows, :] = nt(low_grad, square(wo_ref)).astype(BF16)
            return d_gain + row_sum(grad * normed), d_shift + row_sum(grad)

        zero = jnp.zeros((1, width), F32)
        d_gain, d_shift = lax.fori_loop(0, chunks, body, (zero, zero))
        d_small_ref[0:1, :] = d_gain
        d_small_ref[1:2, :] = d_shift
        slot = panels % 2
        in_copy(panels - 2, slot).wait()
        d_wo = tn(mixed_ref[...], d_inner[...])
        d_in_stage[slot] = d_wo.astype(BF16).reshape(d_in_stage.shape[1:])
        in_copy(panels, slot).start()
        out_copy(panels - 2, slot).wait()
        in_copy(panels - 1, 1 - slot).wait()
        out_copy(panels - 1, 1 - slot).wait()
        in_copy(panels, slot).wait()


def feed_forward(x, mixed, cot, small, bias, weights):
    tokens, width = x.shape
    units, column, groups, share, _ = weights.shape
    panels = groups // 2
    panel = width

    def whole(*shape):
        return pl.BlockSpec(
            shape, lambda j: (0,) * len(shape), pipeline_mode=pl.Buffered(buffer_count=1)
        )

    def later(j):
        return jnp.maximum(j - panels, 0)

    return pl.pallas_call(
        functools.partial(ffn_kernel, panels),
        grid=(2 * panels,),
        in_specs=[
            whole(tokens, width),
            whole(tokens, width),
            whole(tokens, width),
            pl.BlockSpec(
                (units, column, 1, share, width),
                lambda j: (0, 0, 2 * panels, 0, 0),
                pipeline_mode=pl.Buffered(buffer_count=1),
            ),
            whole(8, width),
            pl.BlockSpec((1, 1, panel), lambda j: (lax.rem(j, panels), 0, 0)),
            pl.BlockSpec(
                (units, column, 1, share, width), lambda j: (0, 0, panels + lax.rem(j, panels), 0, 0)
            ),
            pl.BlockSpec(
                (units // panels, column, panels, share, width),
                lambda j: (lax.rem(j, panels), 0, 0, 0, 0),
            ),
        ],
        out_specs=[
            whole(tokens, width),
            whole(tokens, width),
            whole(tokens, width),
            whole(8, width),
            pl.BlockSpec((1, 1, panel), lambda j: (later(j), 0, 0)),
            pl.BlockSpec(memory_space=pl.ANY),
        ],
        out_shape=[
            jax.ShapeDtypeStruct((tokens, width), BF16),
            jax.ShapeDtypeStruct((tokens, width), F32),
            jax.ShapeDtypeStruct((tokens, width), BF16),
            jax.ShapeDtypeStruct((8, width), F32),
            jax.ShapeDtypeStruct((panels, 1, panel), F32),
            jax.ShapeDtypeStruct(weights.shape, BF16),
        ],
        scratch_shapes=[
            pltpu.VMEM((tokens, width), F32),
            pltpu.VMEM((tokens, LANES), F32),
            pltpu.VMEM((tokens, width), BF16),
            pltpu.VMEM((panels, tokens, panel), BF16),
            pltpu.VMEM((panels, tokens, panel), F32),
            pltpu.VMEM((tokens, panel), BF16),
            pltpu.VMEM((2, units, column, share, width), BF16),
            pltpu.VMEM((2, units // panels, column, panels, share, width), BF16),
            pltpu.SemaphoreType.DMA((2,)),
            pltpu.SemaphoreType.DMA((2,)),
        ],
        compiler_params=pltpu.CompilerParams(vmem_limit_bytes=60 << 20),
        cost_estimate=QUICK,
        name="ffn",
    )(x, mixed, cot, weights, small, bias, weights, weights)


def pack_kernel(outer_ref, inner_ref, out_ref, packed_ref):
    rows, width = outer_ref.shape
    share = out_ref.shape[0]
    packed_ref[:rows, :] = outer_ref[...]
    for panel in range(inner_ref.shape[1] // width):
        at = rows + panel * share
        packed_ref[at : at + share, :] = inner_ref[:, panel * width : (panel + 1) * width]
    packed_ref[packed_ref.shape[0] - share :, :] = out_ref[...]


def pack(outer, inner, out):
    share, width = out.shape
    panels = inner.shape[1] // width
    if share % 8:
        inner = inner.reshape(share, panels, width).swapaxes(0, 1).reshape(-1, width)
        return jnp.concatenate((outer, inner, out), axis=0)
    rows = outer.shape[0] + (panels + 1) * share
    return pl.pallas_call(
        pack_kernel,
        out_shape=jax.ShapeDtypeStruct((rows, width), BF16),
        cost_estimate=QUICK,
        name="pack",
    )(outer, inner, out)


SMALL = 16


def small_block(taps, vectors, bias, width):
    share = taps.shape[1]
    rows = jnp.concatenate([taps.astype(F32)] + [v.astype(F32) for v in vectors], axis=0)
    rows = jnp.concatenate((rows, jnp.zeros((rows.shape[0], width - share), F32)), axis=1)
    bias = bias.astype(F32)
    last = jnp.concatenate((bias, jnp.zeros((1, width - bias.shape[1]), F32)), axis=1)
    return jnp.concatenate((rows, last), axis=0).astype(BF16)


def stack_kernel(q_ref, k_ref, v_ref, taps_ref, a_ref, b_ref, c_ref, d_ref, e_ref, bias_ref, out_ref):
    share, width = q_ref.shape
    for place, ref in enumerate((q_ref, k_ref, v_ref)):
        out_ref[place * share : (place + 1) * share, :] = ref[...]
    vectors = [ref[...] for ref in (a_ref, b_ref, c_ref, d_ref, e_ref)]
    out_ref[3 * share :, :] = small_block(taps_ref[...], vectors, bias_ref[...], width)


def stack(query, key, value, taps, vectors, bias):
    share, width = query.shape
    vectors = [v.reshape(1, -1) for v in vectors]
    bias = bias.reshape(1, -1)
    if share % 8:
        return jnp.concatenate((query, key, value, small_block(taps, vectors, bias, width)), axis=0)
    return pl.pallas_call(
        stack_kernel,
        out_shape=jax.ShapeDtypeStruct((3 * share + SMALL, width), BF16),
        cost_estimate=QUICK,
        name="stack",
    )(query, key, value, taps, *vectors, bias)


def square_of(w_ref, place):
    units, _, width = w_ref.shape
    part = width // units
    return w_ref[:, place * part : (place + 1) * part, :].reshape(width, width)


def project_own_kernel(x_ref, w_ref, q_ref, k_ref, v_ref):
    for place, ref in enumerate((q_ref, k_ref, v_ref)):
        ref[0] = nn(x_ref[0], square_of(w_ref, place)).astype(BF16)


def project_halos_kernel(
    own_k_ref, own_v_ref, left_ref, right_ref, far_ref, w_ref, k_ref, v_ref, halos
):
    group, width = own_k_ref.shape[1:]
    right = HALO + group
    halos[:HALO, :] = left_ref[0]
    halos[HALO : 2 * HALO, :] = right_ref[0]
    halos[2 * HALO :, :] = padded(far_ref)
    for place, own_ref, ref in ((1, own_k_ref, k_ref), (2, own_v_ref, v_ref)):
        rows = nn(halos[...], square_of(w_ref, place)).astype(BF16)
        ref[0, :HALO, :] = rows[:HALO]
        ref[0, HALO:right, :] = own_ref[0]
        ref[0, right:, :] = rows[HALO:]


def padded(far_ref):
    width = far_ref.shape[2]
    row = lax.broadcasted_iota(jnp.int32, (PAD, width), 0)
    far = jnp.broadcast_to(far_ref[0].astype(F32), (PAD, width))
    return jnp.where(row == 0, far, 0.0).astype(BF16)


def resident(*shape):
    return pl.BlockSpec(
        shape, lambda s: (0,) * len(shape), pipeline_mode=pl.Buffered(buffer_count=1)
    )


def project_own(x, weights):
    seqs, group, width = x.shape
    return pl.pallas_call(
        project_own_kernel,
        grid=(seqs,),
        in_specs=[by_seq(group, width), resident(*weights.shape)],
        out_specs=[by_seq(group, width)] * 3,
        out_shape=[jax.ShapeDtypeStruct(x.shape, BF16)] * 3,
        compiler_params=pltpu.CompilerParams(vmem_limit_bytes=60 << 20),
        cost_estimate=QUICK,
        name="project_own",
    )(x, weights)


def project_halos(own_keys, own_values, left, right, far, weights):
    seqs, group, width = own_keys.shape
    ext = group + 2 * HALO + PAD
    return pl.pallas_call(
        project_halos_kernel,
        grid=(seqs,),
        in_specs=[by_seq(group, width)] * 2
        + [by_seq(HALO, width), by_seq(HALO, width), by_seq(1, width), resident(*weights.shape)],
        out_specs=[by_seq(ext, width)] * 2,
        out_shape=[jax.ShapeDtypeStruct((seqs, ext, width), BF16)] * 2,
        scratch_shapes=[pltpu.VMEM((2 * HALO + PAD, width), BF16)],
        compiler_params=pltpu.CompilerParams(vmem_limit_bytes=60 << 20),
        cost_estimate=QUICK,
        name="project_halos",
    )(own_keys, own_values, left, right, far, weights)


def input_grad_kernel(
    dq_ref, dk_ref, dv_ref, first_ref, w_ref, left_ref, right_ref, far_ref, own_ref
):
    right = HALO + dq_ref.shape[1]
    grad = nt(dk_ref[0], square_of(w_ref, 1)) + nt(dv_ref[0], square_of(w_ref, 2))
    left_ref[0] = grad[:HALO].astype(BF16)
    right_ref[0] = grad[right : right + HALO].astype(BF16)
    far_ref[0] = grad[right + HALO : right + HALO + 1].astype(BF16)
    own_ref[0] = grad[HALO:right] + nt(dq_ref[0], square_of(w_ref, 0)) + first_ref[0]


def input_grads(d_queries, d_keys, d_values, d_first, weights):
    seqs, group, width = d_queries.shape
    ext = d_keys.shape[1]
    rows = (HALO, HALO)
    return pl.pallas_call(
        input_grad_kernel,
        grid=(seqs,),
        in_specs=[
            by_seq(group, width),
            by_seq(ext, width),
            by_seq(ext, width),
            by_seq(group, width),
            resident(*weights.shape),
        ],
        out_specs=[by_seq(n, width) for n in rows + (1, group)],
        out_shape=[jax.ShapeDtypeStruct((seqs, n, width), BF16) for n in rows + (1,)]
        + [jax.ShapeDtypeStruct((seqs, group, width), F32)],
        compiler_params=pltpu.CompilerParams(vmem_limit_bytes=60 << 20),
        cost_estimate=QUICK,
        name="input_grads",
    )(d_queries, d_keys, d_values, d_first, weights)


def split_cores(value, core):
    both = value.reshape((-1, 2) + value.shape[1:])
    mine, other = both[:, 0], both[:, 1]
    return jnp.where(core == 0, mine, other), jnp.where(core == 0, other, mine)


def weight_grad_kernel(
    core_ref,
    x_ref,
    left_ref,
    right_ref,
    far_ref,
    dq_ref,
    dk_ref,
    dv_ref,
    small_ref,
    mine_ref,
    other_ref,
    acc,
    rows,
    x_tail,
    dk_tail,
    dv_tail,
):
    seq = pl.program_id(0)
    core = core_ref[0]
    group, width = dq_ref.shape[1:]
    units = 2 * mine_ref.shape[0]
    part = width // units
    main = 2 * HALO + group

    @pl.when(seq == 0)
    def _():
        acc[...] = jnp.zeros_like(acc)

    rows[:HALO, :] = left_ref[0]
    rows[HALO : HALO + group, :] = x_ref[0]
    rows[HALO + group :, :] = right_ref[0]
    tail = pl.ds(pl.multiple_of(seq * PAD, PAD), PAD)
    x_tail[tail, :] = padded(far_ref)
    dk_tail[tail, :] = dk_ref[0, main:, :]
    dv_tail[tail, :] = dv_ref[0, main:, :]
    acc[0] += tn(x_ref[0], dq_ref[0])
    acc[1] += tn(rows[...], dk_ref[0, :main, :])
    acc[2] += tn(rows[...], dv_ref[0, :main, :])

    @pl.when(seq == pl.num_programs(0) - 1)
    def _():
        ends = (None, tn(x_tail[...], dk_tail[...]), tn(x_tail[...], dv_tail[...]))
        for place, end in enumerate(ends):
            total = acc[place] if end is None else acc[place] + end
            mine, other = split_cores(total.reshape(units, part, width), core)
            at = slice(place * part, (place + 1) * part)
            mine_ref[:, at, :] = mine.astype(BF16)
            other_ref[:, at, :] = other.astype(BF16)
        mine, other = split_cores(small_ref[...], core)
        mine_ref[:, 3 * part :, :] = mine.astype(BF16)
        other_ref[:, 3 * part :, :] = other.astype(BF16)


def weight_grads(core, x, left, right, far, d_queries, d_keys, d_values, small):
    seqs, group, width = d_queries.shape
    ext = d_keys.shape[1]
    units, small_rows, _ = small.shape
    shape = (units // 2, 3 * (width // units) + small_rows, width)
    tail = pltpu.VMEM((seqs * PAD, width), BF16)
    return pl.pallas_call(
        weight_grad_kernel,
        grid=(seqs,),
        in_specs=[
            pl.BlockSpec(memory_space=pltpu.SMEM),
            by_seq(group, width),
            by_seq(HALO, width),
            by_seq(HALO, width),
            by_seq(1, width),
            by_seq(group, width),
            by_seq(ext, width),
            by_seq(ext, width),
            resident(*small.shape),
        ],
        out_specs=[resident(*shape)] * 2,
        out_shape=[jax.ShapeDtypeStruct(shape, BF16)] * 2,
        scratch_shapes=[
            pltpu.VMEM((3, width, width), F32),
            pltpu.VMEM((2 * HALO + group, width), BF16),
            tail,
            tail,
            tail,
        ],
        compiler_params=pltpu.CompilerParams(vmem_limit_bytes=60 << 20),
        cost_estimate=QUICK,
        name="weight_grads",
    )(core, x, left, right, far, d_queries, d_keys, d_values, small)


def document_of(positions, lengths, seq_len):
    count = lengths.shape[1]
    order = jnp.arange(count)
    ends = jnp.sum(jnp.where(order[None, :] <= order[:, None], lengths[:, None, :], 0), axis=2)
    counted = jnp.sum((positions[None, :, None] >= ends[:, None, :]).astype(jnp.int32), axis=2)
    inside = (positions >= 0) & (positions < seq_len)
    return jnp.where(inside[None, :], counted, -1)


def masks(lengths, offset, group, seq_len):
    ext = group + 2 * HALO
    slots = ext // 4
    positions = offset - HALO + jnp.arange(ext + PAD, dtype=jnp.int32)
    doc = document_of(positions, lengths, seq_len)
    slot_doc = doc[:, 2:ext:4]
    biases = []
    for block in range(group // QB):
        near = HALO - WIN // 2 + block * QB
        far = block * QB // 4
        key_place = jnp.concatenate((jnp.arange(near, near + NEAR), 4 * jnp.arange(far, far + FAR) + 2))
        reach = jnp.concatenate((jnp.full((NEAR,), WIN // 2), jnp.full((FAR,), PWIN // 2)))
        key_doc = jnp.concatenate((doc[:, near : near + NEAR], slot_doc[:, far : far + FAR]), axis=1)
        query_place = HALO + block * QB + jnp.arange(QB)
        query_doc = doc[:, HALO + block * QB : HALO + (block + 1) * QB]
        allowed = (jnp.abs(key_place[:, None] - query_place[None, :]) <= reach[:, None])[None] & (
            key_doc[:, :, None] == query_doc[:, None, :]
        )
        biases.append(jnp.where(allowed, 0.0, MASKED).astype(F32))
    same = jnp.stack(
        [(doc[:, tap : tap + ext : 4] == slot_doc).astype(F32) for tap in range(5)], axis=1
    )
    same = jnp.broadcast_to(same[..., None], same.shape + (LANES,))
    return jnp.stack(biases, axis=1), same, slots


def steps(count):
    for k in range(1, count):
        if count & (count - 1) == 0:
            yield [(i, i ^ k) for i in range(count)], lambda me, k=k: (me ^ k, me ^ k)
        else:
            yield (
                [(i, (i + k) % count) for i in range(count)],
                lambda me, k=k: (lax.rem(me + k, count), lax.rem(me - k + count, count)),
            )


def pick(value, index, dim=0):
    return lax.dynamic_index_in_dim(value, index, dim, keepdims=False)


def gather_seq(block, *earlier):
    count, me = lax.axis_size("seq"), lax.axis_index("seq")
    zeros = (0,) * block.ndim
    came_all = after(tuple(lax.ppermute(block, "seq", pairs) for pairs, _ in steps(count)), *earlier)
    column = jnp.zeros((count,) + block.shape, block.dtype)
    column = lax.dynamic_update_slice(column, block[None], (me,) + zeros)
    for came, (_, met) in zip(came_all, steps(count)):
        column = lax.dynamic_update_slice(column, came[None], (met(me)[1],) + zeros)
    return column


def gather_yx(column):
    me = lax.axis_index("yx")
    pieces = [(column, me)]
    for pairs, met in steps(lax.axis_size("yx")):
        pieces.append((lax.ppermute(column, "yx", pairs), met(me)[1]))
    return pieces


def assemble_kernel(count, *refs):
    places, parts, whole, sems = refs[0], refs[1 : 1 + count], refs[-2], refs[-1]
    copies = [
        pltpu.make_async_copy(part, whole.at[places[i]], sems.at[i]) for i, part in enumerate(parts)
    ]
    for copy in copies:
        copy.start()
    for copy in copies:
        copy.wait()


def gather_core(pieces):
    count, me = lax.axis_size("core"), lax.axis_index("core")
    parts, places = [], []
    for piece, place in pieces:
        parts.append(piece)
        places.append(place * count + me)
        for pairs, met in steps(count):
            parts.append(lax.ppermute(piece, "core", pairs))
            places.append(place * count + met(me)[1])
    return pl.pallas_call(
        functools.partial(assemble_kernel, len(parts)),
        in_specs=[pl.BlockSpec(memory_space=pltpu.SMEM)]
        + [pl.BlockSpec(memory_space=pltpu.VMEM)] * len(parts),
        out_specs=pl.BlockSpec(memory_space=pl.ANY),
        out_shape=jax.ShapeDtypeStruct((len(parts),) + parts[0].shape, BF16),
        compiler_params=pltpu.CompilerParams(vmem_limit_bytes=60 << 20),
        scratch_shapes=[pltpu.SemaphoreType.DMA((len(parts),))],
        cost_estimate=QUICK,
        name="assemble",
    )(jnp.stack(places).astype(jnp.int32), *parts)


def after(value, *earlier):
    return lax.optimization_barrier((value, earlier))[0] if earlier else lax.optimization_barrier(value)


def exchange_sum(pieces, axis, *earlier):
    me = lax.axis_index(axis)
    came = [
        lax.ppermute(pick(pieces, met(me)[0]), axis, pairs)
        for pairs, met in steps(lax.axis_size(axis))
    ]
    total = pick(pieces, me).astype(F32)
    for part in after(came, *earlier):
        total = total + part.astype(F32)
    return total


def local(
    tokens,
    doc_lengths,
    query_weight,
    key_weight,
    value_weight,
    out_weight,
    pool_weight,
    first_gain,
    first_shift,
    inner_weight,
    inner_bias,
    outer_weight,
    outer_bias,
    second_gain,
    second_shift,
    cotangent,
):
    seq_count = lax.axis_size("seq")
    yx_count = lax.axis_size("yx")
    core_count = lax.axis_size("core")
    units = yx_count * core_count
    parts = units * seq_count
    core = lax.axis_index("core")
    seq_place = lax.axis_index("seq")
    seqs, group, width = tokens.shape
    ff = inner_weight.shape[1]
    panels = ff // width
    share = query_weight.shape[0]
    count = seqs * group

    def shift(value, by):
        pairs = [(i, i + by) for i in range(seq_count) if 0 <= i + by < seq_count]
        return lax.ppermute(value, "seq", pairs)

    early = stack(
        query_weight,
        key_weight,
        value_weight,
        pool_weight,
        (first_gain, first_shift, outer_bias, second_gain, second_shift),
        inner_bias,
    )
    late = pack(outer_weight, inner_weight, out_weight)
    bias, same, _ = masks(doc_lengths, seq_place * group, group, group * seq_count)
    early_column, bias, same = after((gather_seq(early), bias, same))
    sent = after(tokens, early_column)
    came = (
        shift(sent[:, group - HALO :], 1),
        shift(sent[:, :HALO], -1),
        shift(sent[:, :1], -2),
    )
    early_column = jnp.concatenate(
        [early_column[:, i * share : (i + 1) * share].reshape(-1, width) for i in range(3)]
        + [early_column[:, 3 * share :].reshape(-1, width)],
        axis=0,
    )
    early_pieces = gather_yx(early_column)
    early = gather_core(early_pieces)
    late_column = lax.all_gather(late, "seq", axis=0)
    late_column = after(late_column, [piece for piece, _ in early_pieces[1:]])
    outer_rows = panels * share
    late = lax.all_gather(late_column, ("yx", "core"), axis=0)
    late = late.reshape(units, seq_count, 2 * panels + 1, share, width)
    small = early[:, 3 * seq_count * share :].reshape(parts, SMALL, width)
    vectors = small[:, : SMALL - 1, :share].transpose(1, 0, 2).reshape(SMALL - 1, width).astype(F32)
    taps = jnp.pad(vectors[:10], ((0, 6), (0, 0)))
    small_rows_f32 = jnp.pad(vectors[10:], ((0, 3), (0, 0)))
    bias_inner = small[:, SMALL - 1, : ff // parts].reshape(panels, 1, width).astype(F32)

    flat = tokens.reshape(count, width)

    queries, own_keys, own_values = project_own(tokens, early)
    keys, values = project_halos(own_keys, own_values, *came, early)
    mixed, lse = attention_forward(queries, keys, values, taps, same, bias)
    y, d_first, d_mixed, d_small, d_bias, d_late = feed_forward(
        flat,
        mixed.reshape(count, width),
        cotangent.reshape(count, width),
        small_rows_f32,
        bias_inner,
        late,
    )
    late_sum = lax.psum_scatter(
        d_late.reshape(-1, width), ("yx", "core"), scatter_dimension=0, tiled=True
    )
    d_queries, d_keys, d_values, d_taps = attention_backward(
        queries,
        keys,
        values,
        taps,
        same,
        bias,
        lse,
        d_mixed.reshape(seqs, group, width),
        0,
        seqs,
        (),
    )
    left, right, far, own = input_grads(
        d_queries, d_keys, d_values, d_first.reshape(seqs, group, width), early
    )
    from_far = shift(far, 2)
    back = (from_far, shift(left, -1), shift(right, 1))

    d_taps = jnp.sum(d_taps, axis=0)[:10]
    d_vectors = jnp.concatenate((d_taps, d_small[:5]), axis=0)
    d_vectors = d_vectors.reshape(SMALL - 1, parts, share).transpose(1, 0, 2)
    d_vectors = jnp.pad(d_vectors, ((0, 0), (0, 0), (0, width - share)))
    d_bias = jnp.pad(d_bias.reshape(parts, 1, -1), ((0, 0), (0, 0), (0, width - ff // parts)))
    d_vectors = jnp.concatenate((d_vectors, d_bias), axis=1).astype(BF16)
    d_vectors = d_vectors.reshape(units, seq_count * SMALL, width)
    mine, other = weight_grads(
        core.astype(jnp.int32).reshape(1),
        after(tokens, own),
        *came,
        d_queries,
        d_keys,
        d_values,
        d_vectors,
    )
    (mine, other), back, late_sum = after(((mine, other), back, late_sum))
    late_sum = lax.psum_scatter(late_sum, "seq", scatter_dimension=0, tiled=True).astype(F32)
    swapped = lax.ppermute(other, "core", [(0, 1), (1, 0)])
    early_sum = (mine.astype(F32) + swapped.astype(F32)).astype(BF16)
    early_sum = exchange_sum(early_sum, "yx").astype(BF16)
    whole = 3 * seq_count * share
    early_sum = jnp.concatenate(
        [
            early_sum[:whole]
            .reshape(3, seq_count, share, width)
            .swapaxes(0, 1)
            .reshape(seq_count, 3 * share, width),
            early_sum[whole:].reshape(seq_count, SMALL, width),
        ],
        axis=1,
    )
    early_sum = exchange_sum(early_sum, "seq")

    edge = group - HALO
    from_far, from_right, from_left = (part.astype(F32) for part in back)
    d_input = own + jnp.pad(from_right, ((0, 0), (edge, 0), (0, 0)))
    d_input = d_input + jnp.pad(from_left, ((0, 0), (0, edge), (0, 0)))
    d_input = d_input + jnp.pad(from_far, ((0, 0), (0, group - 1), (0, 0)))

    vector_sum = early_sum[3 * share :]
    pieces = [vector_sum[10 + i, :share] for i in range(5)]
    return (
        y.reshape(seqs, group, width),
        d_input.astype(BF16),
        early_sum[:share],
        early_sum[share : 2 * share],
        early_sum[2 * share : 3 * share],
        late_sum[2 * outer_rows :],
        vector_sum[:10, :share],
        pieces[0],
        pieces[1],
        late_sum[outer_rows : 2 * outer_rows]
        .reshape(panels, share, width)
        .transpose(1, 0, 2)
        .reshape(share, ff),
        vector_sum[SMALL - 1, : ff // parts],
        late_sum[:outer_rows],
        pieces[2],
        pieces[3],
        pieces[4],
    )


def solution(mesh):
    dp, seq = mesh.devices.shape
    cores = 2 if dp % 2 == 0 else 1
    mesh = Mesh(mesh.devices.reshape(dp // cores, cores, seq), ("yx", "core", "seq"))
    every = ("yx", "core", "seq")
    rows = P(every, None)
    vector = P(every)
    whole = P(("yx", "core"), "seq", None)
    taps = P(None, every)
    weights = (rows, rows, rows, rows, taps, vector, vector, rows, vector, rows, vector, vector, vector)
    return jax.shard_map(
        local,
        mesh=mesh,
        in_specs=(whole, P(("yx", "core"), None)) + weights + (whole,),
        out_specs=(whole, whole) + weights,
        check_vma=False,
    )
```

```python
import functools

import jax
import jax.numpy as jnp
from jax import lax
from jax.experimental import pallas as pl
from jax.experimental.pallas import tpu as pltpu
from jax.sharding import Mesh
from jax.sharding import PartitionSpec as P

HEADS = 12
HEAD_DIM = 64
WIN = 128
PWIN = 512
EPS = 1e-05

LANES = 128
QB = 128
GROUP = 6
GROUP_BACK = 2
HALO = PWIN // 2
PAD = 16
NEAR = QB + WIN
FAR = (QB + PWIN) // 4
KEYS = NEAR + FAR
MASKED = -1e30
QUICK = pl.CostEstimate(flops=1 << 20, bytes_accessed=1 << 20, transcendentals=0)

F32 = jnp.float32
BF16 = jnp.bfloat16


def nt(left, right):
    return lax.dot_general(left, right, (((1,), (1,)), ((), ())), preferred_element_type=F32)


def tn(left, right):
    return lax.dot_general(left, right, (((0,), (0,)), ((), ())), preferred_element_type=F32)


def nn(left, right):
    return lax.dot_general(left, right, (((1,), (0,)), ((), ())), preferred_element_type=F32)


def slot_taps(wide, slots):
    return [wide[pl.ds(tap, slots, stride=4), :] for tap in range(5)]


def pool(taps, same_ref, w_ref, first, lanes):
    total = None
    for tap in range(5):
        term = taps[tap] * same_ref[0, tap] * w_ref[first + tap : first + tap + 1, lanes]
        total = term if total is None else total + term
    return total.astype(BF16)


def pair_stack(rows):
    lane = lax.broadcasted_iota(jnp.int32, rows.shape, 1)
    zero = jnp.zeros_like(rows)
    return jnp.concatenate(
        (jnp.where(lane < HEAD_DIM, rows, zero), jnp.where(lane < HEAD_DIM, zero, rows)), axis=0
    )


def pair_join(both):
    joined = jnp.concatenate((both[:HEAD_DIM, :QB], both[HEAD_DIM:, QB:]), axis=0)
    return joined.T


def rows_of(block):
    return slice(block * QB, (block + 1) * QB)


def keys_of(ref, pooled, block, lanes):
    near = HALO - WIN // 2 + block * QB
    far = block * QB // 4
    return jnp.concatenate((ref[0, near : near + NEAR, lanes], pooled[far : far + FAR, :]), axis=0)


def scores_of(keys, stacked, bias):
    return nt(keys, stacked) + jnp.concatenate((bias, bias), axis=1)


def attn_fwd_kernel(
    q_ref, k_ref, v_ref, w_ref, same_ref, bias_ref, out_ref, lse_ref, k_wide, v_wide, pk_ref, pv_ref
):
    slots = pk_ref.shape[1]
    scale = jnp.asarray(HEAD_DIM**-0.5, BF16)

    blocks = q_ref.shape[1] // QB

    def body(step, carry):
        jobs = []
        for lane in range(GROUP):
            pair = step * GROUP + lane
            lanes = pl.ds(pl.multiple_of(pair * LANES, LANES), LANES)
            k_wide[lane] = k_ref[0, :, lanes].astype(F32)
            v_wide[lane] = v_ref[0, :, lanes].astype(F32)
            pk_ref[lane] = pool(slot_taps(k_wide.at[lane], slots), same_ref, w_ref, 0, lanes)
            pv_ref[lane] = pool(slot_taps(v_wide.at[lane], slots), same_ref, w_ref, 5, lanes)
            jobs += [(lane, pair, lanes, block) for block in range(blocks)]
        scores = []
        for lane, pair, lanes, block in jobs:
            stacked = pair_stack(q_ref[0, rows_of(block), lanes] * scale)
            keys = keys_of(k_ref, pk_ref.at[lane], block, lanes)
            scores.append(scores_of(keys, stacked, bias_ref[0, block]))
        probs = []
        for (lane, pair, lanes, block), score in zip(jobs, scores):
            top = jnp.max(score, axis=0, keepdims=True)
            weights = jnp.exp(score - top)
            denom = jnp.sum(weights, axis=0, keepdims=True)
            probs.append((weights * (1.0 / denom)).astype(BF16))
            lse_ref[0, pair, block : block + 1, :] = top + jnp.log(denom)
        mixed = []
        for (lane, pair, lanes, block), prob in zip(jobs, probs):
            mixed.append(tn(keys_of(v_ref, pv_ref.at[lane], block, lanes), prob))
        for (lane, pair, lanes, block), value in zip(jobs, mixed):
            out_ref[0, rows_of(block), lanes] = pair_join(value).astype(BF16)
        return carry

    lax.fori_loop(0, q_ref.shape[2] // (LANES * GROUP), body, 0)


def attn_bwd_kernel(
    q_ref,
    k_ref,
    v_ref,
    w_ref,
    same_ref,
    bias_ref,
    lse_ref,
    do_ref,
    dq_ref,
    dk_ref,
    dv_ref,
    dw_ref,
    k_wide,
    v_wide,
    pk_ref,
    pv_ref,
    dpk_ref,
    dpv_ref,
):
    slots = pk_ref.shape[1]
    scale = jnp.asarray(HEAD_DIM**-0.5, BF16)
    blocks = q_ref.shape[1] // QB

    def body(step, carry):
        jobs = []
        for lane in range(GROUP_BACK):
            pair = step * GROUP_BACK + lane
            lanes = pl.ds(pl.multiple_of(pair * LANES, LANES), LANES)
            k_wide[lane] = k_ref[0, :, lanes].astype(F32)
            v_wide[lane] = v_ref[0, :, lanes].astype(F32)
            pk_ref[lane] = pool(slot_taps(k_wide.at[lane], slots), same_ref, w_ref, 0, lanes)
            pv_ref[lane] = pool(slot_taps(v_wide.at[lane], slots), same_ref, w_ref, 5, lanes)
            jobs += [(lane, pair, lanes, block) for block in range(blocks)]
        dpk_ref[...] = jnp.zeros_like(dpk_ref)
        dpv_ref[...] = jnp.zeros_like(dpv_ref)
        scores, d_probs = [], []
        for lane, pair, lanes, block in jobs:
            keys = keys_of(k_ref, pk_ref.at[lane], block, lanes)
            stacked = pair_stack(q_ref[0, rows_of(block), lanes] * scale)
            scores.append(scores_of(keys, stacked, bias_ref[0, block]))
            values = keys_of(v_ref, pv_ref.at[lane], block, lanes)
            d_probs.append(nt(values, pair_stack(do_ref[0, rows_of(block), lanes])))
        probs, d_scores = [], []
        for (lane, pair, lanes, block), score, d_prob in zip(jobs, scores, d_probs):
            prob = jnp.exp(score - lse_ref[0, pair, block : block + 1, :])
            row_dot = jnp.sum(prob * d_prob, axis=0, keepdims=True)
            d_scores.append((prob * (d_prob - row_dot)).astype(BF16))
            probs.append(prob.astype(BF16))
        parts = []
        for (lane, pair, lanes, block), prob, d_score in zip(jobs, probs, d_scores):
            d_values = nn(prob, pair_stack(do_ref[0, rows_of(block), lanes]))
            d_keys = nn(d_score, pair_stack(q_ref[0, rows_of(block), lanes] * scale))
            far = slice(block * QB // 4, block * QB // 4 + FAR)
            dpk_ref[lane, far, :] += d_keys[NEAR:]
            dpv_ref[lane, far, :] += d_values[NEAR:]
            parts.append((d_keys[:NEAR], d_values[:NEAR]))
        d_queries = []
        for (lane, pair, lanes, block), d_score in zip(jobs, d_scores):
            d_queries.append(tn(keys_of(k_ref, pk_ref.at[lane], block, lanes), d_score))
        for (lane, pair, lanes, block), value in zip(jobs, d_queries):
            dq_ref[0, rows_of(block), lanes] = (pair_join(value) * HEAD_DIM**-0.5).astype(BF16)
        for lane in range(GROUP_BACK):
            lanes = jobs[lane * blocks][2]
            for side, (wide_ref, d_pool_ref, out_ref) in enumerate(
                ((k_wide, dpk_ref, dk_ref), (v_wide, dpv_ref, dv_ref))
            ):
                wide = wide_ref.at[lane]
                d_pool = d_pool_ref[lane]
                taps = slot_taps(wide, slots)
                masked = [d_pool * same_ref[0, tap] for tap in range(5)]
                places = [5 * side + tap for tap in range(5)]
                for tap, row in enumerate(places):
                    dw_ref[0, row : row + 1, lanes] = jnp.sum(
                        masked[tap] * taps[tap], axis=0, keepdims=True
                    )
                spread = [
                    masked[tap] * w_ref[row : row + 1, lanes] for tap, row in enumerate(places)
                ]
                wide[4 * slots :, :] = jnp.zeros((wide.shape[0] - 4 * slots, LANES), F32)
                for tap in range(4):
                    wide[pl.ds(tap, slots, stride=4), :] = spread[tap]
                wide[pl.ds(4, slots, stride=4), :] += spread[4]
                for block in range(blocks):
                    near = HALO - WIN // 2 + block * QB
                    wide[near : near + NEAR, :] += parts[lane * blocks + block][side]
                out_ref[0, :, lanes] = wide[...].astype(BF16)
        return carry

    lax.fori_loop(0, q_ref.shape[2] // (LANES * GROUP_BACK), body, 0)
    dw_ref[0, 10:, :] = jnp.zeros((dw_ref.shape[1] - 10, dw_ref.shape[2]), F32)


def by_seq(*shape, first=0):
    return pl.BlockSpec((1,) + shape, lambda s: (s + first,) + (0,) * len(shape))


def attention_specs(ext, group, slots, width, first=0):
    return [
        by_seq(group, width, first=first),
        by_seq(ext, width, first=first),
        by_seq(ext, width, first=first),
        pl.BlockSpec((16, width), lambda s: (0, 0)),
        by_seq(5, slots, LANES, first=first),
        by_seq(group // QB, KEYS, LANES, first=first),
    ]


def attention_forward(queries, keys, values, taps, same, bias):
    seqs, group, width = queries.shape
    ext = keys.shape[1]
    slots = same.shape[2]
    pairs = width // LANES
    blocks = group // QB
    wide = pltpu.VMEM((GROUP, ext, LANES), F32)
    pooled = pltpu.VMEM((GROUP, slots, LANES), BF16)
    return pl.pallas_call(
        attn_fwd_kernel,
        grid=(seqs,),
        in_specs=attention_specs(ext, group, slots, width),
        out_specs=[by_seq(group, width), by_seq(pairs, blocks, 2 * QB)],
        out_shape=[
            jax.ShapeDtypeStruct((seqs, group, width), BF16),
            jax.ShapeDtypeStruct((seqs, pairs, blocks, 2 * QB), F32),
        ],
        scratch_shapes=[wide, wide, pooled, pooled],
        compiler_params=pltpu.CompilerParams(vmem_limit_bytes=60 << 20),
        cost_estimate=QUICK,
        name="attn_fwd",
    )(queries, keys, values, taps, same, bias)


def attention_backward(queries, keys, values, taps, same, bias, lse, d_mixed, first, count, earlier):
    seqs, group, width = queries.shape
    ext = keys.shape[1]
    slots = same.shape[2]
    pairs = width // LANES
    blocks = group // QB
    wide = pltpu.VMEM((GROUP_BACK, ext, LANES), F32)
    pooled = pltpu.VMEM((GROUP_BACK, slots, LANES), BF16)
    d_pooled = pltpu.VMEM((GROUP_BACK, slots, LANES), F32)
    args = (queries, keys, values, taps, same, bias, lse, d_mixed)

    def kernel(*refs):
        attn_bwd_kernel(*refs[: len(args)], *refs[len(args) + len(earlier) :])

    return pl.pallas_call(
        kernel,
        grid=(count,),
        in_specs=attention_specs(ext, group, slots, width, first)
        + [by_seq(pairs, blocks, 2 * QB, first=first), by_seq(group, width, first=first)]
        + [pl.BlockSpec(memory_space=pl.ANY)] * len(earlier),
        out_specs=[
            by_seq(*shape, first=first)
            for shape in ((group, width), (ext, width), (ext, width), (16, width))
        ],
        out_shape=[
            jax.ShapeDtypeStruct((seqs, group, width), BF16),
            jax.ShapeDtypeStruct((seqs, ext, width), BF16),
            jax.ShapeDtypeStruct((seqs, ext, width), BF16),
            jax.ShapeDtypeStruct((seqs, 16, width), F32),
        ],
        input_output_aliases={len(args) + i: i for i in range(len(earlier))},
        scratch_shapes=[wide, wide, pooled, pooled, d_pooled, d_pooled],
        compiler_params=pltpu.CompilerParams(vmem_limit_bytes=60 << 20),
        cost_estimate=QUICK,
        name="attn_bwd",
    )(*args, *earlier)


ROWS = 512
HALF_PI = 0.3989422804014327


def row_sum(value):
    return jnp.sum(value, axis=0, keepdims=True)


def row_mean(value):
    return jnp.mean(value, axis=1, keepdims=True)


def normalize(value):
    centered = value - row_mean(value)
    inv = lax.rsqrt(row_mean(centered * centered) + EPS)
    return centered * inv, inv


def normalize_back(grad, normed, inv):
    return inv * (grad - row_mean(grad) - normed * row_mean(grad * normed))


def ffn_kernel(
    panels,
    x_ref,
    mixed_ref,
    cot_ref,
    wo_ref,
    small_ref,
    bias_ref,
    w_in_ref,
    w_out_ref,
    y_ref,
    d_first_ref,
    d_mixed_ref,
    d_small_ref,
    d_bias_ref,
    d_weights_ref,
    n_one,
    inv_one,
    low,
    hidden,
    slope,
    d_inner,
    d_in_stage,
    d_out_stage,
    in_sems,
    out_sems,
):
    step = pl.program_id(0)
    tokens, width = x_ref.shape
    chunks = tokens // ROWS
    acc, d_outer = d_first_ref, d_mixed_ref
    units = d_weights_ref.shape[0]
    some = units // panels

    def in_copy(panel, slot):
        return pltpu.make_async_copy(
            d_in_stage.at[slot], d_weights_ref.at[:, :, panels + panel], in_sems.at[slot]
        )

    def out_copy(panel, slot):
        return pltpu.make_async_copy(
            d_out_stage.at[slot],
            d_weights_ref.at[pl.ds(panel * some, some), :, pl.ds(0, panels)],
            out_sems.at[slot],
        )

    def square(ref):
        return ref[...].reshape(width, width)

    gain_one, shift_one, outer_bias, gain_two, shift_two = (
        small_ref[i : i + 1, :] for i in range(5)
    )

    @pl.when(step == 0)
    def _():
        def body(i, carry):
            rows = pl.ds(pl.multiple_of(i * ROWS, ROWS), ROWS)
            first = x_ref[rows, :].astype(F32) + nn(mixed_ref[rows, :], square(wo_ref))
            normed, inv = normalize(first)
            n_one[rows, :] = normed
            inv_one[rows, :] = jnp.broadcast_to(inv, (ROWS, LANES))
            out = normed * gain_one + shift_one
            low[rows, :] = out.astype(BF16)
            acc[rows, :] = out + outer_bias
            return carry

        lax.fori_loop(0, chunks, body, 0)

    @pl.when(step < panels)
    def _():
        def body(i, carry):
            rows = pl.ds(pl.multiple_of(i * ROWS, ROWS), ROWS)
            inner = nn(low[rows, :], square(w_in_ref)) + bias_ref[0]
            cdf = 0.5 * (1.0 + lax.erf(inner * 0.7071067811865476))
            pdf = HALF_PI * jnp.exp(-0.5 * inner * inner)
            out = (inner * cdf).astype(BF16)
            hidden[step, rows, :] = out
            slope[step, rows, :] = cdf + inner * pdf
            acc[rows, :] += nn(out, square(w_out_ref))
            return carry

        lax.fori_loop(0, chunks, body, 0, unroll=True)

    @pl.when(step == panels)
    def _():
        def body(i, carry):
            d_gain, d_shift, d_bias = carry
            rows = pl.ds(pl.multiple_of(i * ROWS, ROWS), ROWS)
            normed, inv = normalize(acc[rows, :])
            y_ref[rows, :] = (normed * gain_two + shift_two).astype(BF16)
            grad = cot_ref[rows, :].astype(F32)
            d_second = normalize_back(grad * gain_two, normed, inv)
            low_grad = d_second.astype(BF16)
            acc[rows, :] = d_second
            d_outer[rows, :] = low_grad
            return (
                d_gain + row_sum(grad * normed),
                d_shift + row_sum(grad),
                d_bias + row_sum(low_grad.astype(F32)),
            )

        zero = jnp.zeros((1, width), F32)
        d_gain, d_shift, d_bias = lax.fori_loop(0, chunks, body, (zero, zero, zero))
        d_small_ref[2:3, :] = d_bias
        d_small_ref[3:4, :] = d_gain
        d_small_ref[4:5, :] = d_shift
        d_small_ref[5:, :] = jnp.zeros((3, width), F32)

    @pl.when(step >= panels)
    def _():
        panel = step - panels

        def body(i, d_bias):
            rows = pl.ds(pl.multiple_of(i * ROWS, ROWS), ROWS)
            d_hidden = nt(d_outer[rows, :], square(w_out_ref))
            grad = (d_hidden * slope[panel, rows, :]).astype(BF16)
            d_inner[rows, :] = grad
            acc[rows, :] += nt(grad, square(w_in_ref))
            return d_bias + row_sum(grad.astype(F32))

        d_bias_ref[0] = lax.fori_loop(0, chunks, body, jnp.zeros(d_bias_ref.shape[1:], F32))
        slot = lax.rem(panel, 2)

        @pl.when(panel >= 2)
        def _():
            in_copy(panel - 2, slot).wait()
            out_copy(panel - 2, slot).wait()

        d_out_stage[slot] = tn(hidden[panel], d_outer[...]).astype(BF16).reshape(d_out_stage.shape[1:])
        out_copy(panel, slot).start()
        d_in_stage[slot] = tn(low[...], d_inner[...]).astype(BF16).reshape(d_in_stage.shape[1:])
        in_copy(panel, slot).start()

    @pl.when(step == 2 * panels - 1)
    def _():
        def body(i, carry):
            d_gain, d_shift = carry
            rows = pl.ds(pl.multiple_of(i * ROWS, ROWS), ROWS)
            grad = acc[rows, :]
            normed = n_one[rows, :]
            d_first = normalize_back(grad * gain_one, normed, inv_one[rows, 0:1])
            d_first_ref[rows, :] = d_first
            low_grad = d_first.astype(BF16)
            d_inner[rows, :] = low_grad
            d_mixed_ref[rows, :] = nt(low_grad, square(wo_ref)).astype(BF16)
            return d_gain + row_sum(grad * normed), d_shift + row_sum(grad)

        zero = jnp.zeros((1, width), F32)
        d_gain, d_shift = lax.fori_loop(0, chunks, body, (zero, zero))
        d_small_ref[0:1, :] = d_gain
        d_small_ref[1:2, :] = d_shift
        slot = panels % 2
        in_copy(panels - 2, slot).wait()
        d_wo = tn(mixed_ref[...], d_inner[...])
        d_in_stage[slot] = d_wo.astype(BF16).reshape(d_in_stage.shape[1:])
        in_copy(panels, slot).start()
        out_copy(panels - 2, slot).wait()
        in_copy(panels - 1, 1 - slot).wait()
        out_copy(panels - 1, 1 - slot).wait()
        in_copy(panels, slot).wait()


def feed_forward(x, mixed, cot, small, bias, weights):
    tokens, width = x.shape
    units, column, groups, share, _ = weights.shape
    panels = groups // 2
    panel = width

    def whole(*shape):
        return pl.BlockSpec(
            shape, lambda j: (0,) * len(shape), pipeline_mode=pl.Buffered(buffer_count=1)
        )

    def later(j):
        return jnp.maximum(j - panels, 0)

    return pl.pallas_call(
        functools.partial(ffn_kernel, panels),
        grid=(2 * panels,),
        in_specs=[
            whole(tokens, width),
            whole(tokens, width),
            whole(tokens, width),
            pl.BlockSpec(
                (units, column, 1, share, width),
                lambda j: (0, 0, 2 * panels, 0, 0),
                pipeline_mode=pl.Buffered(buffer_count=1),
            ),
            whole(8, width),
            pl.BlockSpec((1, 1, panel), lambda j: (lax.rem(j, panels), 0, 0)),
            pl.BlockSpec(
                (units, column, 1, share, width), lambda j: (0, 0, panels + lax.rem(j, panels), 0, 0)
            ),
            pl.BlockSpec(
                (units // panels, column, panels, share, width),
                lambda j: (lax.rem(j, panels), 0, 0, 0, 0),
            ),
        ],
        out_specs=[
            whole(tokens, width),
            whole(tokens, width),
            whole(tokens, width),
            whole(8, width),
            pl.BlockSpec((1, 1, panel), lambda j: (later(j), 0, 0)),
            pl.BlockSpec(memory_space=pl.ANY),
        ],
        out_shape=[
            jax.ShapeDtypeStruct((tokens, width), BF16),
            jax.ShapeDtypeStruct((tokens, width), F32),
            jax.ShapeDtypeStruct((tokens, width), BF16),
            jax.ShapeDtypeStruct((8, width), F32),
            jax.ShapeDtypeStruct((panels, 1, panel), F32),
            jax.ShapeDtypeStruct(weights.shape, BF16),
        ],
        scratch_shapes=[
            pltpu.VMEM((tokens, width), F32),
            pltpu.VMEM((tokens, LANES), F32),
            pltpu.VMEM((tokens, width), BF16),
            pltpu.VMEM((panels, tokens, panel), BF16),
            pltpu.VMEM((panels, tokens, panel), F32),
            pltpu.VMEM((tokens, panel), BF16),
            pltpu.VMEM((2, units, column, share, width), BF16),
            pltpu.VMEM((2, units // panels, column, panels, share, width), BF16),
            pltpu.SemaphoreType.DMA((2,)),
            pltpu.SemaphoreType.DMA((2,)),
        ],
        compiler_params=pltpu.CompilerParams(vmem_limit_bytes=60 << 20),
        cost_estimate=QUICK,
        name="ffn",
    )(x, mixed, cot, weights, small, bias, weights, weights)


def pack_kernel(outer_ref, inner_ref, out_ref, packed_ref):
    rows, width = outer_ref.shape
    share = out_ref.shape[0]
    packed_ref[:rows, :] = outer_ref[...]
    for panel in range(inner_ref.shape[1] // width):
        at = rows + panel * share
        packed_ref[at : at + share, :] = inner_ref[:, panel * width : (panel + 1) * width]
    packed_ref[packed_ref.shape[0] - share :, :] = out_ref[...]


def pack(outer, inner, out):
    share, width = out.shape
    panels = inner.shape[1] // width
    if share % 8:
        inner = inner.reshape(share, panels, width).swapaxes(0, 1).reshape(-1, width)
        return jnp.concatenate((outer, inner, out), axis=0)
    rows = outer.shape[0] + (panels + 1) * share
    return pl.pallas_call(
        pack_kernel,
        out_shape=jax.ShapeDtypeStruct((rows, width), BF16),
        cost_estimate=QUICK,
        name="pack",
    )(outer, inner, out)


SMALL = 16


def small_block(taps, vectors, bias, width):
    share = taps.shape[1]
    rows = jnp.concatenate([taps.astype(F32)] + [v.astype(F32) for v in vectors], axis=0)
    rows = jnp.concatenate((rows, jnp.zeros((rows.shape[0], width - share), F32)), axis=1)
    bias = bias.astype(F32)
    last = jnp.concatenate((bias, jnp.zeros((1, width - bias.shape[1]), F32)), axis=1)
    return jnp.concatenate((rows, last), axis=0).astype(BF16)


def stack_kernel(q_ref, k_ref, v_ref, taps_ref, a_ref, b_ref, c_ref, d_ref, e_ref, bias_ref, out_ref):
    share, width = q_ref.shape
    for place, ref in enumerate((q_ref, k_ref, v_ref)):
        out_ref[place * share : (place + 1) * share, :] = ref[...]
    vectors = [ref[...] for ref in (a_ref, b_ref, c_ref, d_ref, e_ref)]
    out_ref[3 * share :, :] = small_block(taps_ref[...], vectors, bias_ref[...], width)


def stack(query, key, value, taps, vectors, bias):
    share, width = query.shape
    vectors = [v.reshape(1, -1) for v in vectors]
    bias = bias.reshape(1, -1)
    if share % 8:
        return jnp.concatenate((query, key, value, small_block(taps, vectors, bias, width)), axis=0)
    return pl.pallas_call(
        stack_kernel,
        out_shape=jax.ShapeDtypeStruct((3 * share + SMALL, width), BF16),
        cost_estimate=QUICK,
        name="stack",
    )(query, key, value, taps, *vectors, bias)


def square_of(w_ref, place):
    units, _, width = w_ref.shape
    part = width // units
    return w_ref[:, place * part : (place + 1) * part, :].reshape(width, width)


def project_own_kernel(x_ref, w_ref, q_ref, k_ref, v_ref):
    for place, ref in enumerate((q_ref, k_ref, v_ref)):
        ref[0] = nn(x_ref[0], square_of(w_ref, place)).astype(BF16)


def project_halos_kernel(
    own_k_ref, own_v_ref, left_ref, right_ref, far_ref, w_ref, k_ref, v_ref, halos
):
    group, width = own_k_ref.shape[1:]
    right = HALO + group
    halos[:HALO, :] = left_ref[0]
    halos[HALO : 2 * HALO, :] = right_ref[0]
    halos[2 * HALO :, :] = padded(far_ref)
    for place, own_ref, ref in ((1, own_k_ref, k_ref), (2, own_v_ref, v_ref)):
        rows = nn(halos[...], square_of(w_ref, place)).astype(BF16)
        ref[0, :HALO, :] = rows[:HALO]
        ref[0, HALO:right, :] = own_ref[0]
        ref[0, right:, :] = rows[HALO:]


def padded(far_ref):
    width = far_ref.shape[2]
    row = lax.broadcasted_iota(jnp.int32, (PAD, width), 0)
    far = jnp.broadcast_to(far_ref[0].astype(F32), (PAD, width))
    return jnp.where(row == 0, far, 0.0).astype(BF16)


def resident(*shape):
    return pl.BlockSpec(
        shape, lambda s: (0,) * len(shape), pipeline_mode=pl.Buffered(buffer_count=1)
    )


def project_own(x, weights):
    seqs, group, width = x.shape
    return pl.pallas_call(
        project_own_kernel,
        grid=(seqs,),
        in_specs=[by_seq(group, width), resident(*weights.shape)],
        out_specs=[by_seq(group, width)] * 3,
        out_shape=[jax.ShapeDtypeStruct(x.shape, BF16)] * 3,
        compiler_params=pltpu.CompilerParams(vmem_limit_bytes=60 << 20),
        cost_estimate=QUICK,
        name="project_own",
    )(x, weights)


def project_halos(own_keys, own_values, left, right, far, weights):
    seqs, group, width = own_keys.shape
    ext = group + 2 * HALO + PAD
    return pl.pallas_call(
        project_halos_kernel,
        grid=(seqs,),
        in_specs=[by_seq(group, width)] * 2
        + [by_seq(HALO, width), by_seq(HALO, width), by_seq(1, width), resident(*weights.shape)],
        out_specs=[by_seq(ext, width)] * 2,
        out_shape=[jax.ShapeDtypeStruct((seqs, ext, width), BF16)] * 2,
        scratch_shapes=[pltpu.VMEM((2 * HALO + PAD, width), BF16)],
        compiler_params=pltpu.CompilerParams(vmem_limit_bytes=60 << 20),
        cost_estimate=QUICK,
        name="project_halos",
    )(own_keys, own_values, left, right, far, weights)


def halo_grad_kernel(dk_ref, dv_ref, wk_ref, wv_ref, left_ref, right_ref, far_ref, dk, dv):
    right = dk_ref.shape[1] - HALO - PAD
    width = dk_ref.shape[2]
    for rows, ref in ((dk, dk_ref), (dv, dv_ref)):
        rows[:HALO, :] = ref[0, :HALO, :]
        rows[HALO:, :] = ref[0, right:, :]
    grad = nt(dk[...], wk_ref[...].reshape(width, width)) + nt(
        dv[...], wv_ref[...].reshape(width, width)
    )
    left_ref[0] = grad[:HALO].astype(BF16)
    right_ref[0] = grad[HALO : 2 * HALO].astype(BF16)
    far_ref[0] = grad[2 * HALO : 2 * HALO + 1].astype(BF16)


def halo_grads(d_keys, d_values, weights):
    seqs, ext, width = d_keys.shape
    units = weights.shape[0]

    def part(place):
        return pl.BlockSpec(
            (units, width // units, width),
            lambda s: (0, place, 0),
            pipeline_mode=pl.Buffered(buffer_count=1),
        )

    rows = (HALO, HALO, 1)
    kept = pltpu.VMEM((2 * HALO + PAD, width), BF16)
    return pl.pallas_call(
        halo_grad_kernel,
        grid=(seqs,),
        in_specs=[by_seq(ext, width), by_seq(ext, width), part(1), part(2)],
        out_specs=[by_seq(n, width) for n in rows],
        out_shape=[jax.ShapeDtypeStruct((seqs, n, width), BF16) for n in rows],
        scratch_shapes=[kept, kept],
        compiler_params=pltpu.CompilerParams(vmem_limit_bytes=60 << 20),
        cost_estimate=QUICK,
        name="halo_grads",
    )(d_keys, d_values, weights, weights)


def own_grad_kernel(dq_ref, dk_ref, dv_ref, first_ref, w_ref, own_ref):
    grad = nt(dq_ref[0], square_of(w_ref, 0)) + nt(dk_ref[0], square_of(w_ref, 1))
    own_ref[0] = grad + nt(dv_ref[0], square_of(w_ref, 2)) + first_ref[0]


def own_grads(d_queries, d_keys, d_values, d_first, weights):
    seqs, group, width = d_queries.shape
    middle = pl.BlockSpec((1, group, width), lambda s: (s, HALO // group, 0))
    return pl.pallas_call(
        own_grad_kernel,
        grid=(seqs,),
        in_specs=[
            by_seq(group, width),
            middle,
            middle,
            by_seq(group, width),
            resident(*weights.shape),
        ],
        out_specs=by_seq(group, width),
        out_shape=jax.ShapeDtypeStruct((seqs, group, width), F32),
        compiler_params=pltpu.CompilerParams(vmem_limit_bytes=60 << 20),
        cost_estimate=QUICK,
        name="own_grads",
    )(d_queries, d_keys, d_values, d_first, weights)


def split_cores(value, core):
    both = value.reshape((-1, 2) + value.shape[1:])
    mine, other = both[:, 0], both[:, 1]
    return jnp.where(core == 0, mine, other), jnp.where(core == 0, other, mine)


def weight_grad_kernel(
    core_ref,
    x_ref,
    left_ref,
    right_ref,
    far_ref,
    dq_ref,
    dk_ref,
    dv_ref,
    small_ref,
    mine_ref,
    other_ref,
    acc,
    rows,
    x_tail,
    dk_tail,
    dv_tail,
):
    seq = pl.program_id(0)
    core = core_ref[0]
    group, width = dq_ref.shape[1:]
    units = 2 * mine_ref.shape[0]
    part = width // units
    main = 2 * HALO + group

    @pl.when(seq == 0)
    def _():
        acc[...] = jnp.zeros_like(acc)

    rows[:HALO, :] = left_ref[0]
    rows[HALO : HALO + group, :] = x_ref[0]
    rows[HALO + group :, :] = right_ref[0]
    tail = pl.ds(pl.multiple_of(seq * PAD, PAD), PAD)
    x_tail[tail, :] = padded(far_ref)
    dk_tail[tail, :] = dk_ref[0, main:, :]
    dv_tail[tail, :] = dv_ref[0, main:, :]
    acc[0] += tn(x_ref[0], dq_ref[0])
    acc[1] += tn(rows[...], dk_ref[0, :main, :])
    acc[2] += tn(rows[...], dv_ref[0, :main, :])

    @pl.when(seq == pl.num_programs(0) - 1)
    def _():
        ends = (None, tn(x_tail[...], dk_tail[...]), tn(x_tail[...], dv_tail[...]))
        for place, end in enumerate(ends):
            total = acc[place] if end is None else acc[place] + end
            mine, other = split_cores(total.reshape(units, part, width), core)
            at = slice(place * part, (place + 1) * part)
            mine_ref[:, at, :] = mine.astype(BF16)
            other_ref[:, at, :] = other.astype(BF16)
        mine, other = split_cores(small_ref[...], core)
        mine_ref[:, 3 * part :, :] = mine.astype(BF16)
        other_ref[:, 3 * part :, :] = other.astype(BF16)


def weight_grads(core, x, left, right, far, d_queries, d_keys, d_values, small):
    seqs, group, width = d_queries.shape
    ext = d_keys.shape[1]
    units, small_rows, _ = small.shape
    shape = (units // 2, 3 * (width // units) + small_rows, width)
    tail = pltpu.VMEM((seqs * PAD, width), BF16)
    return pl.pallas_call(
        weight_grad_kernel,
        grid=(seqs,),
        in_specs=[
            pl.BlockSpec(memory_space=pltpu.SMEM),
            by_seq(group, width),
            by_seq(HALO, width),
            by_seq(HALO, width),
            by_seq(1, width),
            by_seq(group, width),
            by_seq(ext, width),
            by_seq(ext, width),
            resident(*small.shape),
        ],
        out_specs=[resident(*shape)] * 2,
        out_shape=[jax.ShapeDtypeStruct(shape, BF16)] * 2,
        scratch_shapes=[
            pltpu.VMEM((3, width, width), F32),
            pltpu.VMEM((2 * HALO + group, width), BF16),
            tail,
            tail,
            tail,
        ],
        compiler_params=pltpu.CompilerParams(vmem_limit_bytes=60 << 20),
        cost_estimate=QUICK,
        name="weight_grads",
    )(core, x, left, right, far, d_queries, d_keys, d_values, small)


def document_of(positions, lengths, seq_len):
    count = lengths.shape[1]
    order = jnp.arange(count)
    ends = jnp.sum(jnp.where(order[None, :] <= order[:, None], lengths[:, None, :], 0), axis=2)
    counted = jnp.sum((positions[None, :, None] >= ends[:, None, :]).astype(jnp.int32), axis=2)
    inside = (positions >= 0) & (positions < seq_len)
    return jnp.where(inside[None, :], counted, -1)


def masks(lengths, offset, group, seq_len):
    ext = group + 2 * HALO
    slots = ext // 4
    positions = offset - HALO + jnp.arange(ext + PAD, dtype=jnp.int32)
    doc = document_of(positions, lengths, seq_len)
    slot_doc = doc[:, 2:ext:4]
    biases = []
    for block in range(group // QB):
        near = HALO - WIN // 2 + block * QB
        far = block * QB // 4
        key_place = jnp.concatenate((jnp.arange(near, near + NEAR), 4 * jnp.arange(far, far + FAR) + 2))
        reach = jnp.concatenate((jnp.full((NEAR,), WIN // 2), jnp.full((FAR,), PWIN // 2)))
        key_doc = jnp.concatenate((doc[:, near : near + NEAR], slot_doc[:, far : far + FAR]), axis=1)
        query_place = HALO + block * QB + jnp.arange(QB)
        query_doc = doc[:, HALO + block * QB : HALO + (block + 1) * QB]
        allowed = (jnp.abs(key_place[:, None] - query_place[None, :]) <= reach[:, None])[None] & (
            key_doc[:, :, None] == query_doc[:, None, :]
        )
        biases.append(jnp.where(allowed, 0.0, MASKED).astype(F32))
    same = jnp.stack(
        [(doc[:, tap : tap + ext : 4] == slot_doc).astype(F32) for tap in range(5)], axis=1
    )
    same = jnp.broadcast_to(same[..., None], same.shape + (LANES,))
    return jnp.stack(biases, axis=1), same, slots


def steps(count):
    for k in range(1, count):
        if count & (count - 1) == 0:
            yield [(i, i ^ k) for i in range(count)], lambda me, k=k: (me ^ k, me ^ k)
        else:
            yield (
                [(i, (i + k) % count) for i in range(count)],
                lambda me, k=k: (lax.rem(me + k, count), lax.rem(me - k + count, count)),
            )


def pick(value, index, dim=0):
    return lax.dynamic_index_in_dim(value, index, dim, keepdims=False)


def gather_seq(block, *earlier):
    count, me = lax.axis_size("seq"), lax.axis_index("seq")
    zeros = (0,) * block.ndim
    came_all = after(tuple(lax.ppermute(block, "seq", pairs) for pairs, _ in steps(count)), *earlier)
    column = jnp.zeros((count,) + block.shape, block.dtype)
    column = lax.dynamic_update_slice(column, block[None], (me,) + zeros)
    for came, (_, met) in zip(came_all, steps(count)):
        column = lax.dynamic_update_slice(column, came[None], (met(me)[1],) + zeros)
    return column


def gather_yx(column):
    me = lax.axis_index("yx")
    pieces = [(column, me)]
    for pairs, met in steps(lax.axis_size("yx")):
        pieces.append((lax.ppermute(column, "yx", pairs), met(me)[1]))
    return pieces


def assemble_kernel(count, *refs):
    places, parts, whole, sems = refs[0], refs[1 : 1 + count], refs[-2], refs[-1]
    copies = [
        pltpu.make_async_copy(part, whole.at[places[i]], sems.at[i]) for i, part in enumerate(parts)
    ]
    for copy in copies:
        copy.start()
    for copy in copies:
        copy.wait()


def gather_core(pieces):
    count, me = lax.axis_size("core"), lax.axis_index("core")
    parts, places = [], []
    for piece, place in pieces:
        parts.append(piece)
        places.append(place * count + me)
        for pairs, met in steps(count):
            parts.append(lax.ppermute(piece, "core", pairs))
            places.append(place * count + met(me)[1])
    return pl.pallas_call(
        functools.partial(assemble_kernel, len(parts)),
        in_specs=[pl.BlockSpec(memory_space=pltpu.SMEM)]
        + [pl.BlockSpec(memory_space=pltpu.VMEM)] * len(parts),
        out_specs=pl.BlockSpec(memory_space=pl.ANY),
        out_shape=jax.ShapeDtypeStruct((len(parts),) + parts[0].shape, BF16),
        compiler_params=pltpu.CompilerParams(vmem_limit_bytes=60 << 20),
        scratch_shapes=[pltpu.SemaphoreType.DMA((len(parts),))],
        cost_estimate=QUICK,
        name="assemble",
    )(jnp.stack(places).astype(jnp.int32), *parts)


def after(value, *earlier):
    return lax.optimization_barrier((value, earlier))[0] if earlier else lax.optimization_barrier(value)


def exchange_sum(pieces, axis, *earlier):
    me = lax.axis_index(axis)
    came = [
        lax.ppermute(pick(pieces, met(me)[0]), axis, pairs)
        for pairs, met in steps(lax.axis_size(axis))
    ]
    total = pick(pieces, me).astype(F32)
    for part in after(came, *earlier):
        total = total + part.astype(F32)
    return total


def local(
    tokens,
    doc_lengths,
    query_weight,
    key_weight,
    value_weight,
    out_weight,
    pool_weight,
    first_gain,
    first_shift,
    inner_weight,
    inner_bias,
    outer_weight,
    outer_bias,
    second_gain,
    second_shift,
    cotangent,
):
    seq_count = lax.axis_size("seq")
    yx_count = lax.axis_size("yx")
    core_count = lax.axis_size("core")
    units = yx_count * core_count
    parts = units * seq_count
    core = lax.axis_index("core")
    seq_place = lax.axis_index("seq")
    seqs, group, width = tokens.shape
    ff = inner_weight.shape[1]
    panels = ff // width
    share = query_weight.shape[0]
    count = seqs * group

    def shift(value, by):
        pairs = [(i, i + by) for i in range(seq_count) if 0 <= i + by < seq_count]
        return lax.ppermute(value, "seq", pairs)

    early = stack(
        query_weight,
        key_weight,
        value_weight,
        pool_weight,
        (first_gain, first_shift, outer_bias, second_gain, second_shift),
        inner_bias,
    )
    late = pack(outer_weight, inner_weight, out_weight)
    bias, same, _ = masks(doc_lengths, seq_place * group, group, group * seq_count)
    early_column, bias, same = after((gather_seq(early), bias, same))
    sent = after(tokens, early_column)
    came = (
        shift(sent[:, group - HALO :], 1),
        shift(sent[:, :HALO], -1),
        shift(sent[:, :1], -2),
    )
    early_column = jnp.concatenate(
        [early_column[:, i * share : (i + 1) * share].reshape(-1, width) for i in range(3)]
        + [early_column[:, 3 * share :].reshape(-1, width)],
        axis=0,
    )
    early_pieces = gather_yx(early_column)
    early = gather_core(early_pieces)
    late_column = lax.all_gather(late, "seq", axis=0)
    late_column = after(late_column, [piece for piece, _ in early_pieces[1:]])
    outer_rows = panels * share
    late = lax.all_gather(late_column, ("yx", "core"), axis=0)
    late = late.reshape(units, seq_count, 2 * panels + 1, share, width)
    small = early[:, 3 * seq_count * share :].reshape(parts, SMALL, width)
    vectors = small[:, : SMALL - 1, :share].transpose(1, 0, 2).reshape(SMALL - 1, width).astype(F32)
    taps = jnp.pad(vectors[:10], ((0, 6), (0, 0)))
    small_rows_f32 = jnp.pad(vectors[10:], ((0, 3), (0, 0)))
    bias_inner = small[:, SMALL - 1, : ff // parts].reshape(panels, 1, width).astype(F32)

    flat = tokens.reshape(count, width)

    queries, own_keys, own_values = project_own(tokens, early)
    keys, values = project_halos(own_keys, own_values, *came, early)
    mixed, lse = attention_forward(queries, keys, values, taps, same, bias)
    y, d_first, d_mixed, d_small, d_bias, d_late = feed_forward(
        flat,
        mixed.reshape(count, width),
        cotangent.reshape(count, width),
        small_rows_f32,
        bias_inner,
        late,
    )
    late_sum = lax.psum_scatter(
        d_late.reshape(-1, width), ("yx", "core"), scatter_dimension=0, tiled=True
    )
    d_queries, d_keys, d_values, d_taps = attention_backward(
        queries,
        keys,
        values,
        taps,
        same,
        bias,
        lse,
        d_mixed.reshape(seqs, group, width),
        0,
        seqs,
        (),
    )
    left, right, far = halo_grads(d_keys, d_values, early)
    from_far = shift(far, 2)
    back = (from_far, shift(left, -1), shift(right, 1))

    d_taps = jnp.sum(d_taps, axis=0)[:10]
    d_vectors = jnp.concatenate((d_taps, d_small[:5]), axis=0)
    d_vectors = d_vectors.reshape(SMALL - 1, parts, share).transpose(1, 0, 2)
    d_vectors = jnp.pad(d_vectors, ((0, 0), (0, 0), (0, width - share)))
    d_bias = jnp.pad(d_bias.reshape(parts, 1, -1), ((0, 0), (0, 0), (0, width - ff // parts)))
    d_vectors = jnp.concatenate((d_vectors, d_bias), axis=1).astype(BF16)
    d_vectors = d_vectors.reshape(units, seq_count * SMALL, width)
    mine, other = weight_grads(
        core.astype(jnp.int32).reshape(1),
        after(tokens, left),
        *came,
        d_queries,
        d_keys,
        d_values,
        d_vectors,
    )
    own = own_grads(
        d_queries,
        *after((d_keys, d_values), mine),
        d_first.reshape(seqs, group, width),
        early,
    )
    (mine, other), back, late_sum, own = after(((mine, other), back, late_sum, own))
    late_sum = lax.psum_scatter(late_sum, "seq", scatter_dimension=0, tiled=True).astype(F32)
    swapped = lax.ppermute(other, "core", [(0, 1), (1, 0)])
    early_sum = (mine.astype(F32) + swapped.astype(F32)).astype(BF16)
    early_sum = exchange_sum(early_sum, "yx").astype(BF16)
    whole = 3 * seq_count * share
    early_sum = jnp.concatenate(
        [
            early_sum[:whole]
            .reshape(3, seq_count, share, width)
            .swapaxes(0, 1)
            .reshape(seq_count, 3 * share, width),
            early_sum[whole:].reshape(seq_count, SMALL, width),
        ],
        axis=1,
    )
    early_sum = exchange_sum(early_sum, "seq")

    edge = group - HALO
    from_far, from_right, from_left = (part.astype(F32) for part in back)
    d_input = own + jnp.pad(from_right, ((0, 0), (edge, 0), (0, 0)))
    d_input = d_input + jnp.pad(from_left, ((0, 0), (0, edge), (0, 0)))
    d_input = d_input + jnp.pad(from_far, ((0, 0), (0, group - 1), (0, 0)))

    vector_sum = early_sum[3 * share :]
    pieces = [vector_sum[10 + i, :share] for i in range(5)]
    return (
        y.reshape(seqs, group, width),
        d_input.astype(BF16),
        early_sum[:share],
        early_sum[share : 2 * share],
        early_sum[2 * share : 3 * share],
        late_sum[2 * outer_rows :],
        vector_sum[:10, :share],
        pieces[0],
        pieces[1],
        late_sum[outer_rows : 2 * outer_rows]
        .reshape(panels, share, width)
        .transpose(1, 0, 2)
        .reshape(share, ff),
        vector_sum[SMALL - 1, : ff // parts],
        late_sum[:outer_rows],
        pieces[2],
        pieces[3],
        pieces[4],
    )


def solution(mesh):
    dp, seq = mesh.devices.shape
    cores = 2 if dp % 2 == 0 else 1
    mesh = Mesh(mesh.devices.reshape(dp // cores, cores, seq), ("yx", "core", "seq"))
    every = ("yx", "core", "seq")
    rows = P(every, None)
    vector = P(every)
    whole = P(("yx", "core"), "seq", None)
    taps = P(None, every)
    weights = (rows, rows, rows, rows, taps, vector, vector, rows, vector, rows, vector, vector, vector)
    return jax.shard_map(
        local,
        mesh=mesh,
        in_specs=(whole, P(("yx", "core"), None)) + weights + (whole,),
        out_specs=(whole, whole) + weights,
        check_vma=False,
    )
```

```python
import functools

import jax
import jax.numpy as jnp
from jax import lax
from jax.experimental import pallas as pl
from jax.experimental.pallas import tpu as pltpu
from jax.sharding import Mesh
from jax.sharding import PartitionSpec as P

HEADS = 12
HEAD_DIM = 64
WIN = 128
PWIN = 512
EPS = 1e-05

LANES = 128
QB = 128
GROUP = 6
GROUP_BACK = 2
HALO = PWIN // 2
PAD = 16
NEAR = QB + WIN
FAR = (QB + PWIN) // 4
KEYS = NEAR + FAR
MASKED = -1e30
QUICK = pl.CostEstimate(flops=1 << 20, bytes_accessed=1 << 20, transcendentals=0)

F32 = jnp.float32
BF16 = jnp.bfloat16


def nt(left, right):
    return lax.dot_general(left, right, (((1,), (1,)), ((), ())), preferred_element_type=F32)


def tn(left, right):
    return lax.dot_general(left, right, (((0,), (0,)), ((), ())), preferred_element_type=F32)


def nn(left, right):
    return lax.dot_general(left, right, (((1,), (0,)), ((), ())), preferred_element_type=F32)


def slot_taps(wide, slots):
    return [wide[pl.ds(tap, slots, stride=4), :] for tap in range(5)]


def pool(taps, same_ref, w_ref, first, lanes):
    total = None
    for tap in range(5):
        term = taps[tap] * same_ref[0, tap] * w_ref[first + tap : first + tap + 1, lanes]
        total = term if total is None else total + term
    return total.astype(BF16)


def pair_stack(rows):
    lane = lax.broadcasted_iota(jnp.int32, rows.shape, 1)
    zero = jnp.zeros_like(rows)
    return jnp.concatenate(
        (jnp.where(lane < HEAD_DIM, rows, zero), jnp.where(lane < HEAD_DIM, zero, rows)), axis=0
    )


def pair_join(both):
    joined = jnp.concatenate((both[:HEAD_DIM, :QB], both[HEAD_DIM:, QB:]), axis=0)
    return joined.T


def rows_of(block):
    return slice(block * QB, (block + 1) * QB)


def keys_of(ref, pooled, block, lanes):
    near = HALO - WIN // 2 + block * QB
    far = block * QB // 4
    return jnp.concatenate((ref[0, near : near + NEAR, lanes], pooled[far : far + FAR, :]), axis=0)


def scores_of(keys, stacked, bias):
    return nt(keys, stacked) + jnp.concatenate((bias, bias), axis=1)


def attn_fwd_kernel(
    q_ref, k_ref, v_ref, w_ref, same_ref, bias_ref, out_ref, lse_ref, k_wide, v_wide, pk_ref, pv_ref
):
    slots = pk_ref.shape[1]
    scale = jnp.asarray(HEAD_DIM**-0.5, BF16)

    blocks = q_ref.shape[1] // QB

    def body(step, carry):
        jobs = []
        for lane in range(GROUP):
            pair = step * GROUP + lane
            lanes = pl.ds(pl.multiple_of(pair * LANES, LANES), LANES)
            k_wide[lane] = k_ref[0, :, lanes].astype(F32)
            v_wide[lane] = v_ref[0, :, lanes].astype(F32)
            pk_ref[lane] = pool(slot_taps(k_wide.at[lane], slots), same_ref, w_ref, 0, lanes)
            pv_ref[lane] = pool(slot_taps(v_wide.at[lane], slots), same_ref, w_ref, 5, lanes)
            jobs += [(lane, pair, lanes, block) for block in range(blocks)]
        scores = []
        for lane, pair, lanes, block in jobs:
            stacked = pair_stack(q_ref[0, rows_of(block), lanes] * scale)
            keys = keys_of(k_ref, pk_ref.at[lane], block, lanes)
            scores.append(scores_of(keys, stacked, bias_ref[0, block]))
        probs = []
        for (lane, pair, lanes, block), score in zip(jobs, scores):
            top = jnp.max(score, axis=0, keepdims=True)
            weights = jnp.exp(score - top)
            denom = jnp.sum(weights, axis=0, keepdims=True)
            probs.append((weights * (1.0 / denom)).astype(BF16))
            lse_ref[0, pair, block : block + 1, :] = top + jnp.log(denom)
        mixed = []
        for (lane, pair, lanes, block), prob in zip(jobs, probs):
            mixed.append(tn(keys_of(v_ref, pv_ref.at[lane], block, lanes), prob))
        for (lane, pair, lanes, block), value in zip(jobs, mixed):
            out_ref[0, rows_of(block), lanes] = pair_join(value).astype(BF16)
        return carry

    lax.fori_loop(0, q_ref.shape[2] // (LANES * GROUP), body, 0)


def attn_bwd_kernel(
    q_ref,
    k_ref,
    v_ref,
    w_ref,
    same_ref,
    bias_ref,
    lse_ref,
    do_ref,
    dq_ref,
    dk_ref,
    dv_ref,
    dw_ref,
    k_wide,
    v_wide,
    pk_ref,
    pv_ref,
    dpk_ref,
    dpv_ref,
):
    slots = pk_ref.shape[1]
    scale = jnp.asarray(HEAD_DIM**-0.5, BF16)
    blocks = q_ref.shape[1] // QB

    def body(step, carry):
        jobs = []
        for lane in range(GROUP_BACK):
            pair = step * GROUP_BACK + lane
            lanes = pl.ds(pl.multiple_of(pair * LANES, LANES), LANES)
            k_wide[lane] = k_ref[0, :, lanes].astype(F32)
            v_wide[lane] = v_ref[0, :, lanes].astype(F32)
            pk_ref[lane] = pool(slot_taps(k_wide.at[lane], slots), same_ref, w_ref, 0, lanes)
            pv_ref[lane] = pool(slot_taps(v_wide.at[lane], slots), same_ref, w_ref, 5, lanes)
            jobs += [(lane, pair, lanes, block) for block in range(blocks)]
        dpk_ref[...] = jnp.zeros_like(dpk_ref)
        dpv_ref[...] = jnp.zeros_like(dpv_ref)
        scores, d_probs = [], []
        for lane, pair, lanes, block in jobs:
            keys = keys_of(k_ref, pk_ref.at[lane], block, lanes)
            stacked = pair_stack(q_ref[0, rows_of(block), lanes] * scale)
            scores.append(scores_of(keys, stacked, bias_ref[0, block]))
            values = keys_of(v_ref, pv_ref.at[lane], block, lanes)
            d_probs.append(nt(values, pair_stack(do_ref[0, rows_of(block), lanes])))
        probs, d_scores = [], []
        for (lane, pair, lanes, block), score, d_prob in zip(jobs, scores, d_probs):
            prob = jnp.exp(score - lse_ref[0, pair, block : block + 1, :])
            row_dot = jnp.sum(prob * d_prob, axis=0, keepdims=True)
            d_scores.append((prob * (d_prob - row_dot)).astype(BF16))
            probs.append(prob.astype(BF16))
        parts = []
        for (lane, pair, lanes, block), prob, d_score in zip(jobs, probs, d_scores):
            d_values = nn(prob, pair_stack(do_ref[0, rows_of(block), lanes]))
            d_keys = nn(d_score, pair_stack(q_ref[0, rows_of(block), lanes] * scale))
            far = slice(block * QB // 4, block * QB // 4 + FAR)
            dpk_ref[lane, far, :] += d_keys[NEAR:]
            dpv_ref[lane, far, :] += d_values[NEAR:]
            parts.append((d_keys[:NEAR], d_values[:NEAR]))
        d_queries = []
        for (lane, pair, lanes, block), d_score in zip(jobs, d_scores):
            d_queries.append(tn(keys_of(k_ref, pk_ref.at[lane], block, lanes), d_score))
        for (lane, pair, lanes, block), value in zip(jobs, d_queries):
            dq_ref[0, rows_of(block), lanes] = (pair_join(value) * HEAD_DIM**-0.5).astype(BF16)
        for lane in range(GROUP_BACK):
            lanes = jobs[lane * blocks][2]
            for side, (wide_ref, d_pool_ref, out_ref) in enumerate(
                ((k_wide, dpk_ref, dk_ref), (v_wide, dpv_ref, dv_ref))
            ):
                wide = wide_ref.at[lane]
                d_pool = d_pool_ref[lane]
                taps = slot_taps(wide, slots)
                masked = [d_pool * same_ref[0, tap] for tap in range(5)]
                places = [5 * side + tap for tap in range(5)]
                for tap, row in enumerate(places):
                    dw_ref[0, row : row + 1, lanes] = jnp.sum(
                        masked[tap] * taps[tap], axis=0, keepdims=True
                    )
                spread = [
                    masked[tap] * w_ref[row : row + 1, lanes] for tap, row in enumerate(places)
                ]
                wide[4 * slots :, :] = jnp.zeros((wide.shape[0] - 4 * slots, LANES), F32)
                for tap in range(4):
                    wide[pl.ds(tap, slots, stride=4), :] = spread[tap]
                wide[pl.ds(4, slots, stride=4), :] += spread[4]
                for block in range(blocks):
                    near = HALO - WIN // 2 + block * QB
                    wide[near : near + NEAR, :] += parts[lane * blocks + block][side]
                out_ref[0, :, lanes] = wide[...].astype(BF16)
        return carry

    lax.fori_loop(0, q_ref.shape[2] // (LANES * GROUP_BACK), body, 0)
    dw_ref[0, 10:, :] = jnp.zeros((dw_ref.shape[1] - 10, dw_ref.shape[2]), F32)


def by_seq(*shape, first=0):
    return pl.BlockSpec((1,) + shape, lambda s: (s + first,) + (0,) * len(shape))


def attention_specs(ext, group, slots, width, first=0):
    return [
        by_seq(group, width, first=first),
        by_seq(ext, width, first=first),
        by_seq(ext, width, first=first),
        pl.BlockSpec((16, width), lambda s: (0, 0)),
        by_seq(5, slots, LANES, first=first),
        by_seq(group // QB, KEYS, LANES, first=first),
    ]


def attention_forward(queries, keys, values, taps, same, bias):
    seqs, group, width = queries.shape
    ext = keys.shape[1]
    slots = same.shape[2]
    pairs = width // LANES
    blocks = group // QB
    wide = pltpu.VMEM((GROUP, ext, LANES), F32)
    pooled = pltpu.VMEM((GROUP, slots, LANES), BF16)
    return pl.pallas_call(
        attn_fwd_kernel,
        grid=(seqs,),
        in_specs=attention_specs(ext, group, slots, width),
        out_specs=[by_seq(group, width), by_seq(pairs, blocks, 2 * QB)],
        out_shape=[
            jax.ShapeDtypeStruct((seqs, group, width), BF16),
            jax.ShapeDtypeStruct((seqs, pairs, blocks, 2 * QB), F32),
        ],
        scratch_shapes=[wide, wide, pooled, pooled],
        compiler_params=pltpu.CompilerParams(vmem_limit_bytes=60 << 20),
        cost_estimate=QUICK,
        name="attn_fwd",
    )(queries, keys, values, taps, same, bias)


def attention_backward(queries, keys, values, taps, same, bias, lse, d_mixed, first, count, earlier):
    seqs, group, width = queries.shape
    ext = keys.shape[1]
    slots = same.shape[2]
    pairs = width // LANES
    blocks = group // QB
    wide = pltpu.VMEM((GROUP_BACK, ext, LANES), F32)
    pooled = pltpu.VMEM((GROUP_BACK, slots, LANES), BF16)
    d_pooled = pltpu.VMEM((GROUP_BACK, slots, LANES), F32)
    args = (queries, keys, values, taps, same, bias, lse, d_mixed)

    def kernel(*refs):
        attn_bwd_kernel(*refs[: len(args)], *refs[len(args) + len(earlier) :])

    return pl.pallas_call(
        kernel,
        grid=(count,),
        in_specs=attention_specs(ext, group, slots, width, first)
        + [by_seq(pairs, blocks, 2 * QB, first=first), by_seq(group, width, first=first)]
        + [pl.BlockSpec(memory_space=pl.ANY)] * len(earlier),
        out_specs=[
            by_seq(*shape, first=first)
            for shape in ((group, width), (ext, width), (ext, width), (16, width))
        ],
        out_shape=[
            jax.ShapeDtypeStruct((seqs, group, width), BF16),
            jax.ShapeDtypeStruct((seqs, ext, width), BF16),
            jax.ShapeDtypeStruct((seqs, ext, width), BF16),
            jax.ShapeDtypeStruct((seqs, 16, width), F32),
        ],
        input_output_aliases={len(args) + i: i for i in range(len(earlier))},
        scratch_shapes=[wide, wide, pooled, pooled, d_pooled, d_pooled],
        compiler_params=pltpu.CompilerParams(vmem_limit_bytes=60 << 20),
        cost_estimate=QUICK,
        name="attn_bwd",
    )(*args, *earlier)


ROWS = 512
HALF_PI = 0.3989422804014327


def row_sum(value):
    return jnp.sum(value, axis=0, keepdims=True)


def row_mean(value):
    return jnp.mean(value, axis=1, keepdims=True)


def normalize(value):
    centered = value - row_mean(value)
    inv = lax.rsqrt(row_mean(centered * centered) + EPS)
    return centered * inv, inv


def normalize_back(grad, normed, inv):
    return inv * (grad - row_mean(grad) - normed * row_mean(grad * normed))


def ffn_kernel(
    panels,
    x_ref,
    mixed_ref,
    cot_ref,
    wo_ref,
    small_ref,
    bias_ref,
    w_in_ref,
    w_out_ref,
    y_ref,
    d_first_ref,
    d_mixed_ref,
    d_small_ref,
    d_bias_ref,
    d_weights_ref,
    n_one,
    inv_one,
    low,
    hidden,
    slope,
    d_inner,
    cot,
    y_all,
    d_in_stage,
    d_out_stage,
    in_sems,
    out_sems,
):
    step = pl.program_id(0)
    tokens, width = x_ref.shape
    chunks = tokens // ROWS
    acc, d_outer = d_first_ref, d_mixed_ref
    units = d_weights_ref.shape[0]
    some = units // panels

    def in_copy(panel, slot):
        return pltpu.make_async_copy(
            d_in_stage.at[slot], d_weights_ref.at[:, :, panels + panel], in_sems.at[slot]
        )

    def out_copy(panel, slot):
        return pltpu.make_async_copy(
            d_out_stage.at[slot],
            d_weights_ref.at[pl.ds(panel * some, some), :, pl.ds(0, panels)],
            out_sems.at[slot],
        )

    def square(ref):
        return ref[...].reshape(width, width)

    gain_one, shift_one, outer_bias, gain_two, shift_two = (
        small_ref[i : i + 1, :] for i in range(5)
    )

    piece = cot_ref.shape[0]
    piece_rows = pl.ds(pl.multiple_of(lax.rem(step, panels) * piece, piece), piece)

    @pl.when(step < panels)
    def _():
        cot[piece_rows, :] = cot_ref[...]

    @pl.when(step == 0)
    def _():
        def body(i, carry):
            rows = pl.ds(pl.multiple_of(i * ROWS, ROWS), ROWS)
            first = x_ref[rows, :].astype(F32) + nn(mixed_ref[rows, :], square(wo_ref))
            normed, inv = normalize(first)
            n_one[rows, :] = normed
            inv_one[rows, :] = jnp.broadcast_to(inv, (ROWS, LANES))
            out = normed * gain_one + shift_one
            low[rows, :] = out.astype(BF16)
            acc[rows, :] = out + outer_bias
            return carry

        lax.fori_loop(0, chunks, body, 0)

    @pl.when(step < panels)
    def _():
        def body(i, carry):
            rows = pl.ds(pl.multiple_of(i * ROWS, ROWS), ROWS)
            inner = nn(low[rows, :], square(w_in_ref)) + bias_ref[0]
            cdf = 0.5 * (1.0 + lax.erf(inner * 0.7071067811865476))
            pdf = HALF_PI * jnp.exp(-0.5 * inner * inner)
            out = (inner * cdf).astype(BF16)
            hidden[step, rows, :] = out
            slope[step, rows, :] = cdf + inner * pdf
            acc[rows, :] += nn(out, square(w_out_ref))
            return carry

        lax.fori_loop(0, chunks, body, 0, unroll=True)

    @pl.when(step == panels)
    def _():
        def body(i, carry):
            d_gain, d_shift, d_bias = carry
            rows = pl.ds(pl.multiple_of(i * ROWS, ROWS), ROWS)
            normed, inv = normalize(acc[rows, :])
            y_all[rows, :] = (normed * gain_two + shift_two).astype(BF16)
            grad = cot[rows, :].astype(F32)
            d_second = normalize_back(grad * gain_two, normed, inv)
            low_grad = d_second.astype(BF16)
            acc[rows, :] = d_second
            d_outer[rows, :] = low_grad
            return (
                d_gain + row_sum(grad * normed),
                d_shift + row_sum(grad),
                d_bias + row_sum(low_grad.astype(F32)),
            )

        zero = jnp.zeros((1, width), F32)
        d_gain, d_shift, d_bias = lax.fori_loop(0, chunks, body, (zero, zero, zero))
        d_small_ref[2:3, :] = d_bias
        d_small_ref[3:4, :] = d_gain
        d_small_ref[4:5, :] = d_shift
        d_small_ref[5:, :] = jnp.zeros((3, width), F32)

    @pl.when(step >= panels)
    def _():
        panel = step - panels
        y_ref[...] = y_all[piece_rows, :]

        def body(i, d_bias):
            rows = pl.ds(pl.multiple_of(i * ROWS, ROWS), ROWS)
            d_hidden = nt(d_outer[rows, :], square(w_out_ref))
            grad = (d_hidden * slope[panel, rows, :]).astype(BF16)
            d_inner[rows, :] = grad
            acc[rows, :] += nt(grad, square(w_in_ref))
            return d_bias + row_sum(grad.astype(F32))

        d_bias_ref[0] = lax.fori_loop(0, chunks, body, jnp.zeros(d_bias_ref.shape[1:], F32))
        slot = lax.rem(panel, 2)

        @pl.when(panel >= 2)
        def _():
            in_copy(panel - 2, slot).wait()
            out_copy(panel - 2, slot).wait()

        d_out_stage[slot] = tn(hidden[panel], d_outer[...]).astype(BF16).reshape(d_out_stage.shape[1:])
        out_copy(panel, slot).start()
        d_in_stage[slot] = tn(low[...], d_inner[...]).astype(BF16).reshape(d_in_stage.shape[1:])
        in_copy(panel, slot).start()

    @pl.when(step == 2 * panels - 1)
    def _():
        def body(i, carry):
            d_gain, d_shift = carry
            rows = pl.ds(pl.multiple_of(i * ROWS, ROWS), ROWS)
            grad = acc[rows, :]
            normed = n_one[rows, :]
            d_first = normalize_back(grad * gain_one, normed, inv_one[rows, 0:1])
            d_first_ref[rows, :] = d_first
            low_grad = d_first.astype(BF16)
            d_inner[rows, :] = low_grad
            d_mixed_ref[rows, :] = nt(low_grad, square(wo_ref)).astype(BF16)
            return d_gain + row_sum(grad * normed), d_shift + row_sum(grad)

        zero = jnp.zeros((1, width), F32)
        d_gain, d_shift = lax.fori_loop(0, chunks, body, (zero, zero))
        d_small_ref[0:1, :] = d_gain
        d_small_ref[1:2, :] = d_shift
        slot = panels % 2
        in_copy(panels - 2, slot).wait()
        d_wo = tn(mixed_ref[...], d_inner[...])
        d_in_stage[slot] = d_wo.astype(BF16).reshape(d_in_stage.shape[1:])
        in_copy(panels, slot).start()
        out_copy(panels - 2, slot).wait()
        in_copy(panels - 1, 1 - slot).wait()
        out_copy(panels - 1, 1 - slot).wait()
        in_copy(panels, slot).wait()


def feed_forward(x, mixed, cot, small, bias, weights):
    tokens, width = x.shape
    units, column, groups, share, _ = weights.shape
    panels = groups // 2
    panel = width

    def whole(*shape):
        return pl.BlockSpec(
            shape, lambda j: (0,) * len(shape), pipeline_mode=pl.Buffered(buffer_count=1)
        )

    def later(j):
        return jnp.maximum(j - panels, 0)

    return pl.pallas_call(
        functools.partial(ffn_kernel, panels),
        grid=(2 * panels,),
        in_specs=[
            whole(tokens, width),
            whole(tokens, width),
            pl.BlockSpec((tokens // panels, width), lambda j: (jnp.minimum(j, panels - 1), 0)),
            pl.BlockSpec(
                (units, column, 1, share, width),
                lambda j: (0, 0, 2 * panels, 0, 0),
                pipeline_mode=pl.Buffered(buffer_count=1),
            ),
            whole(8, width),
            pl.BlockSpec((1, 1, panel), lambda j: (lax.rem(j, panels), 0, 0)),
            pl.BlockSpec(
                (units, column, 1, share, width), lambda j: (0, 0, panels + lax.rem(j, panels), 0, 0)
            ),
            pl.BlockSpec(
                (units // panels, column, panels, share, width),
                lambda j: (lax.rem(j, panels), 0, 0, 0, 0),
            ),
        ],
        out_specs=[
            pl.BlockSpec((tokens // panels, width), lambda j: (later(j), 0)),
            whole(tokens, width),
            whole(tokens, width),
            whole(8, width),
            pl.BlockSpec((1, 1, panel), lambda j: (later(j), 0, 0)),
            pl.BlockSpec(memory_space=pl.ANY),
        ],
        out_shape=[
            jax.ShapeDtypeStruct((tokens, width), BF16),
            jax.ShapeDtypeStruct((tokens, width), F32),
            jax.ShapeDtypeStruct((tokens, width), BF16),
            jax.ShapeDtypeStruct((8, width), F32),
            jax.ShapeDtypeStruct((panels, 1, panel), F32),
            jax.ShapeDtypeStruct(weights.shape, BF16),
        ],
        scratch_shapes=[
            pltpu.VMEM((tokens, width), F32),
            pltpu.VMEM((tokens, LANES), F32),
            pltpu.VMEM((tokens, width), BF16),
            pltpu.VMEM((panels, tokens, panel), BF16),
            pltpu.VMEM((panels, tokens, panel), F32),
            pltpu.VMEM((tokens, panel), BF16),
            pltpu.VMEM((tokens, width), BF16),
            pltpu.VMEM((tokens, width), BF16),
            pltpu.VMEM((2, units, column, share, width), BF16),
            pltpu.VMEM((2, units // panels, column, panels, share, width), BF16),
            pltpu.SemaphoreType.DMA((2,)),
            pltpu.SemaphoreType.DMA((2,)),
        ],
        compiler_params=pltpu.CompilerParams(vmem_limit_bytes=60 << 20),
        cost_estimate=QUICK,
        name="ffn",
    )(x, mixed, cot, weights, small, bias, weights, weights)


def pack_kernel(outer_ref, inner_ref, out_ref, packed_ref):
    rows, width = outer_ref.shape
    share = out_ref.shape[0]
    packed_ref[:rows, :] = outer_ref[...]
    for panel in range(inner_ref.shape[1] // width):
        at = rows + panel * share
        packed_ref[at : at + share, :] = inner_ref[:, panel * width : (panel + 1) * width]
    packed_ref[packed_ref.shape[0] - share :, :] = out_ref[...]


def pack(outer, inner, out):
    share, width = out.shape
    panels = inner.shape[1] // width
    if share % 8:
        inner = inner.reshape(share, panels, width).swapaxes(0, 1).reshape(-1, width)
        return jnp.concatenate((outer, inner, out), axis=0)
    rows = outer.shape[0] + (panels + 1) * share
    return pl.pallas_call(
        pack_kernel,
        out_shape=jax.ShapeDtypeStruct((rows, width), BF16),
        cost_estimate=QUICK,
        name="pack",
    )(outer, inner, out)


SMALL = 16


def small_block(taps, vectors, bias, width):
    share = taps.shape[1]
    rows = jnp.concatenate([taps.astype(F32)] + [v.astype(F32) for v in vectors], axis=0)
    rows = jnp.concatenate((rows, jnp.zeros((rows.shape[0], width - share), F32)), axis=1)
    bias = bias.astype(F32)
    last = jnp.concatenate((bias, jnp.zeros((1, width - bias.shape[1]), F32)), axis=1)
    return jnp.concatenate((rows, last), axis=0).astype(BF16)


def stack_kernel(q_ref, k_ref, v_ref, taps_ref, a_ref, b_ref, c_ref, d_ref, e_ref, bias_ref, out_ref):
    share, width = q_ref.shape
    for place, ref in enumerate((q_ref, k_ref, v_ref)):
        out_ref[place * share : (place + 1) * share, :] = ref[...]
    vectors = [ref[...] for ref in (a_ref, b_ref, c_ref, d_ref, e_ref)]
    out_ref[3 * share :, :] = small_block(taps_ref[...], vectors, bias_ref[...], width)


def stack(query, key, value, taps, vectors, bias):
    share, width = query.shape
    vectors = [v.reshape(1, -1) for v in vectors]
    bias = bias.reshape(1, -1)
    if share % 8:
        return jnp.concatenate((query, key, value, small_block(taps, vectors, bias, width)), axis=0)
    return pl.pallas_call(
        stack_kernel,
        out_shape=jax.ShapeDtypeStruct((3 * share + SMALL, width), BF16),
        cost_estimate=QUICK,
        name="stack",
    )(query, key, value, taps, *vectors, bias)


def square_of(w_ref, place):
    units, _, width = w_ref.shape
    part = width // units
    return w_ref[:, place * part : (place + 1) * part, :].reshape(width, width)


def project_own_kernel(x_ref, w_ref, q_ref, k_ref, v_ref):
    for place, ref in enumerate((q_ref, k_ref, v_ref)):
        ref[0] = nn(x_ref[0], square_of(w_ref, place)).astype(BF16)


def project_halos_kernel(
    own_k_ref, own_v_ref, left_ref, right_ref, far_ref, wk_ref, wv_ref, k_ref, v_ref, halos
):
    group, width = own_k_ref.shape[1:]
    right = HALO + group
    halos[:HALO, :] = left_ref[0]
    halos[HALO : 2 * HALO, :] = right_ref[0]
    halos[2 * HALO :, :] = padded(far_ref)
    for w_ref, own_ref, ref in ((wk_ref, own_k_ref, k_ref), (wv_ref, own_v_ref, v_ref)):
        rows = nn(halos[...], w_ref[...].reshape(width, width)).astype(BF16)
        ref[0, :HALO, :] = rows[:HALO]
        ref[0, HALO:right, :] = own_ref[0]
        ref[0, right:, :] = rows[HALO:]


def padded(far_ref):
    width = far_ref.shape[2]
    row = lax.broadcasted_iota(jnp.int32, (PAD, width), 0)
    far = jnp.broadcast_to(far_ref[0].astype(F32), (PAD, width))
    return jnp.where(row == 0, far, 0.0).astype(BF16)


def resident(*shape):
    return pl.BlockSpec(
        shape, lambda s: (0,) * len(shape), pipeline_mode=pl.Buffered(buffer_count=1)
    )


def one_of(weights, place):
    units, _, width = weights.shape
    return pl.BlockSpec(
        (units, width // units, width),
        lambda s: (0, place, 0),
        pipeline_mode=pl.Buffered(buffer_count=1),
    )


def project_own(x, weights):
    seqs, group, width = x.shape
    return pl.pallas_call(
        project_own_kernel,
        grid=(seqs,),
        in_specs=[by_seq(group, width), resident(*weights.shape)],
        out_specs=[by_seq(group, width)] * 3,
        out_shape=[jax.ShapeDtypeStruct(x.shape, BF16)] * 3,
        compiler_params=pltpu.CompilerParams(vmem_limit_bytes=60 << 20),
        cost_estimate=QUICK,
        name="project_own",
    )(x, weights)


def project_halos(own_keys, own_values, left, right, far, weights):
    seqs, group, width = own_keys.shape
    ext = group + 2 * HALO + PAD
    return pl.pallas_call(
        project_halos_kernel,
        grid=(seqs,),
        in_specs=[by_seq(group, width)] * 2
        + [by_seq(HALO, width), by_seq(HALO, width), by_seq(1, width)]
        + [one_of(weights, 1), one_of(weights, 2)],
        out_specs=[by_seq(ext, width)] * 2,
        out_shape=[jax.ShapeDtypeStruct((seqs, ext, width), BF16)] * 2,
        scratch_shapes=[pltpu.VMEM((2 * HALO + PAD, width), BF16)],
        compiler_params=pltpu.CompilerParams(vmem_limit_bytes=60 << 20),
        cost_estimate=QUICK,
        name="project_halos",
    )(own_keys, own_values, left, right, far, weights, weights)


def halo_grad_kernel(dk_ref, dv_ref, wk_ref, wv_ref, left_ref, right_ref, far_ref, dk, dv):
    right = dk_ref.shape[1] - HALO - PAD
    width = dk_ref.shape[2]
    for rows, ref in ((dk, dk_ref), (dv, dv_ref)):
        rows[:HALO, :] = ref[0, :HALO, :]
        rows[HALO:, :] = ref[0, right:, :]
    grad = nt(dk[...], wk_ref[...].reshape(width, width)) + nt(
        dv[...], wv_ref[...].reshape(width, width)
    )
    left_ref[0] = grad[:HALO].astype(BF16)
    right_ref[0] = grad[HALO : 2 * HALO].astype(BF16)
    far_ref[0] = grad[2 * HALO : 2 * HALO + 1].astype(BF16)


def halo_grads(d_keys, d_values, weights):
    seqs, ext, width = d_keys.shape
    rows = (HALO, HALO, 1)
    kept = pltpu.VMEM((2 * HALO + PAD, width), BF16)
    return pl.pallas_call(
        halo_grad_kernel,
        grid=(seqs,),
        in_specs=[by_seq(ext, width), by_seq(ext, width), one_of(weights, 1), one_of(weights, 2)],
        out_specs=[by_seq(n, width) for n in rows],
        out_shape=[jax.ShapeDtypeStruct((seqs, n, width), BF16) for n in rows],
        scratch_shapes=[kept, kept],
        compiler_params=pltpu.CompilerParams(vmem_limit_bytes=60 << 20),
        cost_estimate=QUICK,
        name="halo_grads",
    )(d_keys, d_values, weights, weights)


def own_grad_kernel(dq_ref, dk_ref, dv_ref, first_ref, w_ref, own_ref):
    grad = nt(dq_ref[0], square_of(w_ref, 0)) + nt(dk_ref[0], square_of(w_ref, 1))
    own_ref[0] = grad + nt(dv_ref[0], square_of(w_ref, 2)) + first_ref[0]


def own_grads(d_queries, d_keys, d_values, d_first, weights):
    seqs, group, width = d_queries.shape
    middle = pl.BlockSpec((1, group, width), lambda s: (s, HALO // group, 0))
    return pl.pallas_call(
        own_grad_kernel,
        grid=(seqs,),
        in_specs=[
            by_seq(group, width),
            middle,
            middle,
            by_seq(group, width),
            resident(*weights.shape),
        ],
        out_specs=by_seq(group, width),
        out_shape=jax.ShapeDtypeStruct((seqs, group, width), F32),
        compiler_params=pltpu.CompilerParams(vmem_limit_bytes=60 << 20),
        cost_estimate=QUICK,
        name="own_grads",
    )(d_queries, d_keys, d_values, d_first, weights)


def split_cores(value, core):
    both = value.reshape((-1, 2) + value.shape[1:])
    mine, other = both[:, 0], both[:, 1]
    return jnp.where(core == 0, mine, other), jnp.where(core == 0, other, mine)


def weight_grad_kernel(
    core_ref,
    x_ref,
    left_ref,
    right_ref,
    far_ref,
    dq_ref,
    dk_ref,
    dv_ref,
    small_ref,
    mine_ref,
    other_ref,
    acc,
    rows,
    x_tail,
    dk_tail,
    dv_tail,
):
    seq = pl.program_id(0)
    core = core_ref[0]
    group, width = dq_ref.shape[1:]
    units = 2 * mine_ref.shape[0]
    part = width // units
    main = 2 * HALO + group

    @pl.when(seq == 0)
    def _():
        acc[...] = jnp.zeros_like(acc)

    rows[:HALO, :] = left_ref[0]
    rows[HALO : HALO + group, :] = x_ref[0]
    rows[HALO + group :, :] = right_ref[0]
    tail = pl.ds(pl.multiple_of(seq * PAD, PAD), PAD)
    x_tail[tail, :] = padded(far_ref)
    dk_tail[tail, :] = dk_ref[0, main:, :]
    dv_tail[tail, :] = dv_ref[0, main:, :]
    acc[0] += tn(x_ref[0], dq_ref[0])
    acc[1] += tn(rows[...], dk_ref[0, :main, :])
    acc[2] += tn(rows[...], dv_ref[0, :main, :])

    @pl.when(seq == pl.num_programs(0) - 1)
    def _():
        ends = (None, tn(x_tail[...], dk_tail[...]), tn(x_tail[...], dv_tail[...]))
        for place, end in enumerate(ends):
            total = acc[place] if end is None else acc[place] + end
            mine, other = split_cores(total.reshape(units, part, width), core)
            at = slice(place * part, (place + 1) * part)
            mine_ref[:, at, :] = mine.astype(BF16)
            other_ref[:, at, :] = other.astype(BF16)
        used = small_ref.shape[2]
        for ref, half in zip((mine_ref, other_ref), split_cores(small_ref[...], core)):
            ref[:, 3 * part :, :used] = half.astype(BF16)
            ref[:, 3 * part :, used:] = jnp.zeros(half.shape[:2] + (width - used,), BF16)


def weight_grads(core, x, left, right, far, d_queries, d_keys, d_values, small):
    seqs, group, width = d_queries.shape
    ext = d_keys.shape[1]
    units, small_rows, _ = small.shape
    shape = (units // 2, 3 * (width // units) + small_rows, width)
    tail = pltpu.VMEM((seqs * PAD, width), BF16)
    return pl.pallas_call(
        weight_grad_kernel,
        grid=(seqs,),
        in_specs=[
            pl.BlockSpec(memory_space=pltpu.SMEM),
            by_seq(group, width),
            by_seq(HALO, width),
            by_seq(HALO, width),
            by_seq(1, width),
            by_seq(group, width),
            by_seq(ext, width),
            by_seq(ext, width),
            resident(*small.shape),
        ],
        out_specs=[resident(*shape)] * 2,
        out_shape=[jax.ShapeDtypeStruct(shape, BF16)] * 2,
        scratch_shapes=[
            pltpu.VMEM((3, width, width), F32),
            pltpu.VMEM((2 * HALO + group, width), BF16),
            tail,
            tail,
            tail,
        ],
        compiler_params=pltpu.CompilerParams(vmem_limit_bytes=60 << 20),
        cost_estimate=QUICK,
        name="weight_grads",
    )(core, x, left, right, far, d_queries, d_keys, d_values, small)


def document_of(positions, lengths, seq_len):
    count = lengths.shape[1]
    order = jnp.arange(count)
    ends = jnp.sum(jnp.where(order[None, :] <= order[:, None], lengths[:, None, :], 0), axis=2)
    counted = jnp.sum((positions[None, :, None] >= ends[:, None, :]).astype(jnp.int32), axis=2)
    inside = (positions >= 0) & (positions < seq_len)
    return jnp.where(inside[None, :], counted, -1)


def masks(lengths, offset, group, seq_len):
    ext = group + 2 * HALO
    slots = ext // 4
    positions = offset - HALO + jnp.arange(ext + PAD, dtype=jnp.int32)
    doc = document_of(positions, lengths, seq_len)
    slot_doc = doc[:, 2:ext:4]
    biases = []
    for block in range(group // QB):
        near = HALO - WIN // 2 + block * QB
        far = block * QB // 4
        key_place = jnp.concatenate((jnp.arange(near, near + NEAR), 4 * jnp.arange(far, far + FAR) + 2))
        reach = jnp.concatenate((jnp.full((NEAR,), WIN // 2), jnp.full((FAR,), PWIN // 2)))
        key_doc = jnp.concatenate((doc[:, near : near + NEAR], slot_doc[:, far : far + FAR]), axis=1)
        query_place = HALO + block * QB + jnp.arange(QB)
        query_doc = doc[:, HALO + block * QB : HALO + (block + 1) * QB]
        allowed = (jnp.abs(key_place[:, None] - query_place[None, :]) <= reach[:, None])[None] & (
            key_doc[:, :, None] == query_doc[:, None, :]
        )
        biases.append(jnp.where(allowed, 0.0, MASKED).astype(F32))
    same = jnp.stack(
        [(doc[:, tap : tap + ext : 4] == slot_doc).astype(F32) for tap in range(5)], axis=1
    )
    same = jnp.broadcast_to(same[..., None], same.shape + (LANES,))
    return jnp.stack(biases, axis=1), same, slots


def steps(count):
    for k in range(1, count):
        if count & (count - 1) == 0:
            yield [(i, i ^ k) for i in range(count)], lambda me, k=k: (me ^ k, me ^ k)
        else:
            yield (
                [(i, (i + k) % count) for i in range(count)],
                lambda me, k=k: (lax.rem(me + k, count), lax.rem(me - k + count, count)),
            )


def pick(value, index, dim=0):
    return lax.dynamic_index_in_dim(value, index, dim, keepdims=False)


def gather_seq(block, *earlier):
    count, me = lax.axis_size("seq"), lax.axis_index("seq")
    zeros = (0,) * block.ndim
    came_all = after(tuple(lax.ppermute(block, "seq", pairs) for pairs, _ in steps(count)), *earlier)
    column = jnp.zeros((count,) + block.shape, block.dtype)
    column = lax.dynamic_update_slice(column, block[None], (me,) + zeros)
    for came, (_, met) in zip(came_all, steps(count)):
        column = lax.dynamic_update_slice(column, came[None], (met(me)[1],) + zeros)
    return column


def gather_yx(column):
    me = lax.axis_index("yx")
    pieces = [(column, me)]
    for pairs, met in steps(lax.axis_size("yx")):
        pieces.append((lax.ppermute(column, "yx", pairs), met(me)[1]))
    return pieces


def assemble_kernel(count, *refs):
    places, parts, whole, sems = refs[0], refs[1 : 1 + count], refs[-2], refs[-1]
    copies = [
        pltpu.make_async_copy(part, whole.at[places[i]], sems.at[i]) for i, part in enumerate(parts)
    ]
    for copy in copies:
        copy.start()
    for copy in copies:
        copy.wait()


def gather_core(pieces):
    count, me = lax.axis_size("core"), lax.axis_index("core")
    parts, places = [], []
    for piece, place in pieces:
        parts.append(piece)
        places.append(place * count + me)
        for pairs, met in steps(count):
            parts.append(lax.ppermute(piece, "core", pairs))
            places.append(place * count + met(me)[1])
    return pl.pallas_call(
        functools.partial(assemble_kernel, len(parts)),
        in_specs=[pl.BlockSpec(memory_space=pltpu.SMEM)]
        + [pl.BlockSpec(memory_space=pltpu.VMEM)] * len(parts),
        out_specs=pl.BlockSpec(memory_space=pl.ANY),
        out_shape=jax.ShapeDtypeStruct((len(parts),) + parts[0].shape, BF16),
        compiler_params=pltpu.CompilerParams(vmem_limit_bytes=60 << 20),
        scratch_shapes=[pltpu.SemaphoreType.DMA((len(parts),))],
        cost_estimate=QUICK,
        name="assemble",
    )(jnp.stack(places).astype(jnp.int32), *parts)


def after(value, *earlier):
    return lax.optimization_barrier((value, earlier))[0] if earlier else lax.optimization_barrier(value)


def exchange_sum(pieces, axis, *earlier):
    me = lax.axis_index(axis)
    came = [
        lax.ppermute(pick(pieces, met(me)[0]), axis, pairs)
        for pairs, met in steps(lax.axis_size(axis))
    ]
    total = pick(pieces, me).astype(F32)
    for part in after(came, *earlier):
        total = total + part.astype(F32)
    return total


def local(
    tokens,
    doc_lengths,
    query_weight,
    key_weight,
    value_weight,
    out_weight,
    pool_weight,
    first_gain,
    first_shift,
    inner_weight,
    inner_bias,
    outer_weight,
    outer_bias,
    second_gain,
    second_shift,
    cotangent,
):
    seq_count = lax.axis_size("seq")
    yx_count = lax.axis_size("yx")
    core_count = lax.axis_size("core")
    units = yx_count * core_count
    parts = units * seq_count
    core = lax.axis_index("core")
    seq_place = lax.axis_index("seq")
    seqs, group, width = tokens.shape
    ff = inner_weight.shape[1]
    panels = ff // width
    share = query_weight.shape[0]
    count = seqs * group

    def shift(value, by):
        pairs = [(i, i + by) for i in range(seq_count) if 0 <= i + by < seq_count]
        return lax.ppermute(value, "seq", pairs)

    early = stack(
        query_weight,
        key_weight,
        value_weight,
        pool_weight,
        (first_gain, first_shift, outer_bias, second_gain, second_shift),
        inner_bias,
    )
    late = pack(outer_weight, inner_weight, out_weight)
    bias, same, _ = masks(doc_lengths, seq_place * group, group, group * seq_count)
    early_column, bias, same = after((gather_seq(early), bias, same))
    sent = after(tokens, early_column)
    came = (
        shift(sent[:, group - HALO :], 1),
        shift(sent[:, :HALO], -1),
        shift(sent[:, :1], -2),
    )
    early_column = jnp.concatenate(
        [early_column[:, i * share : (i + 1) * share].reshape(-1, width) for i in range(3)]
        + [early_column[:, 3 * share :].reshape(-1, width)],
        axis=0,
    )
    early_pieces = gather_yx(early_column)
    early = gather_core(early_pieces)
    late_column = lax.all_gather(late, "seq", axis=0)
    late_column = after(late_column, [piece for piece, _ in early_pieces[1:]])
    outer_rows = panels * share
    late = lax.all_gather(late_column, ("yx", "core"), axis=0)
    late = late.reshape(units, seq_count, 2 * panels + 1, share, width)
    small = early[:, 3 * seq_count * share :].reshape(parts, SMALL, width)
    vectors = small[:, : SMALL - 1, :share].transpose(1, 0, 2).reshape(SMALL - 1, width).astype(F32)
    taps = jnp.pad(vectors[:10], ((0, 6), (0, 0)))
    small_rows_f32 = jnp.pad(vectors[10:], ((0, 3), (0, 0)))
    bias_inner = small[:, SMALL - 1, : ff // parts].reshape(panels, 1, width).astype(F32)

    flat = tokens.reshape(count, width)

    queries, own_keys, own_values = project_own(tokens, early)
    keys, values = project_halos(own_keys, own_values, *came, early)
    mixed, lse = attention_forward(queries, keys, values, taps, same, bias)
    y, d_first, d_mixed, d_small, d_bias, d_late = feed_forward(
        flat,
        mixed.reshape(count, width),
        cotangent.reshape(count, width),
        small_rows_f32,
        bias_inner,
        late,
    )
    late_sum = lax.psum_scatter(
        d_late.reshape(-1, width), ("yx", "core"), scatter_dimension=0, tiled=True
    )
    d_queries, d_keys, d_values, d_taps = attention_backward(
        queries,
        keys,
        values,
        taps,
        same,
        bias,
        lse,
        d_mixed.reshape(seqs, group, width),
        0,
        seqs,
        (),
    )
    left, right, far = halo_grads(d_keys, d_values, early)
    from_far = shift(far, 2)
    back = (from_far, shift(left, -1), shift(right, 1))

    d_taps = jnp.sum(d_taps, axis=0)[:10]
    d_vectors = jnp.concatenate((d_taps, d_small[:5]), axis=0)
    d_vectors = d_vectors.reshape(SMALL - 1, parts, share).transpose(1, 0, 2)
    d_vectors = jnp.pad(d_vectors, ((0, 0), (0, 0), (0, LANES - share)))
    d_bias = jnp.pad(d_bias.reshape(parts, 1, -1), ((0, 0), (0, 0), (0, LANES - ff // parts)))
    d_vectors = jnp.concatenate((d_vectors, d_bias), axis=1)
    d_vectors = d_vectors.reshape(units, seq_count * SMALL, LANES)
    mine, other = weight_grads(
        core.astype(jnp.int32).reshape(1),
        after(tokens, left),
        *came,
        d_queries,
        d_keys,
        d_values,
        d_vectors,
    )
    own = own_grads(
        d_queries,
        *after((d_keys, d_values), mine),
        d_first.reshape(seqs, group, width),
        early,
    )
    (mine, other), back, late_sum, own = after(((mine, other), back, late_sum, own))
    late_sum = lax.psum_scatter(late_sum, "seq", scatter_dimension=0, tiled=True).astype(F32)
    swapped = lax.ppermute(other, "core", [(0, 1), (1, 0)])
    early_sum = (mine.astype(F32) + swapped.astype(F32)).astype(BF16)
    early_sum = exchange_sum(early_sum, "yx").astype(BF16)
    whole = 3 * seq_count * share
    early_sum = jnp.concatenate(
        [
            early_sum[:whole]
            .reshape(3, seq_count, share, width)
            .swapaxes(0, 1)
            .reshape(seq_count, 3 * share, width),
            early_sum[whole:].reshape(seq_count, SMALL, width),
        ],
        axis=1,
    )
    early_sum = exchange_sum(early_sum, "seq")

    edge = group - HALO
    from_far, from_right, from_left = (part.astype(F32) for part in back)
    d_input = own + jnp.pad(from_right, ((0, 0), (edge, 0), (0, 0)))
    d_input = d_input + jnp.pad(from_left, ((0, 0), (0, edge), (0, 0)))
    d_input = d_input + jnp.pad(from_far, ((0, 0), (0, group - 1), (0, 0)))

    vector_sum = early_sum[3 * share :]
    pieces = [vector_sum[10 + i, :share] for i in range(5)]
    return (
        y.reshape(seqs, group, width),
        d_input.astype(BF16),
        early_sum[:share],
        early_sum[share : 2 * share],
        early_sum[2 * share : 3 * share],
        late_sum[2 * outer_rows :],
        vector_sum[:10, :share],
        pieces[0],
        pieces[1],
        late_sum[outer_rows : 2 * outer_rows]
        .reshape(panels, share, width)
        .transpose(1, 0, 2)
        .reshape(share, ff),
        vector_sum[SMALL - 1, : ff // parts],
        late_sum[:outer_rows],
        pieces[2],
        pieces[3],
        pieces[4],
    )


def solution(mesh):
    dp, seq = mesh.devices.shape
    cores = 2 if dp % 2 == 0 else 1
    mesh = Mesh(mesh.devices.reshape(dp // cores, cores, seq), ("yx", "core", "seq"))
    every = ("yx", "core", "seq")
    rows = P(every, None)
    vector = P(every)
    whole = P(("yx", "core"), "seq", None)
    taps = P(None, every)
    weights = (rows, rows, rows, rows, taps, vector, vector, rows, vector, rows, vector, vector, vector)
    return jax.shard_map(
        local,
        mesh=mesh,
        in_specs=(whole, P(("yx", "core"), None)) + weights + (whole,),
        out_specs=(whole, whole) + weights,
        check_vma=False,
    )
```

```python
import functools

import jax
import jax.numpy as jnp
from jax import lax
from jax.experimental import pallas as pl
from jax.experimental.pallas import tpu as pltpu
from jax.sharding import Mesh
from jax.sharding import PartitionSpec as P

HEADS = 12
HEAD_DIM = 64
WIN = 128
PWIN = 512
EPS = 1e-05

LANES = 128
QB = 128
GROUP = 6
GROUP_BACK = 2
HALO = PWIN // 2
PAD = 16
NEAR = QB + WIN
FAR = (QB + PWIN) // 4
KEYS = NEAR + FAR
MASKED = -1e30
QUICK = pl.CostEstimate(flops=1 << 20, bytes_accessed=1 << 20, transcendentals=0)

F32 = jnp.float32
BF16 = jnp.bfloat16


def nt(left, right):
    return lax.dot_general(left, right, (((1,), (1,)), ((), ())), preferred_element_type=F32)


def tn(left, right):
    return lax.dot_general(left, right, (((0,), (0,)), ((), ())), preferred_element_type=F32)


def nn(left, right):
    return lax.dot_general(left, right, (((1,), (0,)), ((), ())), preferred_element_type=F32)


def slot_taps(wide, slots):
    return [wide[pl.ds(tap, slots, stride=4), :] for tap in range(5)]


def pool(taps, same_ref, w_ref, first, lanes):
    total = None
    for tap in range(5):
        term = taps[tap] * same_ref[0, tap] * w_ref[first + tap : first + tap + 1, lanes]
        total = term if total is None else total + term
    return total.astype(BF16)


def pair_stack(rows):
    lane = lax.broadcasted_iota(jnp.int32, rows.shape, 1)
    zero = jnp.zeros_like(rows)
    return jnp.concatenate(
        (jnp.where(lane < HEAD_DIM, rows, zero), jnp.where(lane < HEAD_DIM, zero, rows)), axis=0
    )


def pair_join(both):
    joined = jnp.concatenate((both[:HEAD_DIM, :QB], both[HEAD_DIM:, QB:]), axis=0)
    return joined.T


def rows_of(block):
    return slice(block * QB, (block + 1) * QB)


def keys_of(ref, pooled, block, lanes):
    near = HALO - WIN // 2 + block * QB
    far = block * QB // 4
    return jnp.concatenate((ref[0, near : near + NEAR, lanes], pooled[far : far + FAR, :]), axis=0)


def scores_of(keys, stacked, bias):
    return nt(keys, stacked) + jnp.concatenate((bias, bias), axis=1)


def attn_fwd_kernel(
    q_ref, k_ref, v_ref, w_ref, same_ref, bias_ref, out_ref, lse_ref, k_wide, v_wide, pk_ref, pv_ref
):
    slots = pk_ref.shape[1]
    scale = jnp.asarray(HEAD_DIM**-0.5, BF16)

    blocks = q_ref.shape[1] // QB

    def body(step, carry):
        jobs = []
        for lane in range(GROUP):
            pair = step * GROUP + lane
            lanes = pl.ds(pl.multiple_of(pair * LANES, LANES), LANES)
            k_wide[lane] = k_ref[0, :, lanes].astype(F32)
            v_wide[lane] = v_ref[0, :, lanes].astype(F32)
            pk_ref[lane] = pool(slot_taps(k_wide.at[lane], slots), same_ref, w_ref, 0, lanes)
            pv_ref[lane] = pool(slot_taps(v_wide.at[lane], slots), same_ref, w_ref, 5, lanes)
            jobs += [(lane, pair, lanes, block) for block in range(blocks)]
        scores = []
        for lane, pair, lanes, block in jobs:
            stacked = pair_stack(q_ref[0, rows_of(block), lanes] * scale)
            keys = keys_of(k_ref, pk_ref.at[lane], block, lanes)
            scores.append(scores_of(keys, stacked, bias_ref[0, block]))
        probs = []
        for (lane, pair, lanes, block), score in zip(jobs, scores):
            top = jnp.max(score, axis=0, keepdims=True)
            weights = jnp.exp(score - top)
            denom = jnp.sum(weights, axis=0, keepdims=True)
            probs.append((weights * (1.0 / denom)).astype(BF16))
            lse_ref[0, pair, block : block + 1, :] = top + jnp.log(denom)
        mixed = []
        for (lane, pair, lanes, block), prob in zip(jobs, probs):
            mixed.append(tn(keys_of(v_ref, pv_ref.at[lane], block, lanes), prob))
        for (lane, pair, lanes, block), value in zip(jobs, mixed):
            out_ref[0, rows_of(block), lanes] = pair_join(value).astype(BF16)
        return carry

    lax.fori_loop(0, q_ref.shape[2] // (LANES * GROUP), body, 0)


def attn_bwd_kernel(
    q_ref,
    k_ref,
    v_ref,
    w_ref,
    same_ref,
    bias_ref,
    lse_ref,
    do_ref,
    dq_ref,
    dk_ref,
    dv_ref,
    dw_ref,
    k_wide,
    v_wide,
    pk_ref,
    pv_ref,
    dpk_ref,
    dpv_ref,
):
    slots = pk_ref.shape[1]
    scale = jnp.asarray(HEAD_DIM**-0.5, BF16)
    blocks = q_ref.shape[1] // QB

    def body(step, carry):
        jobs = []
        for lane in range(GROUP_BACK):
            pair = step * GROUP_BACK + lane
            lanes = pl.ds(pl.multiple_of(pair * LANES, LANES), LANES)
            k_wide[lane] = k_ref[0, :, lanes].astype(F32)
            v_wide[lane] = v_ref[0, :, lanes].astype(F32)
            pk_ref[lane] = pool(slot_taps(k_wide.at[lane], slots), same_ref, w_ref, 0, lanes)
            pv_ref[lane] = pool(slot_taps(v_wide.at[lane], slots), same_ref, w_ref, 5, lanes)
            jobs += [(lane, pair, lanes, block) for block in range(blocks)]
        dpk_ref[...] = jnp.zeros_like(dpk_ref)
        dpv_ref[...] = jnp.zeros_like(dpv_ref)
        scores, d_probs = [], []
        for lane, pair, lanes, block in jobs:
            keys = keys_of(k_ref, pk_ref.at[lane], block, lanes)
            stacked = pair_stack(q_ref[0, rows_of(block), lanes] * scale)
            scores.append(scores_of(keys, stacked, bias_ref[0, block]))
            values = keys_of(v_ref, pv_ref.at[lane], block, lanes)
            d_probs.append(nt(values, pair_stack(do_ref[0, rows_of(block), lanes])))
        probs, d_scores = [], []
        for (lane, pair, lanes, block), score, d_prob in zip(jobs, scores, d_probs):
            prob = jnp.exp(score - lse_ref[0, pair, block : block + 1, :])
            row_dot = jnp.sum(prob * d_prob, axis=0, keepdims=True)
            d_scores.append((prob * (d_prob - row_dot)).astype(BF16))
            probs.append(prob.astype(BF16))
        parts = []
        for (lane, pair, lanes, block), prob, d_score in zip(jobs, probs, d_scores):
            d_values = nn(prob, pair_stack(do_ref[0, rows_of(block), lanes]))
            d_keys = nn(d_score, pair_stack(q_ref[0, rows_of(block), lanes] * scale))
            far = slice(block * QB // 4, block * QB // 4 + FAR)
            dpk_ref[lane, far, :] += d_keys[NEAR:]
            dpv_ref[lane, far, :] += d_values[NEAR:]
            parts.append((d_keys[:NEAR], d_values[:NEAR]))
        d_queries = []
        for (lane, pair, lanes, block), d_score in zip(jobs, d_scores):
            d_queries.append(tn(keys_of(k_ref, pk_ref.at[lane], block, lanes), d_score))
        for (lane, pair, lanes, block), value in zip(jobs, d_queries):
            dq_ref[0, rows_of(block), lanes] = (pair_join(value) * HEAD_DIM**-0.5).astype(BF16)
        for lane in range(GROUP_BACK):
            lanes = jobs[lane * blocks][2]
            for side, (wide_ref, d_pool_ref, out_ref) in enumerate(
                ((k_wide, dpk_ref, dk_ref), (v_wide, dpv_ref, dv_ref))
            ):
                wide = wide_ref.at[lane]
                d_pool = d_pool_ref[lane]
                taps = slot_taps(wide, slots)
                masked = [d_pool * same_ref[0, tap] for tap in range(5)]
                places = [5 * side + tap for tap in range(5)]
                for tap, row in enumerate(places):
                    dw_ref[0, row : row + 1, lanes] = jnp.sum(
                        masked[tap] * taps[tap], axis=0, keepdims=True
                    )
                spread = [
                    masked[tap] * w_ref[row : row + 1, lanes] for tap, row in enumerate(places)
                ]
                wide[4 * slots :, :] = jnp.zeros((wide.shape[0] - 4 * slots, LANES), F32)
                for tap in range(4):
                    wide[pl.ds(tap, slots, stride=4), :] = spread[tap]
                wide[pl.ds(4, slots, stride=4), :] += spread[4]
                for block in range(blocks):
                    near = HALO - WIN // 2 + block * QB
                    wide[near : near + NEAR, :] += parts[lane * blocks + block][side]
                out_ref[0, :, lanes] = wide[...].astype(BF16)
        return carry

    lax.fori_loop(0, q_ref.shape[2] // (LANES * GROUP_BACK), body, 0)
    dw_ref[0, 10:, :] = jnp.zeros((dw_ref.shape[1] - 10, dw_ref.shape[2]), F32)


def by_seq(*shape, first=0):
    return pl.BlockSpec((1,) + shape, lambda s: (s + first,) + (0,) * len(shape))


def attention_specs(ext, group, slots, width, first=0):
    return [
        by_seq(group, width, first=first),
        by_seq(ext, width, first=first),
        by_seq(ext, width, first=first),
        pl.BlockSpec((16, width), lambda s: (0, 0)),
        by_seq(5, slots, LANES, first=first),
        by_seq(group // QB, KEYS, LANES, first=first),
    ]


def attention_forward(queries, keys, values, taps, same, bias):
    seqs, group, width = queries.shape
    ext = keys.shape[1]
    slots = same.shape[2]
    pairs = width // LANES
    blocks = group // QB
    wide = pltpu.VMEM((GROUP, ext, LANES), F32)
    pooled = pltpu.VMEM((GROUP, slots, LANES), BF16)
    return pl.pallas_call(
        attn_fwd_kernel,
        grid=(seqs,),
        in_specs=attention_specs(ext, group, slots, width),
        out_specs=[by_seq(group, width), by_seq(pairs, blocks, 2 * QB)],
        out_shape=[
            jax.ShapeDtypeStruct((seqs, group, width), BF16),
            jax.ShapeDtypeStruct((seqs, pairs, blocks, 2 * QB), F32),
        ],
        scratch_shapes=[wide, wide, pooled, pooled],
        compiler_params=pltpu.CompilerParams(vmem_limit_bytes=60 << 20),
        cost_estimate=QUICK,
        name="attn_fwd",
    )(queries, keys, values, taps, same, bias)


def attention_backward(queries, keys, values, taps, same, bias, lse, d_mixed, first, count, earlier):
    seqs, group, width = queries.shape
    ext = keys.shape[1]
    slots = same.shape[2]
    pairs = width // LANES
    blocks = group // QB
    wide = pltpu.VMEM((GROUP_BACK, ext, LANES), F32)
    pooled = pltpu.VMEM((GROUP_BACK, slots, LANES), BF16)
    d_pooled = pltpu.VMEM((GROUP_BACK, slots, LANES), F32)
    args = (queries, keys, values, taps, same, bias, lse, d_mixed)

    def kernel(*refs):
        attn_bwd_kernel(*refs[: len(args)], *refs[len(args) + len(earlier) :])

    return pl.pallas_call(
        kernel,
        grid=(count,),
        in_specs=attention_specs(ext, group, slots, width, first)
        + [by_seq(pairs, blocks, 2 * QB, first=first), by_seq(group, width, first=first)]
        + [pl.BlockSpec(memory_space=pl.ANY)] * len(earlier),
        out_specs=[
            by_seq(*shape, first=first)
            for shape in ((group, width), (ext, width), (ext, width), (16, width))
        ],
        out_shape=[
            jax.ShapeDtypeStruct((seqs, group, width), BF16),
            jax.ShapeDtypeStruct((seqs, ext, width), BF16),
            jax.ShapeDtypeStruct((seqs, ext, width), BF16),
            jax.ShapeDtypeStruct((seqs, 16, width), F32),
        ],
        input_output_aliases={len(args) + i: i for i in range(len(earlier))},
        scratch_shapes=[wide, wide, pooled, pooled, d_pooled, d_pooled],
        compiler_params=pltpu.CompilerParams(vmem_limit_bytes=60 << 20),
        cost_estimate=QUICK,
        name="attn_bwd",
    )(*args, *earlier)


ROWS = 512
HALF_PI = 0.3989422804014327


def row_sum(value):
    return jnp.sum(value, axis=0, keepdims=True)


def row_mean(value):
    return jnp.mean(value, axis=1, keepdims=True)


def normalize(value):
    centered = value - row_mean(value)
    inv = lax.rsqrt(row_mean(centered * centered) + EPS)
    return centered * inv, inv


def normalize_back(grad, normed, inv):
    return inv * (grad - row_mean(grad) - normed * row_mean(grad * normed))


def ffn_kernel(
    panels,
    x_ref,
    mixed_ref,
    cot_ref,
    wo_ref,
    small_ref,
    bias_ref,
    w_in_ref,
    w_out_ref,
    y_ref,
    d_first_ref,
    d_mixed_ref,
    d_small_ref,
    d_bias_ref,
    d_weights_ref,
    n_one,
    inv_one,
    low,
    hidden,
    slope,
    d_inner,
    cot,
    y_all,
    d_in_stage,
    d_out_stage,
    in_sems,
    out_sems,
):
    step = pl.program_id(0)
    tokens, width = x_ref.shape
    chunks = tokens // ROWS
    acc, d_outer = d_first_ref, d_mixed_ref
    units = d_weights_ref.shape[0]
    some = units // panels

    def in_copy(panel, slot):
        return pltpu.make_async_copy(
            d_in_stage.at[slot], d_weights_ref.at[:, :, panels + panel], in_sems.at[slot]
        )

    def out_copy(panel, slot):
        return pltpu.make_async_copy(
            d_out_stage.at[slot],
            d_weights_ref.at[pl.ds(panel * some, some), :, pl.ds(0, panels)],
            out_sems.at[slot],
        )

    def square(ref):
        return ref[...].reshape(width, width)

    gain_one, shift_one, outer_bias, gain_two, shift_two = (
        small_ref[i : i + 1, :] for i in range(5)
    )

    piece = cot_ref.shape[0]
    piece_rows = pl.ds(pl.multiple_of(lax.rem(step, panels) * piece, piece), piece)

    @pl.when(step < panels)
    def _():
        cot[piece_rows, :] = cot_ref[...]

    @pl.when(step == 0)
    def _():
        def body(i, carry):
            rows = pl.ds(pl.multiple_of(i * ROWS, ROWS), ROWS)
            first = x_ref[rows, :].astype(F32) + nn(mixed_ref[rows, :], square(wo_ref))
            normed, inv = normalize(first)
            n_one[rows, :] = normed
            inv_one[rows, :] = jnp.broadcast_to(inv, (ROWS, LANES))
            out = normed * gain_one + shift_one
            low[rows, :] = out.astype(BF16)
            acc[rows, :] = out + outer_bias
            return carry

        lax.fori_loop(0, chunks, body, 0)

    @pl.when(step < panels)
    def _():
        def body(i, carry):
            rows = pl.ds(pl.multiple_of(i * ROWS, ROWS), ROWS)
            inner = nn(low[rows, :], square(w_in_ref)) + bias_ref[0]
            cdf = 0.5 * (1.0 + lax.erf(inner * 0.7071067811865476))
            pdf = HALF_PI * jnp.exp(-0.5 * inner * inner)
            out = (inner * cdf).astype(BF16)
            hidden[step, rows, :] = out
            slope[step, rows, :] = cdf + inner * pdf
            acc[rows, :] += nn(out, square(w_out_ref))
            return carry

        lax.fori_loop(0, chunks, body, 0, unroll=True)

    @pl.when(step == panels)
    def _():
        def body(i, carry):
            d_gain, d_shift, d_bias = carry
            rows = pl.ds(pl.multiple_of(i * ROWS, ROWS), ROWS)
            normed, inv = normalize(acc[rows, :])
            y_all[rows, :] = (normed * gain_two + shift_two).astype(BF16)
            grad = cot[rows, :].astype(F32)
            d_second = normalize_back(grad * gain_two, normed, inv)
            low_grad = d_second.astype(BF16)
            acc[rows, :] = d_second
            d_outer[rows, :] = low_grad
            return (
                d_gain + row_sum(grad * normed),
                d_shift + row_sum(grad),
                d_bias + row_sum(low_grad.astype(F32)),
            )

        zero = jnp.zeros((1, width), F32)
        d_gain, d_shift, d_bias = lax.fori_loop(0, chunks, body, (zero, zero, zero))
        d_small_ref[2:3, :] = d_bias
        d_small_ref[3:4, :] = d_gain
        d_small_ref[4:5, :] = d_shift
        d_small_ref[5:, :] = jnp.zeros((3, width), F32)

    @pl.when(step >= panels)
    def _():
        panel = step - panels
        y_ref[...] = y_all[piece_rows, :]

        def body(i, d_bias):
            rows = pl.ds(pl.multiple_of(i * ROWS, ROWS), ROWS)
            d_hidden = nt(d_outer[rows, :], square(w_out_ref))
            grad = (d_hidden * slope[panel, rows, :]).astype(BF16)
            d_inner[rows, :] = grad
            acc[rows, :] += nt(grad, square(w_in_ref))
            return d_bias + row_sum(grad.astype(F32))

        zero = jnp.zeros(d_bias_ref.shape[1:], F32)
        d_bias_ref[0] = lax.fori_loop(0, chunks, body, zero, unroll=True)
        slot = lax.rem(panel, 2)

        @pl.when(panel >= 2)
        def _():
            in_copy(panel - 2, slot).wait()
            out_copy(panel - 2, slot).wait()

        d_out_stage[slot] = tn(hidden[panel], d_outer[...]).astype(BF16).reshape(d_out_stage.shape[1:])
        out_copy(panel, slot).start()
        d_in_stage[slot] = tn(low[...], d_inner[...]).astype(BF16).reshape(d_in_stage.shape[1:])
        in_copy(panel, slot).start()

    @pl.when(step == 2 * panels - 1)
    def _():
        def body(i, carry):
            d_gain, d_shift = carry
            rows = pl.ds(pl.multiple_of(i * ROWS, ROWS), ROWS)
            grad = acc[rows, :]
            normed = n_one[rows, :]
            d_first = normalize_back(grad * gain_one, normed, inv_one[rows, 0:1])
            d_first_ref[rows, :] = d_first
            low_grad = d_first.astype(BF16)
            d_inner[rows, :] = low_grad
            d_mixed_ref[rows, :] = nt(low_grad, square(wo_ref)).astype(BF16)
            return d_gain + row_sum(grad * normed), d_shift + row_sum(grad)

        zero = jnp.zeros((1, width), F32)
        d_gain, d_shift = lax.fori_loop(0, chunks, body, (zero, zero))
        d_small_ref[0:1, :] = d_gain
        d_small_ref[1:2, :] = d_shift
        slot = panels % 2
        in_copy(panels - 2, slot).wait()
        d_wo = tn(mixed_ref[...], d_inner[...])
        d_in_stage[slot] = d_wo.astype(BF16).reshape(d_in_stage.shape[1:])
        in_copy(panels, slot).start()
        out_copy(panels - 2, slot).wait()
        in_copy(panels - 1, 1 - slot).wait()
        out_copy(panels - 1, 1 - slot).wait()
        in_copy(panels, slot).wait()


def feed_forward(x, mixed, cot, small, bias, weights):
    tokens, width = x.shape
    units, column, groups, share, _ = weights.shape
    panels = groups // 2
    panel = width

    def whole(*shape):
        return pl.BlockSpec(
            shape, lambda j: (0,) * len(shape), pipeline_mode=pl.Buffered(buffer_count=1)
        )

    def later(j):
        return jnp.maximum(j - panels, 0)

    return pl.pallas_call(
        functools.partial(ffn_kernel, panels),
        grid=(2 * panels,),
        in_specs=[
            whole(tokens, width),
            whole(tokens, width),
            pl.BlockSpec((tokens // panels, width), lambda j: (jnp.minimum(j, panels - 1), 0)),
            pl.BlockSpec(
                (units, column, 1, share, width),
                lambda j: (0, 0, 2 * panels, 0, 0),
                pipeline_mode=pl.Buffered(buffer_count=1),
            ),
            whole(8, width),
            pl.BlockSpec((1, 1, panel), lambda j: (lax.rem(j, panels), 0, 0)),
            pl.BlockSpec(
                (units, column, 1, share, width), lambda j: (0, 0, panels + lax.rem(j, panels), 0, 0)
            ),
            pl.BlockSpec(
                (units // panels, column, panels, share, width),
                lambda j: (lax.rem(j, panels), 0, 0, 0, 0),
            ),
        ],
        out_specs=[
            pl.BlockSpec((tokens // panels, width), lambda j: (later(j), 0)),
            whole(tokens, width),
            whole(tokens, width),
            whole(8, width),
            pl.BlockSpec((1, 1, panel), lambda j: (later(j), 0, 0)),
            pl.BlockSpec(memory_space=pl.ANY),
        ],
        out_shape=[
            jax.ShapeDtypeStruct((tokens, width), BF16),
            jax.ShapeDtypeStruct((tokens, width), F32),
            jax.ShapeDtypeStruct((tokens, width), BF16),
            jax.ShapeDtypeStruct((8, width), F32),
            jax.ShapeDtypeStruct((panels, 1, panel), F32),
            jax.ShapeDtypeStruct(weights.shape, BF16),
        ],
        scratch_shapes=[
            pltpu.VMEM((tokens, width), F32),
            pltpu.VMEM((tokens, LANES), F32),
            pltpu.VMEM((tokens, width), BF16),
            pltpu.VMEM((panels, tokens, panel), BF16),
            pltpu.VMEM((panels, tokens, panel), F32),
            pltpu.VMEM((tokens, panel), BF16),
            pltpu.VMEM((tokens, width), BF16),
            pltpu.VMEM((tokens, width), BF16),
            pltpu.VMEM((2, units, column, share, width), BF16),
            pltpu.VMEM((2, units // panels, column, panels, share, width), BF16),
            pltpu.SemaphoreType.DMA((2,)),
            pltpu.SemaphoreType.DMA((2,)),
        ],
        compiler_params=pltpu.CompilerParams(vmem_limit_bytes=60 << 20),
        cost_estimate=QUICK,
        name="ffn",
    )(x, mixed, cot, weights, small, bias, weights, weights)


def pack_kernel(outer_ref, inner_ref, out_ref, packed_ref):
    rows, width = outer_ref.shape
    share = out_ref.shape[0]
    packed_ref[:rows, :] = outer_ref[...]
    for panel in range(inner_ref.shape[1] // width):
        at = rows + panel * share
        packed_ref[at : at + share, :] = inner_ref[:, panel * width : (panel + 1) * width]
    packed_ref[packed_ref.shape[0] - share :, :] = out_ref[...]


def pack(outer, inner, out):
    share, width = out.shape
    panels = inner.shape[1] // width
    if share % 8:
        inner = inner.reshape(share, panels, width).swapaxes(0, 1).reshape(-1, width)
        return jnp.concatenate((outer, inner, out), axis=0)
    rows = outer.shape[0] + (panels + 1) * share
    return pl.pallas_call(
        pack_kernel,
        out_shape=jax.ShapeDtypeStruct((rows, width), BF16),
        cost_estimate=QUICK,
        name="pack",
    )(outer, inner, out)


SMALL = 16


def small_block(taps, vectors, bias, width):
    share = taps.shape[1]
    rows = jnp.concatenate([taps.astype(F32)] + [v.astype(F32) for v in vectors], axis=0)
    rows = jnp.concatenate((rows, jnp.zeros((rows.shape[0], width - share), F32)), axis=1)
    bias = bias.astype(F32)
    last = jnp.concatenate((bias, jnp.zeros((1, width - bias.shape[1]), F32)), axis=1)
    return jnp.concatenate((rows, last), axis=0).astype(BF16)


def stack_kernel(q_ref, k_ref, v_ref, taps_ref, a_ref, b_ref, c_ref, d_ref, e_ref, bias_ref, out_ref):
    share, width = q_ref.shape
    for place, ref in enumerate((q_ref, k_ref, v_ref)):
        out_ref[place * share : (place + 1) * share, :] = ref[...]
    vectors = [ref[...] for ref in (a_ref, b_ref, c_ref, d_ref, e_ref)]
    out_ref[3 * share :, :] = small_block(taps_ref[...], vectors, bias_ref[...], width)


def stack(query, key, value, taps, vectors, bias):
    share, width = query.shape
    vectors = [v.reshape(1, -1) for v in vectors]
    bias = bias.reshape(1, -1)
    if share % 8:
        return jnp.concatenate((query, key, value, small_block(taps, vectors, bias, width)), axis=0)
    return pl.pallas_call(
        stack_kernel,
        out_shape=jax.ShapeDtypeStruct((3 * share + SMALL, width), BF16),
        cost_estimate=QUICK,
        name="stack",
    )(query, key, value, taps, *vectors, bias)


def square_of(w_ref, place):
    units, _, width = w_ref.shape
    part = width // units
    return w_ref[:, place * part : (place + 1) * part, :].reshape(width, width)


def project_own_kernel(x_ref, w_ref, q_ref, k_ref, v_ref):
    for place, ref in enumerate((q_ref, k_ref, v_ref)):
        ref[0] = nn(x_ref[0], square_of(w_ref, place)).astype(BF16)


def project_halos_kernel(
    own_k_ref, own_v_ref, left_ref, right_ref, far_ref, wk_ref, wv_ref, k_ref, v_ref, halos
):
    group, width = own_k_ref.shape[1:]
    right = HALO + group
    halos[:HALO, :] = left_ref[0]
    halos[HALO : 2 * HALO, :] = right_ref[0]
    halos[2 * HALO :, :] = padded(far_ref)
    for w_ref, own_ref, ref in ((wk_ref, own_k_ref, k_ref), (wv_ref, own_v_ref, v_ref)):
        rows = nn(halos[...], w_ref[...].reshape(width, width)).astype(BF16)
        ref[0, :HALO, :] = rows[:HALO]
        ref[0, HALO:right, :] = own_ref[0]
        ref[0, right:, :] = rows[HALO:]


def padded(far_ref):
    width = far_ref.shape[2]
    row = lax.broadcasted_iota(jnp.int32, (PAD, width), 0)
    far = jnp.broadcast_to(far_ref[0].astype(F32), (PAD, width))
    return jnp.where(row == 0, far, 0.0).astype(BF16)


def resident(*shape):
    return pl.BlockSpec(
        shape, lambda s: (0,) * len(shape), pipeline_mode=pl.Buffered(buffer_count=1)
    )


def one_of(weights, place):
    units, _, width = weights.shape
    return pl.BlockSpec(
        (units, width // units, width),
        lambda s: (0, place, 0),
        pipeline_mode=pl.Buffered(buffer_count=1),
    )


def project_own(x, weights):
    seqs, group, width = x.shape
    return pl.pallas_call(
        project_own_kernel,
        grid=(seqs,),
        in_specs=[by_seq(group, width), resident(*weights.shape)],
        out_specs=[by_seq(group, width)] * 3,
        out_shape=[jax.ShapeDtypeStruct(x.shape, BF16)] * 3,
        compiler_params=pltpu.CompilerParams(vmem_limit_bytes=60 << 20),
        cost_estimate=QUICK,
        name="project_own",
    )(x, weights)


def project_halos(own_keys, own_values, left, right, far, weights):
    seqs, group, width = own_keys.shape
    ext = group + 2 * HALO + PAD
    return pl.pallas_call(
        project_halos_kernel,
        grid=(seqs,),
        in_specs=[by_seq(group, width)] * 2
        + [by_seq(HALO, width), by_seq(HALO, width), by_seq(1, width)]
        + [one_of(weights, 1), one_of(weights, 2)],
        out_specs=[by_seq(ext, width)] * 2,
        out_shape=[jax.ShapeDtypeStruct((seqs, ext, width), BF16)] * 2,
        scratch_shapes=[pltpu.VMEM((2 * HALO + PAD, width), BF16)],
        compiler_params=pltpu.CompilerParams(vmem_limit_bytes=60 << 20),
        cost_estimate=QUICK,
        name="project_halos",
    )(own_keys, own_values, left, right, far, weights, weights)


def halo_grad_kernel(dk_ref, dv_ref, wk_ref, wv_ref, left_ref, right_ref, far_ref, dk, dv):
    right = dk_ref.shape[1] - HALO - PAD
    width = dk_ref.shape[2]
    for rows, ref in ((dk, dk_ref), (dv, dv_ref)):
        rows[:HALO, :] = ref[0, :HALO, :]
        rows[HALO:, :] = ref[0, right:, :]
    grad = nt(dk[...], wk_ref[...].reshape(width, width)) + nt(
        dv[...], wv_ref[...].reshape(width, width)
    )
    left_ref[0] = grad[:HALO].astype(BF16)
    right_ref[0] = grad[HALO : 2 * HALO].astype(BF16)
    far_ref[0] = grad[2 * HALO : 2 * HALO + 1].astype(BF16)


def halo_grads(d_keys, d_values, weights):
    seqs, ext, width = d_keys.shape
    rows = (HALO, HALO, 1)
    kept = pltpu.VMEM((2 * HALO + PAD, width), BF16)
    return pl.pallas_call(
        halo_grad_kernel,
        grid=(seqs,),
        in_specs=[by_seq(ext, width), by_seq(ext, width), one_of(weights, 1), one_of(weights, 2)],
        out_specs=[by_seq(n, width) for n in rows],
        out_shape=[jax.ShapeDtypeStruct((seqs, n, width), BF16) for n in rows],
        scratch_shapes=[kept, kept],
        compiler_params=pltpu.CompilerParams(vmem_limit_bytes=60 << 20),
        cost_estimate=QUICK,
        name="halo_grads",
    )(d_keys, d_values, weights, weights)


def own_grad_kernel(dq_ref, dk_ref, dv_ref, first_ref, w_ref, own_ref):
    grad = nt(dq_ref[0], square_of(w_ref, 0)) + nt(dk_ref[0], square_of(w_ref, 1))
    own_ref[0] = grad + nt(dv_ref[0], square_of(w_ref, 2)) + first_ref[0]


def own_grads(d_queries, d_keys, d_values, d_first, weights):
    seqs, group, width = d_queries.shape
    middle = pl.BlockSpec((1, group, width), lambda s: (s, HALO // group, 0))
    return pl.pallas_call(
        own_grad_kernel,
        grid=(seqs,),
        in_specs=[
            by_seq(group, width),
            middle,
            middle,
            by_seq(group, width),
            resident(*weights.shape),
        ],
        out_specs=by_seq(group, width),
        out_shape=jax.ShapeDtypeStruct((seqs, group, width), F32),
        compiler_params=pltpu.CompilerParams(vmem_limit_bytes=60 << 20),
        cost_estimate=QUICK,
        name="own_grads",
    )(d_queries, d_keys, d_values, d_first, weights)


def split_cores(value, core):
    both = value.reshape((-1, 2) + value.shape[1:])
    mine, other = both[:, 0], both[:, 1]
    return jnp.where(core == 0, mine, other), jnp.where(core == 0, other, mine)


def weight_grad_kernel(
    core_ref,
    x_ref,
    left_ref,
    right_ref,
    far_ref,
    dq_ref,
    dk_ref,
    dv_ref,
    small_ref,
    mine_ref,
    other_ref,
    acc,
    rows,
    x_tail,
    dk_tail,
    dv_tail,
):
    seq = pl.program_id(0)
    core = core_ref[0]
    group, width = dq_ref.shape[1:]
    units = 2 * mine_ref.shape[0]
    part = width // units
    main = 2 * HALO + group

    @pl.when(seq == 0)
    def _():
        acc[...] = jnp.zeros_like(acc)

    rows[:HALO, :] = left_ref[0]
    rows[HALO : HALO + group, :] = x_ref[0]
    rows[HALO + group :, :] = right_ref[0]
    tail = pl.ds(pl.multiple_of(seq * PAD, PAD), PAD)
    x_tail[tail, :] = padded(far_ref)
    dk_tail[tail, :] = dk_ref[0, main:, :]
    dv_tail[tail, :] = dv_ref[0, main:, :]
    acc[0] += tn(x_ref[0], dq_ref[0])
    acc[1] += tn(rows[...], dk_ref[0, :main, :])
    acc[2] += tn(rows[...], dv_ref[0, :main, :])

    @pl.when(seq == pl.num_programs(0) - 1)
    def _():
        ends = (None, tn(x_tail[...], dk_tail[...]), tn(x_tail[...], dv_tail[...]))
        for place, end in enumerate(ends):
            total = acc[place] if end is None else acc[place] + end
            mine, other = split_cores(total.reshape(units, part, width), core)
            at = slice(place * part, (place + 1) * part)
            mine_ref[:, at, :] = mine.astype(BF16)
            other_ref[:, at, :] = other.astype(BF16)
        used = small_ref.shape[2]
        for ref, half in zip((mine_ref, other_ref), split_cores(small_ref[...], core)):
            ref[:, 3 * part :, :used] = half.astype(BF16)
            ref[:, 3 * part :, used:] = jnp.zeros(half.shape[:2] + (width - used,), BF16)


def weight_grads(core, x, left, right, far, d_queries, d_keys, d_values, small):
    seqs, group, width = d_queries.shape
    ext = d_keys.shape[1]
    units, small_rows, _ = small.shape
    shape = (units // 2, 3 * (width // units) + small_rows, width)
    tail = pltpu.VMEM((seqs * PAD, width), BF16)
    return pl.pallas_call(
        weight_grad_kernel,
        grid=(seqs,),
        in_specs=[
            pl.BlockSpec(memory_space=pltpu.SMEM),
            by_seq(group, width),
            by_seq(HALO, width),
            by_seq(HALO, width),
            by_seq(1, width),
            by_seq(group, width),
            by_seq(ext, width),
            by_seq(ext, width),
            resident(*small.shape),
        ],
        out_specs=[resident(*shape)] * 2,
        out_shape=[jax.ShapeDtypeStruct(shape, BF16)] * 2,
        scratch_shapes=[
            pltpu.VMEM((3, width, width), F32),
            pltpu.VMEM((2 * HALO + group, width), BF16),
            tail,
            tail,
            tail,
        ],
        compiler_params=pltpu.CompilerParams(vmem_limit_bytes=60 << 20),
        cost_estimate=QUICK,
        name="weight_grads",
    )(core, x, left, right, far, d_queries, d_keys, d_values, small)


def document_of(positions, lengths, seq_len):
    count = lengths.shape[1]
    order = jnp.arange(count)
    ends = jnp.sum(jnp.where(order[None, :] <= order[:, None], lengths[:, None, :], 0), axis=2)
    counted = jnp.sum((positions[None, :, None] >= ends[:, None, :]).astype(jnp.int32), axis=2)
    inside = (positions >= 0) & (positions < seq_len)
    return jnp.where(inside[None, :], counted, -1)


def masks(lengths, offset, group, seq_len):
    ext = group + 2 * HALO
    slots = ext // 4
    positions = offset - HALO + jnp.arange(ext + PAD, dtype=jnp.int32)
    doc = document_of(positions, lengths, seq_len)
    slot_doc = doc[:, 2:ext:4]
    biases = []
    for block in range(group // QB):
        near = HALO - WIN // 2 + block * QB
        far = block * QB // 4
        key_place = jnp.concatenate((jnp.arange(near, near + NEAR), 4 * jnp.arange(far, far + FAR) + 2))
        reach = jnp.concatenate((jnp.full((NEAR,), WIN // 2), jnp.full((FAR,), PWIN // 2)))
        key_doc = jnp.concatenate((doc[:, near : near + NEAR], slot_doc[:, far : far + FAR]), axis=1)
        query_place = HALO + block * QB + jnp.arange(QB)
        query_doc = doc[:, HALO + block * QB : HALO + (block + 1) * QB]
        allowed = (jnp.abs(key_place[:, None] - query_place[None, :]) <= reach[:, None])[None] & (
            key_doc[:, :, None] == query_doc[:, None, :]
        )
        biases.append(jnp.where(allowed, 0.0, MASKED).astype(F32))
    same = jnp.stack(
        [(doc[:, tap : tap + ext : 4] == slot_doc).astype(F32) for tap in range(5)], axis=1
    )
    same = jnp.broadcast_to(same[..., None], same.shape + (LANES,))
    return jnp.stack(biases, axis=1), same, slots


def steps(count):
    for k in range(1, count):
        if count & (count - 1) == 0:
            yield [(i, i ^ k) for i in range(count)], lambda me, k=k: (me ^ k, me ^ k)
        else:
            yield (
                [(i, (i + k) % count) for i in range(count)],
                lambda me, k=k: (lax.rem(me + k, count), lax.rem(me - k + count, count)),
            )


def pick(value, index, dim=0):
    return lax.dynamic_index_in_dim(value, index, dim, keepdims=False)


def gather_seq(block, *earlier):
    count, me = lax.axis_size("seq"), lax.axis_index("seq")
    zeros = (0,) * block.ndim
    came_all = after(tuple(lax.ppermute(block, "seq", pairs) for pairs, _ in steps(count)), *earlier)
    column = jnp.zeros((count,) + block.shape, block.dtype)
    column = lax.dynamic_update_slice(column, block[None], (me,) + zeros)
    for came, (_, met) in zip(came_all, steps(count)):
        column = lax.dynamic_update_slice(column, came[None], (met(me)[1],) + zeros)
    return column


def gather_yx(column):
    me = lax.axis_index("yx")
    pieces = [(column, me)]
    for pairs, met in steps(lax.axis_size("yx")):
        pieces.append((lax.ppermute(column, "yx", pairs), met(me)[1]))
    return pieces


def assemble_kernel(count, *refs):
    places, parts, whole, sems = refs[0], refs[1 : 1 + count], refs[-2], refs[-1]
    copies = [
        pltpu.make_async_copy(part, whole.at[places[i]], sems.at[i]) for i, part in enumerate(parts)
    ]
    for copy in copies:
        copy.start()
    for copy in copies:
        copy.wait()


def gather_core(pieces):
    count, me = lax.axis_size("core"), lax.axis_index("core")
    parts, places = [], []
    for piece, place in pieces:
        parts.append(piece)
        places.append(place * count + me)
        for pairs, met in steps(count):
            parts.append(lax.ppermute(piece, "core", pairs))
            places.append(place * count + met(me)[1])
    return pl.pallas_call(
        functools.partial(assemble_kernel, len(parts)),
        in_specs=[pl.BlockSpec(memory_space=pltpu.SMEM)]
        + [pl.BlockSpec(memory_space=pltpu.VMEM)] * len(parts),
        out_specs=pl.BlockSpec(memory_space=pl.ANY),
        out_shape=jax.ShapeDtypeStruct((len(parts),) + parts[0].shape, BF16),
        compiler_params=pltpu.CompilerParams(vmem_limit_bytes=60 << 20),
        scratch_shapes=[pltpu.SemaphoreType.DMA((len(parts),))],
        cost_estimate=QUICK,
        name="assemble",
    )(jnp.stack(places).astype(jnp.int32), *parts)


def after(value, *earlier):
    return lax.optimization_barrier((value, earlier))[0] if earlier else lax.optimization_barrier(value)


def exchange_sum(pieces, axis, *earlier):
    me = lax.axis_index(axis)
    came = [
        lax.ppermute(pick(pieces, met(me)[0]), axis, pairs)
        for pairs, met in steps(lax.axis_size(axis))
    ]
    total = pick(pieces, me).astype(F32)
    for part in after(came, *earlier):
        total = total + part.astype(F32)
    return total


def local(
    tokens,
    doc_lengths,
    query_weight,
    key_weight,
    value_weight,
    out_weight,
    pool_weight,
    first_gain,
    first_shift,
    inner_weight,
    inner_bias,
    outer_weight,
    outer_bias,
    second_gain,
    second_shift,
    cotangent,
):
    seq_count = lax.axis_size("seq")
    yx_count = lax.axis_size("yx")
    core_count = lax.axis_size("core")
    units = yx_count * core_count
    parts = units * seq_count
    core = lax.axis_index("core")
    seq_place = lax.axis_index("seq")
    seqs, group, width = tokens.shape
    ff = inner_weight.shape[1]
    panels = ff // width
    share = query_weight.shape[0]
    count = seqs * group

    def shift(value, by):
        pairs = [(i, i + by) for i in range(seq_count) if 0 <= i + by < seq_count]
        return lax.ppermute(value, "seq", pairs)

    early = stack(
        query_weight,
        key_weight,
        value_weight,
        pool_weight,
        (first_gain, first_shift, outer_bias, second_gain, second_shift),
        inner_bias,
    )
    late = pack(outer_weight, inner_weight, out_weight)
    bias, same, _ = masks(doc_lengths, seq_place * group, group, group * seq_count)
    early_column, bias, same = after((gather_seq(early), bias, same))
    sent = after(tokens, early_column)
    came = (
        shift(sent[:, group - HALO :], 1),
        shift(sent[:, :HALO], -1),
        shift(sent[:, :1], -2),
    )
    early_column = jnp.concatenate(
        [early_column[:, i * share : (i + 1) * share].reshape(-1, width) for i in range(3)]
        + [early_column[:, 3 * share :].reshape(-1, width)],
        axis=0,
    )
    early_pieces = gather_yx(early_column)
    early = gather_core(early_pieces)
    late_column = lax.all_gather(late, "seq", axis=0)
    late_column = after(late_column, [piece for piece, _ in early_pieces[1:]])
    outer_rows = panels * share
    late = lax.all_gather(late_column, ("yx", "core"), axis=0)
    late = late.reshape(units, seq_count, 2 * panels + 1, share, width)
    small = early[:, 3 * seq_count * share :].reshape(parts, SMALL, width)
    vectors = small[:, : SMALL - 1, :share].transpose(1, 0, 2).reshape(SMALL - 1, width).astype(F32)
    taps = jnp.pad(vectors[:10], ((0, 6), (0, 0)))
    small_rows_f32 = jnp.pad(vectors[10:], ((0, 3), (0, 0)))
    bias_inner = small[:, SMALL - 1, : ff // parts].reshape(panels, 1, width).astype(F32)

    flat = tokens.reshape(count, width)

    queries, own_keys, own_values = project_own(tokens, early)
    keys, values = project_halos(own_keys, own_values, *came, early)
    mixed, lse = attention_forward(queries, keys, values, taps, same, bias)
    y, d_first, d_mixed, d_small, d_bias, d_late = feed_forward(
        flat,
        mixed.reshape(count, width),
        cotangent.reshape(count, width),
        small_rows_f32,
        bias_inner,
        late,
    )
    late_sum = lax.psum_scatter(
        d_late.reshape(-1, width), ("yx", "core"), scatter_dimension=0, tiled=True
    )
    d_queries, d_keys, d_values, d_taps = attention_backward(
        queries,
        keys,
        values,
        taps,
        same,
        bias,
        lse,
        d_mixed.reshape(seqs, group, width),
        0,
        seqs,
        (),
    )
    left, right, far = halo_grads(d_keys, d_values, early)
    from_far = shift(far, 2)
    back = (from_far, shift(left, -1), shift(right, 1))

    d_taps = jnp.sum(d_taps, axis=0)[:10]
    d_vectors = jnp.concatenate((d_taps, d_small[:5]), axis=0)
    d_vectors = d_vectors.reshape(SMALL - 1, parts, share).transpose(1, 0, 2)
    d_vectors = jnp.pad(d_vectors, ((0, 0), (0, 0), (0, LANES - share)))
    d_bias = jnp.pad(d_bias.reshape(parts, 1, -1), ((0, 0), (0, 0), (0, LANES - ff // parts)))
    d_vectors = jnp.concatenate((d_vectors, d_bias), axis=1)
    d_vectors = d_vectors.reshape(units, seq_count * SMALL, LANES)
    mine, other = weight_grads(
        core.astype(jnp.int32).reshape(1),
        after(tokens, left),
        *came,
        d_queries,
        d_keys,
        d_values,
        d_vectors,
    )
    own = own_grads(
        d_queries,
        *after((d_keys, d_values), mine),
        d_first.reshape(seqs, group, width),
        early,
    )
    (mine, other), back, late_sum, own = after(((mine, other), back, late_sum, own))
    late_sum = lax.psum_scatter(late_sum, "seq", scatter_dimension=0, tiled=True).astype(F32)
    swapped = lax.ppermute(other, "core", [(0, 1), (1, 0)])
    early_sum = (mine.astype(F32) + swapped.astype(F32)).astype(BF16)
    early_sum = exchange_sum(early_sum, "yx").astype(BF16)
    whole = 3 * seq_count * share
    early_sum = jnp.concatenate(
        [
            early_sum[:whole]
            .reshape(3, seq_count, share, width)
            .swapaxes(0, 1)
            .reshape(seq_count, 3 * share, width),
            early_sum[whole:].reshape(seq_count, SMALL, width),
        ],
        axis=1,
    )
    early_sum = exchange_sum(early_sum, "seq")

    edge = group - HALO
    from_far, from_right, from_left = (part.astype(F32) for part in back)
    d_input = own + jnp.pad(from_right, ((0, 0), (edge, 0), (0, 0)))
    d_input = d_input + jnp.pad(from_left, ((0, 0), (0, edge), (0, 0)))
    d_input = d_input + jnp.pad(from_far, ((0, 0), (0, group - 1), (0, 0)))

    vector_sum = early_sum[3 * share :]
    pieces = [vector_sum[10 + i, :share] for i in range(5)]
    return (
        y.reshape(seqs, group, width),
        d_input.astype(BF16),
        early_sum[:share],
        early_sum[share : 2 * share],
        early_sum[2 * share : 3 * share],
        late_sum[2 * outer_rows :],
        vector_sum[:10, :share],
        pieces[0],
        pieces[1],
        late_sum[outer_rows : 2 * outer_rows]
        .reshape(panels, share, width)
        .transpose(1, 0, 2)
        .reshape(share, ff),
        vector_sum[SMALL - 1, : ff // parts],
        late_sum[:outer_rows],
        pieces[2],
        pieces[3],
        pieces[4],
    )


def solution(mesh):
    dp, seq = mesh.devices.shape
    cores = 2 if dp % 2 == 0 else 1
    mesh = Mesh(mesh.devices.reshape(dp // cores, cores, seq), ("yx", "core", "seq"))
    every = ("yx", "core", "seq")
    rows = P(every, None)
    vector = P(every)
    whole = P(("yx", "core"), "seq", None)
    taps = P(None, every)
    weights = (rows, rows, rows, rows, taps, vector, vector, rows, vector, rows, vector, vector, vector)
    return jax.shard_map(
        local,
        mesh=mesh,
        in_specs=(whole, P(("yx", "core"), None)) + weights + (whole,),
        out_specs=(whole, whole) + weights,
        check_vma=False,
    )
```
